32 devices in a mesh: shard: 8 (over y, x, core), rep: 4 (over z).
Axes of the slice: x: 2, y: 2, z: 4, core: 2. Of those that a mesh axis runs over, the one named last changes fastest.
Arguments:
- tokens: bfloat16 [16384, 2048], P(('shard', 'rep')), may hold values from -6 to 6
- out_grad: bfloat16 [16384, 2048], P(('shard', 'rep')), may hold values from -6 to 6
- token_perm: int32 [16384], replicated, may hold values from 0 to 16383, as said below
- seq_lens: int32 [32, 4], P(('shard', 'rep')), may hold values from 0 to 512, as said below
- adapter_ids: int32 [32, 4, 5], P(('shard', 'rep')), may hold values from 0 to 7
- attn_norm_gain: bfloat16 [2048], P('shard'), may hold values from 0.099609375 to 1.8984375
- attn_norm_bias: bfloat16 [2048], P('shard'), may hold values from -1.75 to 1.75
- query_weight: bfloat16 [2048, 2048], P('shard'), may hold values from -0.125 to 0.125
- query_bias: bfloat16 [2048], P('shard'), may hold values from -1.75 to 1.75
- keyval_weight: bfloat16 [2048, 256], P('shard'), may hold values from -0.125 to 0.125
- value_bias: bfloat16 [128], P('shard'), may hold values from -0.625 to 0.625
- mixer_weight: bfloat16 [2048, 2048], P('shard'), may hold values from -0.75 to 0.75
- mixer_bias: bfloat16 [2048], P('shard'), may hold values from -1.75 to 1.75
- mlp_norm_gain: bfloat16 [2048], P('shard'), may hold values from 0.099609375 to 1.8984375
- mlp_norm_bias: bfloat16 [2048], P('shard'), may hold values from -1.75 to 1.75
- expand_weight: bfloat16 [2048, 8192], P('shard'), may hold values from -0.125 to 0.125
- expand_bias: bfloat16 [8192], P('shard'), may hold values from -1.75 to 1.75
- reduce_weight: bfloat16 [8192, 2048], P('shard'), may hold values from -0.09375 to 0.09375
- reduce_bias: bfloat16 [2048], P('shard'), may hold values from -1.75 to 1.75
- query_down: bfloat16 [8, 16, 2048], replicated, may hold values from -0.125 to 0.125
- query_up: bfloat16 [8, 16, 2048], replicated, may hold values from -0.75 to 0.75
- keyval_down: bfloat16 [8, 16, 2048], replicated, may hold values from -0.125 to 0.125
- keyval_up: bfloat16 [8, 16, 256], replicated, may hold values from -0.75 to 0.75
- mixer_down: bfloat16 [8, 16, 2048], replicated, may hold values from -0.75 to 0.75
- mixer_up: bfloat16 [8, 16, 2048], replicated, may hold values from -0.75 to 0.75
- expand_down: bfloat16 [8, 16, 2048], replicated, may hold values from -0.125 to 0.125
- expand_up: bfloat16 [8, 16, 8192], replicated, may hold values from -0.75 to 0.75
- reduce_down: bfloat16 [8, 16, 8192], replicated, may hold values from -0.09375 to 0.09375
- reduce_up: bfloat16 [8, 16, 2048], replicated, may hold values from -0.75 to 0.75
Outputs:
- layer_out: bfloat16 [16384, 2048], P(('shard', 'rep'))
- tokens_grad: bfloat16 [16384, 2048], P(('shard', 'rep'))
- query_down_grad: float32 [8, 16, 2048], P(None, None, 'shard')
- query_up_grad: float32 [8, 16, 2048], P(None, None, 'shard')
- keyval_down_grad: float32 [8, 16, 2048], P(None, None, 'shard')
- keyval_up_grad: float32 [8, 16, 256], P(None, None, 'shard')
- mixer_down_grad: float32 [8, 16, 2048], P(None, None, 'shard')
- mixer_up_grad: float32 [8, 16, 2048], P(None, None, 'shard')
- expand_down_grad: float32 [8, 16, 2048], P(None, None, 'shard')
- expand_up_grad: float32 [8, 16, 8192], P(None, None, 'shard')
- reduce_down_grad: float32 [8, 16, 8192], P(None, None, 'shard')
- reduce_up_grad: float32 [8, 16, 2048], P(None, None, 'shard')
The draws below stay inside these ranges and needn't reach their ends.
Inputs may be any that keep to these rules, and one draw needn't show every extreme that they name: token_perm is a permutation. Dealt block s * 4 + r takes its tokens only from the given-order blocks of devices with the same rep index r. From any device to any one device of its shard group go at most 96 tokens, and in every draw some pair carries exactly 96. `seq_lens`: each row sums to 512; every length is a multiple of 128, and a length of 0 is an empty slot. Some block holds one sequence of 512 tokens in every draw.
All inputs are finite; a program needn't handle non-finite values.
Results may differ from the reference program's by a relative error of at most 0.015.
Values may be sent and summed in bfloat16 or wider, within the bound.
A program may use at most 320 MiB of HBM per device.

```python
import jax
import jax.numpy as jnp
from jax import lax

D = 2048
HD = 128
FF = 8192
E = 8
R = 16
SEQ_DEV = 4
TOK_DEV = 512
TOKENS = 16384
N_SHARD = 8
N_REP = 4
DEVICES = 32


def deal_group(group_key, replica):
    members = N_SHARD
    replicas = N_REP
    pieces = 2 * members
    piece_len = TOK_DEV // pieces
    keys_all = jax.random.split(group_key, 4)
    member_order = jax.random.permutation(keys_all[0], members).astype(jnp.int32)
    offsets = jax.random.permutation(keys_all[1], members).astype(jnp.int32)
    pattern = jnp.concatenate([jnp.repeat(offsets[:members // 2], 3), offsets[members // 2:]])

    def shuffle_row(row_key):
        return jax.random.permutation(row_key, pattern)
    shuffled = jax.vmap(shuffle_row)(jax.random.split(keys_all[2], members))
    source = (member_order[:, None] + shuffled) % members
    total = members * pieces
    tiebreak = jax.random.permutation(keys_all[3], total).astype(jnp.int32)
    ranking = source.reshape(total).astype(jnp.int32) * total + tiebreak
    order_ids = jnp.argsort(ranking, stable=True)
    placed = jnp.zeros((total,), jnp.int32).at[order_ids].set(jnp.arange(total, dtype=jnp.int32))
    sender = placed // pieces
    sender_piece = placed % pieces
    first_tok = (sender * replicas + replica) * TOK_DEV + sender_piece * piece_len
    spans = first_tok[:, None] + jnp.arange(piece_len, dtype=jnp.int32)[None, :]
    return spans.reshape(members, TOK_DEV)


def draw_token_perm(key, part):
    layout = jax.vmap(deal_group)(jax.random.split(key, N_REP), jnp.arange(N_REP, dtype=jnp.int32))
    return jnp.transpose(layout, (1, 0, 2)).reshape(N_SHARD * N_REP * TOK_DEV).astype(jnp.int32)


def draw_seq_lens(key, part):
    device_count = N_SHARD * N_REP
    cut_key, full_key = jax.random.split(key)
    cuts = jnp.sort(jax.random.randint(cut_key, (device_count, SEQ_DEV - 1), 0, 5), axis=1)
    full_row = jax.random.randint(full_key, (), 0, device_count)
    cuts = jnp.where(jnp.arange(device_count)[:, None] == full_row, 4, cuts).astype(jnp.int32)
    bounds = jnp.concatenate([jnp.zeros((device_count, 1), jnp.int32), cuts, jnp.full((device_count, 1), 4, jnp.int32)], axis=1)
    return ((bounds[:, 1:] - bounds[:, :-1]) * (TOK_DEV // 4)).astype(jnp.int32)


def place_ends(array, rng, smallest, top_value):
    longest = array.shape.index(max(array.shape))
    spots = []
    for shift in (0, 1):
        where = [jax.random.randint(jax.random.fold_in(rng, axis), (), 0, length) for axis, length in enumerate(array.shape)]
        where[longest] = (where[longest] + shift) % array.shape[longest]
        spots.append(tuple(where))
    return array.at[spots[0]].set(smallest).at[spots[1]].set(top_value)


def block_scale(stream_key, shape, shards, smallest, top_value):
    def one(axis_at, blocks):
        steps = jax.random.uniform(jax.random.fold_in(jax.random.fold_in(stream_key, 6), axis_at), (blocks,), jnp.float32, smallest / len(shards), top_value / len(shards))
        return jnp.repeat(jnp.exp(steps), shape[axis_at] // blocks).reshape((-1,) + (1,) * (len(shape) - axis_at - 1))

    factor_of = one(*shards[0])
    for cut in shards[1:]:
        factor_of = factor_of * one(*cut)
    return factor_of


def noise(stream_key, extent, deviation, bound, cuts=(), held_as=jnp.bfloat16):
    result = deviation * jax.random.normal(stream_key, extent, jnp.float32)
    if cuts:
        result = result * block_scale(stream_key, extent, cuts, -0.22, 0.18)
    return jnp.clip(result, -bound, bound).astype(held_as)


def setup_inputs(seed: int = 0) -> dict:
    key_of = jax.random.split(jax.random.key(seed), 30)
    return {
        "tokens": noise(key_of[0], (TOKENS, D), 1.0, 6.0, ((0, 32),)),
        "out_grad": noise(key_of[1], (TOKENS, D), 1.0, 6.0, ((0, 32),)),
        "token_perm": draw_token_perm(jax.random.fold_in(key_of[29], 71), 0),
        "seq_lens": draw_seq_lens(jax.random.fold_in(key_of[29], 71), 0),
        "adapter_ids": place_ends(jax.random.randint(key_of[4], (DEVICES, SEQ_DEV, 5), 0, E), jax.random.fold_in(key_of[4], 1), 0, E - 1).astype(jnp.int32),
        "attn_norm_gain": jnp.clip(1.0 + 0.18 * jax.random.normal(key_of[5], (D,), jnp.float32), 0.099609375, 1.8984375).astype(jnp.bfloat16),
        "attn_norm_bias": noise(key_of[6], (D,), 0.3, 1.75, ((0, 8),)),
        "query_weight": noise(key_of[7], (D, D), D ** -0.5, 0.125, ((0, 8),)),
        "query_bias": noise(key_of[8], (D,), 0.3, 1.75, ((0, 8),)),
        "keyval_weight": noise(key_of[9], (D, 2 * HD), D ** -0.5, 0.125, ((0, 8),)),
        "value_bias": noise(key_of[10], (HD,), 0.1, 0.625, ((0, 8),)),
        "mixer_weight": noise(key_of[11], (D, D), (D // 32) ** -0.5, 0.75, ((0, 8),)),
        "mixer_bias": noise(key_of[12], (D,), 0.3, 1.75, ((0, 8),)),
        "mlp_norm_gain": jnp.clip(1.0 + 0.18 * jax.random.normal(key_of[13], (D,), jnp.float32), 0.099609375, 1.8984375).astype(jnp.bfloat16),
        "mlp_norm_bias": noise(key_of[14], (D,), 0.3, 1.75, ((0, 8),)),
        "expand_weight": noise(key_of[15], (D, FF), D ** -0.5, 0.125, ((0, 8),)),
        "expand_bias": noise(key_of[16], (FF,), 0.3, 1.75, ((0, 8),)),
        "reduce_weight": noise(key_of[17], (FF, D), (FF // 2) ** -0.5, 0.09375, ((0, 8),)),
        "reduce_bias": noise(key_of[18], (D,), 0.3, 1.75, ((0, 8),)),
        "query_down": noise(key_of[19], (E, R, D), D ** -0.5, 0.125),
        "query_up": noise(key_of[20], (E, R, D), (4 * R) ** -0.5, 0.75),
        "keyval_down": noise(key_of[21], (E, R, D), D ** -0.5, 0.125),
        "keyval_up": noise(key_of[22], (E, R, 2 * HD), (4 * R) ** -0.5, 0.75),
        "mixer_down": noise(key_of[23], (E, R, D), (D // 32) ** -0.5, 0.75),
        "mixer_up": noise(key_of[24], (E, R, D), (4 * R) ** -0.5, 0.75),
        "expand_down": noise(key_of[25], (E, R, D), D ** -0.5, 0.125),
        "expand_up": noise(key_of[26], (E, R, FF), (4 * R) ** -0.5, 0.75),
        "reduce_down": noise(key_of[27], (E, R, FF), (FF // 2) ** -0.5, 0.09375),
        "reduce_up": noise(key_of[28], (E, R, D), (4 * R) ** -0.5, 0.75),
    }


@jax.custom_vjp
def low(v):
    return lax.optimization_barrier(v.astype(jnp.bfloat16)).astype(jnp.float32)

@jax.custom_vjp
def low_back(v):
    return v

def low_keep(v):
    return (low(v), None)

def low_pass(kept, grad):
    return (grad,)

def back_keep(v):
    return (v, None)

def back_low(kept, grad):
    return (low(grad),)
low.defvjp(low_keep, low_pass)
low_back.defvjp(back_keep, back_low)
adapter_scale = 0.5
norm_epsilon = 1e-05
masked_score = -1e+30
highest = lax.Precision.HIGHEST

def matmul(left_mat, right_mat):
    return jnp.dot(left_mat, right_mat, precision=highest, preferred_element_type=jnp.float32)

def layer_norm(values, norm_gain, norm_bias):
    center = values - lax.optimization_barrier(jnp.mean(values, axis=-1, keepdims=True))
    spread = lax.optimization_barrier(jnp.mean(center * center, axis=-1, keepdims=True))
    return center * lax.rsqrt(spread + norm_epsilon) * norm_gain + norm_bias

def project(inputs, weight, bias_row, down_mat, up_mat, col_mask):
    rank_rows = down_mat.shape[0] * down_mat.shape[1]
    lowered = lax.dot_general(inputs, down_mat.reshape(rank_rows, -1), (((1,), (1,)), ((), ())), precision=highest, preferred_element_type=jnp.float32)
    lowered = low(low_back(lowered) * col_mask)
    return low_back(matmul(inputs, weight) + bias_row + adapter_scale * matmul(lowered, up_mat.reshape(rank_rows, -1)))

def block_forward(inputs, adapters, frozen, segment, chosen):
    attn_gain, attn_bias, query_weight, query_bias, keyval_weight, value_bias, mixer_weight, mixer_bias, mlp_gain, mlp_bias, expand_weight, expand_bias, reduce_weight, reduce_bias = frozen
    length = inputs.shape[0]
    model_width = inputs.shape[1]
    head_size = value_bias.shape[0]
    head_count = model_width // head_size
    rank_size = adapters[0].shape[1]
    rank_cols = jnp.arange(adapters[0].shape[0] * rank_size, dtype=jnp.int32) // rank_size
    col_masks = [(rank_cols[None, :] == chosen[:, which_proj:which_proj + 1]).astype(jnp.float32) for which_proj in range(5)]
    normed = low(layer_norm(inputs, attn_gain, attn_bias))
    query_low = low(project(normed, query_weight, query_bias, adapters[0], adapters[1], col_masks[0]))
    keyval_bias = jnp.concatenate([jnp.zeros((head_size,), jnp.float32), value_bias])
    keyval = low(project(normed, keyval_weight, keyval_bias, adapters[2], adapters[3], col_masks[1]))
    key_rows = keyval[:, :head_size]
    values = keyval[:, head_size:]
    scores = jnp.einsum('thd,ud->htu', query_low.reshape(length, head_count, head_size), key_rows, precision=highest)
    scores = low_back(scores * head_size ** (-0.5))
    places = jnp.arange(length, dtype=jnp.int32)
    allowed = (segment[:, None] == segment[None, :]) & (places[:, None] >= places[None, :])
    scores = jnp.where(allowed[None], scores, masked_score)
    row_max = lax.optimization_barrier(jnp.max(scores, axis=-1, keepdims=True))
    shifted = jnp.exp(scores - row_max)
    softmax_rows = low(shifted / lax.optimization_barrier(jnp.sum(shifted, axis=-1, keepdims=True)))
    attended = jnp.einsum('htu,ud->thd', softmax_rows, values, precision=highest).reshape(length, model_width)
    attended = low(low_back(attended))
    resid = inputs + project(attended, mixer_weight, mixer_bias, adapters[4], adapters[5], col_masks[2])
    normed_mlp = low(layer_norm(resid, mlp_gain, mlp_bias))
    hidden = project(normed_mlp, expand_weight, expand_bias, adapters[6], adapters[7], col_masks[3])
    act_low = low(jax.nn.gelu(hidden, approximate=True))
    return resid + project(act_low, reduce_weight, reduce_bias, adapters[8], adapters[9], col_masks[4])

def reference(tokens, out_grad, token_perm, seq_lens, adapter_ids, attn_norm_gain, attn_norm_bias, query_weight, query_bias, keyval_weight, value_bias, mixer_weight, mixer_bias, mlp_norm_gain, mlp_norm_bias, expand_weight, expand_bias, reduce_weight, reduce_bias, query_down, query_up, keyval_down, keyval_up, mixer_down, mixer_up, expand_down, expand_up, reduce_down, reduce_up):
    frozen = tuple((weight.astype(jnp.float32) for weight in (attn_norm_gain, attn_norm_bias, query_weight, query_bias, keyval_weight, value_bias, mixer_weight, mixer_bias, mlp_norm_gain, mlp_norm_bias, expand_weight, expand_bias, reduce_weight, reduce_bias)))
    adapters = tuple((stacked.astype(jnp.float32) for stacked in (query_down, query_up, keyval_down, keyval_up, mixer_down, mixer_up, expand_down, expand_up, reduce_down, reduce_up)))
    block_count = seq_lens.shape[0]
    model_width = tokens.shape[1]
    dealt_x = tokens[token_perm].reshape(block_count, TOK_DEV, model_width)
    dealt_dy = out_grad[token_perm].reshape(block_count, TOK_DEV, model_width)
    places = jnp.arange(TOK_DEV, dtype=jnp.int32)
    slot_ids = jnp.arange(SEQ_DEV, dtype=jnp.int32)

    def step_block(running, item):
        block_x, block_dy, block_lens, block_ids = item
        seq_ends = jnp.cumsum(block_lens).astype(jnp.int32)
        segment = lax.optimization_barrier(jnp.sum((places[:, None] >= seq_ends[None, :]).astype(jnp.int32), axis=1)).astype(jnp.int32)
        slot_hits = (segment[:, None] == slot_ids[None, :]).astype(jnp.int32)
        chosen = lax.optimization_barrier(jnp.sum(slot_hits[:, :, None] * block_ids[None, :, :], axis=1)).astype(jnp.int32)

        def forward_fn(inputs, adapter_set):
            return block_forward(inputs, adapter_set, frozen, segment, chosen)
        block_out, pull_back = jax.vjp(forward_fn, block_x.astype(jnp.float32), adapters)
        input_grad, adapter_grads = pull_back(block_dy.astype(jnp.float32))
        running = tuple((total + piece for total, piece in zip(running, adapter_grads)))
        return (running, (block_out.astype(jnp.bfloat16), input_grad.astype(jnp.bfloat16)))
    start_sums = tuple((jnp.zeros(stacked.shape, jnp.float32) for stacked in adapters))
    sums, (out_blocks, grad_blocks) = lax.scan(step_block, start_sums, (dealt_x, dealt_dy, seq_lens, adapter_ids))
    layer_out = jnp.zeros_like(tokens).at[token_perm].set(out_blocks.reshape(-1, model_width))
    tokens_grad = jnp.zeros_like(tokens).at[token_perm].set(grad_blocks.reshape(-1, model_width))
    return (layer_out, tokens_grad, sums[0], sums[1], sums[2], sums[3], sums[4], sums[5], sums[6], sums[7], sums[8], sums[9])
```

```python
import jax
import jax.numpy as jnp
from jax import lax
from jax.experimental import pallas as pl
from jax.experimental.pallas import tpu as pltpu
from jax.sharding import PartitionSpec as P

scale_lora = 0.5
eps = 1e-05
f32 = jnp.float32
bf16 = jnp.bfloat16
neg_big = -1e30
gelu_c = 0.7978845608028654
VMEM_LIMIT = 60 * 1024 * 1024


def dot_nn(a, b):
    return lax.dot_general(a, b, (((1,), (0,)), ((), ())), preferred_element_type=f32)


def dot_nt(a, b):
    return lax.dot_general(a, b, (((1,), (1,)), ((), ())), preferred_element_type=f32)


def dot_tn(a, b):
    return lax.dot_general(a, b, (((0,), (0,)), ((), ())), preferred_element_type=f32)


def key_onehot(slot_row, slots):
    ids = lax.broadcasted_iota(jnp.int32, (slots, slot_row.shape[1]), 0)
    return jnp.where(ids == slot_row, 1.0, 0.0).astype(bf16)


def to_rows(x, heads):
    hd = x.shape[1] // heads
    return jnp.concatenate([x[:, h * hd : (h + 1) * hd] for h in range(heads)], axis=0)


def to_cols(x, heads):
    c = x.shape[0] // heads
    return jnp.concatenate([x[h * c : (h + 1) * c] for h in range(heads)], axis=1)


def softmax_rows(qr, kd, span, heads):
    rows, keys = qr.shape[0], kd.shape[0]
    c = rows // heads
    u = lax.broadcasted_iota(jnp.int32, (c, keys), 1)
    allowed = (u >= span[:, 0:1]) & (u <= span[:, 1:2])
    s = dot_nt(qr, kd) * (kd.shape[1] ** (-0.5))
    s = jnp.where(allowed[None], s.reshape(heads, c, keys), neg_big)
    top = jnp.max(s, axis=2, keepdims=True)
    e = jnp.exp(s - top)
    p = e / jnp.sum(e, axis=2, keepdims=True)
    return p.reshape(rows, keys)


def attn_fwd_kernel(heads, slot_ref, span_ref, q_ref, kv_ref, o_ref, kd_ref):
    m, _, c, w = kv_ref.shape
    hd = w // 2
    oh = key_onehot(slot_ref[0], m * c)
    kvd = dot_tn(oh, kv_ref[...].reshape(m * c, w)).astype(bf16)
    kd_ref[0] = kvd
    qr = to_rows(q_ref[0], heads)
    p = softmax_rows(qr, kvd[:, :hd], span_ref[0], heads).astype(bf16)
    o = dot_nn(p, kvd[:, hd:]).astype(bf16)
    o_ref[0] = to_cols(o, heads)


def attn_bwd_kernel(heads, slot_ref, span_ref, q_ref, do_ref, kd_ref, dq_ref, ds_ref):
    m, _, c, w = ds_ref.shape
    hd = w // 2
    kvd = kd_ref[0]
    kd, vd = kvd[:, :hd], kvd[:, hd:]
    qr = to_rows(q_ref[0], heads)
    dor = to_rows(do_ref[0], heads)
    p = softmax_rows(qr, kd, span_ref[0], heads)
    dp = dot_nt(dor, vd)
    rd = jnp.sum(dp * p, axis=1, keepdims=True)
    ds = (p * (dp - rd)).astype(bf16)
    sc = hd ** (-0.5)
    dq = (dot_nn(ds, kd) * sc).astype(bf16)
    dq_ref[0] = to_cols(dq, heads)
    dk = dot_tn(ds, qr) * sc
    dv = dot_tn(p.astype(bf16), dor)
    dkv = jnp.concatenate([dk, dv], axis=1).astype(bf16)
    oh = key_onehot(slot_ref[0], m * c)
    ds_ref[...] = dot_nn(oh, dkv).astype(bf16).reshape(ds_ref.shape)


def attn_fwd(heads, slot, span, qpad, kvs):
    m, c, w = kvs.shape[0], kvs.shape[2], kvs.shape[3]
    length = slot.shape[2]
    d = qpad.shape[2]
    return pl.pallas_call(
        lambda *refs: attn_fwd_kernel(heads, *refs),
        grid=(m,),
        in_specs=[
            pl.BlockSpec((1, 1, length), lambda k: (k, 0, 0)),
            pl.BlockSpec((1, c, 2), lambda k: (k, 0, 0)),
            pl.BlockSpec((1, c, d), lambda k: (k, 0, 0)),
            pl.BlockSpec((m, 1, c, w), lambda k: (0, k, 0, 0)),
        ],
        out_specs=[
            pl.BlockSpec((1, c, d), lambda k: (k, 0, 0)),
            pl.BlockSpec((1, length, w), lambda k: (k, 0, 0)),
        ],
        out_shape=[
            jax.ShapeDtypeStruct((m, c, d), bf16),
            jax.ShapeDtypeStruct((m, length, w), bf16),
        ],
        compiler_params=pltpu.CompilerParams(vmem_limit_bytes=VMEM_LIMIT),
    )(slot, span, qpad, kvs)


def attn_bwd(heads, slot, span, qpad, dopad, kd):
    m, c, d = qpad.shape
    length, w = kd.shape[1], kd.shape[2]
    return pl.pallas_call(
        lambda *refs: attn_bwd_kernel(heads, *refs),
        grid=(m,),
        in_specs=[
            pl.BlockSpec((1, 1, length), lambda k: (k, 0, 0)),
            pl.BlockSpec((1, c, 2), lambda k: (k, 0, 0)),
            pl.BlockSpec((1, c, d), lambda k: (k, 0, 0)),
            pl.BlockSpec((1, c, d), lambda k: (k, 0, 0)),
            pl.BlockSpec((1, length, w), lambda k: (k, 0, 0)),
        ],
        out_specs=[
            pl.BlockSpec((1, c, d), lambda k: (k, 0, 0)),
            pl.BlockSpec((m, 1, c, w), lambda k: (0, k, 0, 0)),
        ],
        out_shape=[
            jax.ShapeDtypeStruct((m, c, d), bf16),
            jax.ShapeDtypeStruct((m, m, c, w), bf16),
        ],
        compiler_params=pltpu.CompilerParams(vmem_limit_bytes=VMEM_LIMIT),
    )(slot, span, qpad, dopad, kd)


def mlp_kernel(m_ref, dy_ref, low_ref, e_ref, we_ref, wr_ref, be_ref, bup_ref, adn_ref,
               y_ref, dm_ref, lowr_ref, er_ref, gup_ref, gdn_ref):
    j = pl.program_id(0)
    members, _, rows, fc = we_ref.shape
    we = we_ref[...].reshape(members * rows, fc)
    wr = wr_ref[...].reshape(fc, wr_ref.shape[3])
    bup, adn = bup_ref[0], adn_ref[0]
    hid = dot_nn(m_ref[...], we) + be_ref[0].astype(f32)
    hid = hid + scale_lora * dot_nn(low_ref[...], bup)
    cube = hid * hid * hid
    t = jnp.tanh(gelu_c * (hid + 0.044715 * cube))
    act = (0.5 * hid * (1.0 + t)).astype(bf16)
    slope = 0.5 * (1.0 + t) + 0.5 * hid * (1.0 - t * t) * (
        gelu_c * (1.0 + 3.0 * 0.044715 * hid * hid)
    )
    dact = dot_nt(dy_ref[...], wr) + dot_nn(e_ref[...], adn)
    dh = (dact * slope).astype(bf16)

    @pl.when(j == 0)
    def _():
        y_ref[...] = jnp.zeros_like(y_ref)
        dm_ref[...] = jnp.zeros_like(dm_ref)
        lowr_ref[...] = jnp.zeros_like(lowr_ref)
        er_ref[...] = jnp.zeros_like(er_ref)

    y_ref[...] += dot_nn(act, wr)
    dm_ref[...] += dot_nt(dh, we)
    lowr_ref[...] += dot_nt(act, adn)
    er_ref[...] += dot_nt(dh, bup)
    gup_ref[0] = scale_lora * dot_tn(low_ref[...], dh)
    gdn_ref[0] = dot_tn(e_ref[...], act)


def mlp(m, dy, low3, e4, we, wr, be, bup, adn):
    n, d = m.shape
    members, chunks, rows, fc = we.shape
    sub = wr.shape[2]
    rk = low3.shape[1]
    whole = lambda j: (0, 0)
    return pl.pallas_call(
        mlp_kernel,
        grid=(chunks,),
        in_specs=[
            pl.BlockSpec((n, d), whole),
            pl.BlockSpec((n, d), whole),
            pl.BlockSpec((n, rk), whole),
            pl.BlockSpec((n, rk), whole),
            pl.BlockSpec((members, 1, rows, fc), lambda j: (0, j, 0, 0)),
            pl.BlockSpec((members, 1, sub, d), lambda j: (0, j, 0, 0)),
            pl.BlockSpec((1, 1, fc), lambda j: (j, 0, 0)),
            pl.BlockSpec((1, rk, fc), lambda j: (j, 0, 0)),
            pl.BlockSpec((1, rk, fc), lambda j: (j, 0, 0)),
        ],
        out_specs=[
            pl.BlockSpec((n, d), whole),
            pl.BlockSpec((n, d), whole),
            pl.BlockSpec((n, rk), whole),
            pl.BlockSpec((n, rk), whole),
            pl.BlockSpec((1, rk, fc), lambda j: (j, 0, 0)),
            pl.BlockSpec((1, rk, fc), lambda j: (j, 0, 0)),
        ],
        out_shape=[
            jax.ShapeDtypeStruct((n, d), f32),
            jax.ShapeDtypeStruct((n, d), f32),
            jax.ShapeDtypeStruct((n, rk), f32),
            jax.ShapeDtypeStruct((n, rk), f32),
            jax.ShapeDtypeStruct((chunks, rk, fc), f32),
            jax.ShapeDtypeStruct((chunks, rk, fc), f32),
        ],
        compiler_params=pltpu.CompilerParams(vmem_limit_bytes=VMEM_LIMIT),
    )(m, dy, low3, e4, we, wr, be, bup, adn)


def norm_parts(v):
    center = v - jnp.mean(v, axis=-1, keepdims=True)
    inv = lax.rsqrt(jnp.mean(center * center, axis=-1, keepdims=True) + eps)
    return center * inv, inv


def norm_back(n, inv, gain, dn):
    w = gain * dn
    return (w - jnp.mean(w, axis=-1, keepdims=True)
            - n * jnp.mean(w * n, axis=-1, keepdims=True)) * inv


def local(tokens, out_grad, token_perm, seq_lens, adapter_ids,
          attn_g, attn_b, wq, bq, wkv, bv, wmix, bmix, mlp_g, mlp_b, wexp, bexp, wred, bred,
          q_dn, q_up, kv_dn, kv_up, mix_dn, mix_up, exp_dn, exp_up, red_dn, red_up):
    members = lax.axis_size("shard")
    replicas = lax.axis_size("rep")
    me = lax.axis_index("shard")
    rep = lax.axis_index("rep")
    length, d = tokens.shape
    cap = 3 * length // (2 * members)
    slots = members * cap
    block = me * replicas + rep
    experts, rank = q_dn.shape[:2]
    rk = experts * rank
    seqs = seq_lens.shape[1]
    projs = adapter_ids.shape[2]
    hd = bv.shape[0] * members
    heads = d // hd
    ff = wexp.shape[1]
    chunks = 8
    sub = ff // members // chunks
    fc = sub * members

    smalls = [attn_g, attn_b, bq, bmix, mlp_g, mlp_b, bred, bexp, bv]
    small = lax.all_gather(jnp.concatenate(smalls)[None], "shard", axis=0, tiled=True)
    wide = []
    at = 0
    for part in smalls:
        wide.append(small[:, at : at + part.shape[0]])
        at += part.shape[0]
    attn_gain, attn_bias, q_bias, mix_bias, mlp_gain, mlp_bias, red_bias = (
        w.reshape(-1).astype(f32) for w in wide[:7])
    be = wide[7].reshape(members, chunks, sub).transpose(1, 0, 2).reshape(chunks, 1, fc)
    v_bias = wide[8].reshape(-1).astype(f32)
    table = jnp.concatenate([seq_lens[0], adapter_ids[0].reshape(-1)])[None]
    table = lax.all_gather(table, "shard", axis=0, tiled=True)
    lens, ids = table[:, :seqs], table[:, seqs:].reshape(members, seqs, projs)

    attn_w = lax.all_gather(jnp.concatenate([wq, wkv, wmix], axis=1), "shard", axis=0, tiled=True)
    wq_f, wkv_f, wmix_f = attn_w[:, :d], attn_w[:, d : d + 2 * hd], attn_w[:, d + 2 * hd :]
    we_c = wexp.reshape(wexp.shape[0], members, chunks, sub).transpose(2, 0, 1, 3)
    we_f = lax.all_gather(we_c.reshape(chunks, wexp.shape[0], fc), "shard", axis=0, tiled=False)
    wr_f = lax.all_gather(wred.reshape(chunks, sub, d), "shard", axis=0, tiled=False)

    group = lax.dynamic_index_in_dim(
        token_perm.reshape(members, replicas, length), rep, 1, keepdims=False)
    src = group // (length * replicas)
    places = jnp.arange(length, dtype=jnp.int32)
    same = (src[:, :, None] == src[:, None, :]) & (places[None, None, :] < places[None, :, None])
    order = jnp.sum(same.astype(jnp.int32), axis=2)
    key_slot = (src * cap + order).reshape(members, 1, length)
    ends = jnp.sum(jnp.where(jnp.arange(seqs)[:, None] >= jnp.arange(seqs)[None, :],
                             lens[:, None, :], 0), axis=2)
    seg = jnp.sum((places[None, :, None] >= ends[:, None, :]).astype(jnp.int32), axis=2)
    start = jnp.sum(jnp.where(places[None, :, None] >= ends[:, None, :], lens[:, None, :], 0), axis=2)
    hit = (src == me)[:, None, :] & (order[:, None, :] == jnp.arange(cap)[None, :, None])

    def pick(values, empty):
        return jnp.sum(jnp.where(hit, values[:, None, :] - empty, 0), axis=2) + empty

    tok = pick(group - block * length, -1)
    lo = pick(start, 1)
    hi = pick(jnp.broadcast_to(places, group.shape), 0)
    span = jnp.stack([lo, hi], axis=2)
    slot_seg = pick(seg, 0)
    put = (tok.reshape(slots, 1) == places[None, :]).astype(bf16)
    seg_hits = slot_seg[:, :, None] == jnp.arange(seqs)[None, None, :]
    slot_ids = jnp.sum(jnp.where(seg_hits[:, :, :, None], ids[:, None, :, :], 0), axis=2)
    chosen = dot_tn(put, slot_ids.reshape(slots, projs).astype(bf16)).astype(jnp.int32)
    owner = jnp.arange(rk, dtype=jnp.int32) // rank
    masks = [(owner[None, :] == chosen[:, p : p + 1]).astype(f32) for p in range(projs)]

    flat = lambda s: s.reshape(rk, s.shape[2])
    q_dn, q_up, kv_dn, kv_up, mix_dn, mix_up, exp_dn, exp_up, red_dn, red_up = map(
        flat, (q_dn, q_up, kv_dn, kv_up, mix_dn, mix_up, exp_dn, exp_up, red_dn, red_up))
    by_chunk = lambda s: s.reshape(rk, members, chunks, sub).transpose(2, 0, 1, 3).reshape(chunks, rk, fc)

    x = tokens.astype(f32)
    nx, inv_x = norm_parts(x)
    a = (nx * attn_gain + attn_bias).astype(bf16)
    both = dot_nt(a, jnp.concatenate([q_dn, kv_dn], axis=0))
    low0 = (both[:, :rk] * masks[0]).astype(bf16)
    low1 = (both[:, rk:] * masks[1]).astype(bf16)
    q = (dot_nn(a, wq_f) + q_bias + scale_lora * dot_nn(low0, q_up)).astype(bf16)
    kv_bias = jnp.concatenate([jnp.zeros((hd,), f32), v_bias])
    kv = (dot_nn(a, wkv_f) + kv_bias + scale_lora * dot_nn(low1, kv_up)).astype(bf16)
    kvp = dot_nn(put, kv).astype(bf16).reshape(members, cap, 2 * hd)
    kvs = lax.all_gather(kvp, "shard", axis=0, tiled=False)
    qpad = dot_nn(put, q).astype(bf16).reshape(members, cap, d)
    opad, kd = attn_fwd(heads, key_slot, span, qpad, kvs)
    o = dot_tn(put, opad.reshape(slots, d)).astype(bf16)
    low2 = (dot_nt(o, mix_dn) * masks[2]).astype(bf16)
    resid = x + dot_nn(o, wmix_f) + mix_bias + scale_lora * dot_nn(low2, mix_up)

    nr, inv_r = norm_parts(resid)
    m = (nr * mlp_gain + mlp_bias).astype(bf16)
    low3 = (dot_nt(m, exp_dn) * masks[3]).astype(bf16)
    e4 = (scale_lora * dot_nt(out_grad, red_up) * masks[4]).astype(bf16)
    y, dm, low4, e3, g_exp_up, g_red_dn = mlp(
        m, out_grad, low3, e4, we_f, wr_f, be, by_chunk(exp_up), by_chunk(red_dn))
    low4 = (low4 * masks[4]).astype(bf16)
    layer_out = (resid + y + red_bias + scale_lora * dot_nn(low4, red_up)).astype(bf16)
    g_red_up = scale_lora * dot_tn(low4, out_grad)
    e3 = (scale_lora * e3 * masks[3]).astype(bf16)
    dm = dm + dot_nn(e3, exp_dn)
    g_exp_dn = dot_tn(e3, m)
    dres = out_grad.astype(f32) + norm_back(nr, inv_r, mlp_gain, dm)

    def to_share(g):
        return g.reshape(rk, members, -1).transpose(1, 0, 2)

    def chunk_share(g):
        return g.reshape(chunks, rk, members, sub).transpose(2, 1, 0, 3).reshape(members, rk, chunks * sub)

    def reduce(parts):
        sizes = [p.shape[2] for p in parts]
        got = lax.psum_scatter(jnp.concatenate(parts, axis=2), "shard", scatter_dimension=0, tiled=True)
        got = lax.psum(got[0], "rep")
        outs, at = [], 0
        for size in sizes:
            outs.append(got[:, at : at + size].reshape(experts, rank, size))
            at += size
        return outs

    r_exp_dn, r_exp_up, r_red_dn, r_red_up = reduce(
        [to_share(g_exp_dn), chunk_share(g_exp_up), chunk_share(g_red_dn), to_share(g_red_up)])

    dresl = dres.astype(bf16)
    e2 = (scale_lora * dot_nt(dresl, mix_up) * masks[2]).astype(bf16)
    do = (dot_nt(dresl, wmix_f) + dot_nn(e2, mix_dn)).astype(bf16)
    g_mix_dn = dot_tn(e2, o)
    g_mix_up = scale_lora * dot_tn(low2, dresl)
    dopad = dot_nn(put, do).astype(bf16).reshape(members, cap, d)
    dqpad, dslots = attn_bwd(heads, key_slot, span, qpad, dopad, kd)
    got = lax.all_to_all(dslots, "shard", split_axis=0, concat_axis=0, tiled=True)
    dkvp = jnp.sum(got.astype(f32), axis=0).astype(bf16).reshape(slots, 2 * hd)
    dq = dot_tn(put, dqpad.reshape(slots, d)).astype(bf16)
    dkv = dot_tn(put, dkvp).astype(bf16)
    e0 = (scale_lora * dot_nt(dq, q_up) * masks[0]).astype(bf16)
    e1 = (scale_lora * dot_nt(dkv, kv_up) * masks[1]).astype(bf16)
    da = (dot_nt(dq, wq_f) + dot_nn(e0, q_dn)) + (dot_nt(dkv, wkv_f) + dot_nn(e1, kv_dn))
    tokens_grad = (dres + norm_back(nx, inv_x, attn_gain, da)).astype(bf16)
    g_down = dot_tn(jnp.concatenate([e0, e1], axis=1), a)
    g_q_up = scale_lora * dot_tn(low0, dq)
    g_kv_up = scale_lora * dot_tn(low1, dkv)
    r_q_dn, r_q_up, r_kv_dn, r_kv_up, r_mix_dn, r_mix_up = reduce(
        [to_share(g_down[:rk]), to_share(g_q_up), to_share(g_down[rk:]), to_share(g_kv_up),
         to_share(g_mix_dn), to_share(g_mix_up)])
    return (layer_out, tokens_grad, r_q_dn, r_q_up, r_kv_dn, r_kv_up, r_mix_dn, r_mix_up,
            r_exp_dn, r_exp_up, r_red_dn, r_red_up)


def solution(mesh):
    both = ("shard", "rep")
    row, vec = P("shard", None), P("shard")
    in_specs = (
        P(both, None), P(both, None), P(), P(both, None), P(both, None, None),
        vec, vec, row, vec, row, vec, row, vec, vec, vec, row, vec, row, vec,
    ) + (P(),) * 10
    out_specs = (P(both, None), P(both, None)) + (P(None, None, "shard"),) * 10
    return jax.shard_map(local, mesh=mesh, in_specs=in_specs, out_specs=out_specs, check_vma=False)
```

```python
import jax
import jax.numpy as jnp
from jax import lax
from jax.experimental import pallas as pl
from jax.experimental.pallas import tpu as pltpu
from jax.sharding import PartitionSpec as P

scale_lora = 0.5
eps = 1e-05
f32 = jnp.float32
bf16 = jnp.bfloat16
neg_big = -1e30
gelu_c = 0.7978845608028654
VMEM_LIMIT = 60 * 1024 * 1024


def dot_nn(a, b):
    return lax.dot_general(a, b, (((1,), (0,)), ((), ())), preferred_element_type=f32)


def dot_nt(a, b):
    return lax.dot_general(a, b, (((1,), (1,)), ((), ())), preferred_element_type=f32)


def dot_tn(a, b):
    return lax.dot_general(a, b, (((0,), (0,)), ((), ())), preferred_element_type=f32)


def key_onehot(slot_row, slots):
    ids = lax.broadcasted_iota(jnp.int32, (slots, slot_row.shape[1]), 0)
    return jnp.where(ids == slot_row, 1.0, 0.0).astype(bf16)


def to_rows(x, heads):
    hd = x.shape[1] // heads
    return jnp.concatenate([x[:, h * hd : (h + 1) * hd] for h in range(heads)], axis=0)


def to_cols(x, heads):
    c = x.shape[0] // heads
    return jnp.concatenate([x[h * c : (h + 1) * c] for h in range(heads)], axis=1)


def softmax_rows(qr, kd, span, heads):
    rows, keys = qr.shape[0], kd.shape[0]
    c = rows // heads
    u = lax.broadcasted_iota(jnp.int32, (c, keys), 1)
    allowed = (u >= span[:, 0:1]) & (u <= span[:, 1:2])
    s = dot_nt(qr, kd) * (kd.shape[1] ** (-0.5))
    s = jnp.where(allowed[None], s.reshape(heads, c, keys), neg_big)
    top = jnp.max(s, axis=2, keepdims=True)
    e = jnp.exp(s - top)
    p = e / jnp.sum(e, axis=2, keepdims=True)
    return p.reshape(rows, keys)


def attn_fwd_kernel(heads, slot_ref, span_ref, q_ref, kv_ref, o_ref, kd_ref):
    m, _, c, w = kv_ref.shape
    hd = w // 2
    oh = key_onehot(slot_ref[0], m * c)
    kvd = dot_tn(oh, kv_ref[...].reshape(m * c, w)).astype(bf16)
    kd_ref[0] = kvd
    qr = to_rows(q_ref[0], heads)
    p = softmax_rows(qr, kvd[:, :hd], span_ref[0], heads).astype(bf16)
    o = dot_nn(p, kvd[:, hd:]).astype(bf16)
    o_ref[0] = to_cols(o, heads)


def attn_bwd_kernel(heads, slot_ref, span_ref, q_ref, do_ref, kd_ref, dq_ref, ds_ref):
    m, _, c, w = ds_ref.shape
    hd = w // 2
    kvd = kd_ref[0]
    kd, vd = kvd[:, :hd], kvd[:, hd:]
    qr = to_rows(q_ref[0], heads)
    dor = to_rows(do_ref[0], heads)
    p = softmax_rows(qr, kd, span_ref[0], heads)
    dp = dot_nt(dor, vd)
    rd = jnp.sum(dp * p, axis=1, keepdims=True)
    ds = (p * (dp - rd)).astype(bf16)
    sc = hd ** (-0.5)
    dq = (dot_nn(ds, kd) * sc).astype(bf16)
    dq_ref[0] = to_cols(dq, heads)
    dk = dot_tn(ds, qr) * sc
    dv = dot_tn(p.astype(bf16), dor)
    dkv = jnp.concatenate([dk, dv], axis=1).astype(bf16)
    oh = key_onehot(slot_ref[0], m * c)
    ds_ref[...] = dot_nn(oh, dkv).astype(bf16).reshape(ds_ref.shape)


def attn_fwd(heads, slot, span, qpad, kvs):
    m, c, w = kvs.shape[0], kvs.shape[2], kvs.shape[3]
    length = slot.shape[2]
    d = qpad.shape[2]
    return pl.pallas_call(
        lambda *refs: attn_fwd_kernel(heads, *refs),
        grid=(m,),
        in_specs=[
            pl.BlockSpec((1, 1, length), lambda k: (k, 0, 0)),
            pl.BlockSpec((1, c, 2), lambda k: (k, 0, 0)),
            pl.BlockSpec((1, c, d), lambda k: (k, 0, 0)),
            pl.BlockSpec((m, 1, c, w), lambda k: (0, k, 0, 0)),
        ],
        out_specs=[
            pl.BlockSpec((1, c, d), lambda k: (k, 0, 0)),
            pl.BlockSpec((1, length, w), lambda k: (k, 0, 0)),
        ],
        out_shape=[
            jax.ShapeDtypeStruct((m, c, d), bf16),
            jax.ShapeDtypeStruct((m, length, w), bf16),
        ],
        compiler_params=pltpu.CompilerParams(vmem_limit_bytes=VMEM_LIMIT),
    )(slot, span, qpad, kvs)


def attn_bwd(heads, slot, span, qpad, dopad, kd):
    m, c, d = qpad.shape
    length, w = kd.shape[1], kd.shape[2]
    return pl.pallas_call(
        lambda *refs: attn_bwd_kernel(heads, *refs),
        grid=(m,),
        in_specs=[
            pl.BlockSpec((1, 1, length), lambda k: (k, 0, 0)),
            pl.BlockSpec((1, c, 2), lambda k: (k, 0, 0)),
            pl.BlockSpec((1, c, d), lambda k: (k, 0, 0)),
            pl.BlockSpec((1, c, d), lambda k: (k, 0, 0)),
            pl.BlockSpec((1, length, w), lambda k: (k, 0, 0)),
        ],
        out_specs=[
            pl.BlockSpec((1, c, d), lambda k: (k, 0, 0)),
            pl.BlockSpec((m, 1, c, w), lambda k: (0, k, 0, 0)),
        ],
        out_shape=[
            jax.ShapeDtypeStruct((m, c, d), bf16),
            jax.ShapeDtypeStruct((m, m, c, w), bf16),
        ],
        compiler_params=pltpu.CompilerParams(vmem_limit_bytes=VMEM_LIMIT),
    )(slot, span, qpad, dopad, kd)


class Gather:
    def __init__(self, members, own, full, send_sem, recv_sem):
        self.members = members
        self.me, self.rep = lax.axis_index("shard"), lax.axis_index("rep")
        self.own, self.full = own, full
        self.send_sem, self.recv_sem = send_sem, recv_sem
        self.bits = [1 << i for i in range(1, members.bit_length() - 1)]
        self.planes = [o for o in range(0, members, 2)]
        self.sent = {}

    def partners(self):
        near = [(self.me ^ b, self.rep) for b in [1] + self.bits]
        return near + [(self.me, self.rep ^ 1)]

    def place(self, kind, slot, offset):
        return self.full[kind].at[slot, self.me ^ offset]

    def copy(self, kind, slot, offset, there, to, from_own, to_slot):
        mine = self.sent.setdefault((kind, slot), {})
        at = mine.setdefault((offset, there, to_slot), len(mine))
        src = self.own[kind](slot) if from_own else self.place(kind, slot, offset)
        cp = pltpu.make_async_remote_copy(
            src, self.full[kind].at[to_slot, self.me ^ offset],
            self.send_sem.at[kind, slot, at], self.recv_sem.at[kind, to_slot, there],
            device_id=to, device_id_type=pl.DeviceIdType.MESH)
        cp.start()

    def wait(self, kind, slot, offset):
        piece = self.place(kind, slot, offset)
        pltpu.make_async_copy(piece, piece, self.recv_sem.at[kind, slot, offset]).wait()

    def order(self, kind):
        return self.bits if kind % 2 == 0 else self.bits[::-1]

    def stage(self, kind, offset):
        return max(i for i, b in enumerate(self.order(kind)) if offset & b)

    def issue(self, slot, kinds, plane=True):
        for kind in kinds:
            if plane:
                for b in self.order(kind):
                    self.copy(kind, slot, 0, b, (self.me ^ b, self.rep), True, slot)
        for kind in kinds:
            self.copy(kind, slot, 0, 1, (self.me ^ 1, self.rep), True, slot)

    def arrive(self, slot, kinds, direct, swap_to=None):
        for kind in kinds:
            order = self.order(kind)
            some = [o for o in self.planes if o and (bin(o).count("1") == 1) == direct]
            some.sort(key=lambda o: self.stage(kind, o))
            for o in some:
                self.wait(kind, slot, o)
                for i in range(self.stage(kind, o) + 1, len(order)):
                    self.copy(kind, slot, o, o ^ order[i], (self.me ^ order[i], self.rep), False, slot)
                if swap_to is not None:
                    self.copy(kind, slot, o, o, (self.me, self.rep ^ 1), False, swap_to)
                self.copy(kind, slot, o, o ^ 1, (self.me ^ 1, self.rep), False, slot)

    def swapped(self, slot, kinds):
        for kind in kinds:
            for o in self.planes:
                if o:
                    self.wait(kind, slot, o)
                    self.copy(kind, slot, o, o ^ 1, (self.me ^ 1, self.rep), False, slot)

    def ready(self, slot, kinds):
        for kind in kinds:
            for o in range(1, self.members, 2):
                self.wait(kind, slot, o)

    def finish(self):
        for (kind, slot), mine in self.sent.items():
            piece = self.place(kind, slot, 0)
            for at in mine.values():
                pltpu.make_async_copy(piece, piece, self.send_sem.at[kind, slot, at]).wait()


U, V, C = (0, 1, 2), (3, 4, 5), (6, 7)
SLOTS = 8
BOTH = (0, 1)


def chunk_of(slot, parity):
    slot = jnp.int32(slot)
    low = jnp.where(slot < 3, slot, slot + 2)
    high = jnp.where(slot < 3, slot + 5, slot - 3)
    return jnp.where(slot >= 6, slot - 3, jnp.where(parity == 0, low, high))


MLP_ORDER = (0, 1, 3, 2, 6, 4, 7, 5)


def mlp_kernel(members, m_ref, dy_ref, low_ref, e_ref, we_ref, wr_ref, be_ref, bup_ref, adn_ref,
               y_ref, dm_ref, lowr_ref, er_ref, gup_ref, gdn_ref, ge_ref, gr_ref,
               we_v, wr_v, send_sem, recv_sem, load_sem):
    parity = lax.rem(lax.axis_index("rep"), 2)
    g = Gather(members,
               (lambda slot: we_ref.at[chunk_of(slot, parity)], lambda slot: wr_ref.at[chunk_of(slot, parity)]),
               (ge_ref, gr_ref), send_sem, recv_sem)
    barrier = pltpu.get_barrier_semaphore()
    for to in g.partners():
        pl.semaphore_signal(barrier, inc=1, device_id=to, device_id_type=pl.DeviceIdType.MESH)
    pl.semaphore_wait(barrier, len(g.partners()))

    g.issue(U[0], BOTH)
    y_ref[...] = jnp.zeros_like(y_ref)
    dm_ref[...] = jnp.zeros_like(dm_ref)
    lowr_ref[...] = jnp.zeros_like(lowr_ref)
    er_ref[...] = jnp.zeros_like(er_ref)
    def load(slot, buf):
        out = []
        for kind, held in enumerate((we_v, wr_v)):
            for o in range(members):
                src = g.own[kind](slot) if o == 0 else g.place(kind, slot, o)
                out.append(pltpu.make_async_copy(src, held.at[buf, g.me ^ o], load_sem.at[kind, buf, o]))
        return out

    def fetch(slot, buf):
        g.ready(slot, BOTH)
        for cp in load(slot, buf):
            cp.start()

    def before(i):
        if i == 0:
            g.arrive(U[0], BOTH, True, V[0])
            g.issue(U[1], BOTH)
            g.arrive(U[0], BOTH, False, V[0])
            for slot in V:
                g.issue(slot, BOTH, False)
        if i == 1:
            g.arrive(U[1], BOTH, True, V[1])
            g.issue(U[2], BOTH)
            g.arrive(U[1], BOTH, False, V[1])
        if i == 2:
            g.swapped(V[0], BOTH)
        if i == 3:
            g.arrive(U[2], BOTH, True, V[2])
            g.issue(C[0], BOTH)
            g.arrive(U[2], BOTH, False, V[2])
        if i == 4:
            g.arrive(C[0], BOTH, True)
            g.issue(C[1], BOTH)
            g.arrive(C[0], BOTH, False)
        if i == 5:
            g.swapped(V[1], BOTH)
        if i == 6:
            g.arrive(C[1], BOTH, True)
            g.arrive(C[1], BOTH, False)
        if i == 7:
            g.swapped(V[2], BOTH)
        fetch(MLP_ORDER[i], i % 2)

    def step(n, _):
        buf = lax.rem(n, 2)
        slot = jnp.int32(0)
        for i, q in enumerate(MLP_ORDER):
            slot = jnp.where(n == i, q, slot)
        for cp in load(slot, buf):
            cp.wait()
        j = chunk_of(slot, parity)
        rows, fc = we_v.shape[2], we_v.shape[3]
        we = we_v[buf].reshape(members * rows, fc)
        wr = wr_v[buf].reshape(fc, wr_v.shape[3])
        bup, adn = bup_ref[j], adn_ref[j]
        hid = dot_nn(m_ref[...], we) + be_ref[j].astype(f32)
        hid = hid + scale_lora * dot_nn(low_ref[...], bup)
        cube = hid * hid * hid
        t = jnp.tanh(gelu_c * (hid + 0.044715 * cube))
        act = (0.5 * hid * (1.0 + t)).astype(bf16)
        slope = 0.5 * (1.0 + t) + 0.5 * hid * (1.0 - t * t) * (
            gelu_c * (1.0 + 3.0 * 0.044715 * hid * hid)
        )
        dact = dot_nt(dy_ref[...], wr) + dot_nn(e_ref[...], adn)
        dh = (dact * slope).astype(bf16)
        for i in range(1, SLOTS):
            pl.when(n == i - 1)(lambda i=i: before(i))
        y_ref[...] += dot_nn(act, wr)
        dm_ref[...] += dot_nt(dh, we)
        lowr_ref[...] += dot_nt(act, adn)
        er_ref[...] += dot_nt(dh, bup)
        gup = (scale_lora * dot_tn(low_ref[...], dh)).astype(bf16)
        gdn = dot_tn(e_ref[...], act).astype(bf16)
        sub = fc // members
        for to in range(members):
            gup_ref[to, j] = gup[:, to * sub : (to + 1) * sub]
            gdn_ref[to, j] = gdn[:, to * sub : (to + 1) * sub]
        return 0

    before(0)
    lax.fori_loop(0, SLOTS, step, 0)
    g.finish()


def mlp(members, m, dy, low3, e4, we, wr, be, bup, adn):
    n, d = m.shape
    chunks, rows, fc = we.shape
    sub = wr.shape[1]
    rk = low3.shape[1]
    vm = pl.BlockSpec(memory_space=pltpu.VMEM)
    hbm = pl.BlockSpec(memory_space=pl.ANY)
    sends = members - 1 + members // 2
    return pl.pallas_call(
        lambda *refs: mlp_kernel(members, *refs),
        in_specs=[vm, vm, vm, vm, hbm, hbm, vm, vm, vm],
        out_specs=[vm] * 6 + [hbm] * 2,
        out_shape=[
            jax.ShapeDtypeStruct((n, d), f32),
            jax.ShapeDtypeStruct((n, d), f32),
            jax.ShapeDtypeStruct((n, rk), f32),
            jax.ShapeDtypeStruct((n, rk), f32),
            jax.ShapeDtypeStruct((members, chunks, rk, sub), bf16),
            jax.ShapeDtypeStruct((members, chunks, rk, sub), bf16),
            jax.ShapeDtypeStruct((chunks, members, rows, fc), bf16),
            jax.ShapeDtypeStruct((chunks, members, sub, d), bf16),
        ],
        scratch_shapes=[
            pltpu.VMEM((2, members, rows, fc), bf16),
            pltpu.VMEM((2, members, sub, d), bf16),
            pltpu.SemaphoreType.DMA((2, SLOTS, sends)),
            pltpu.SemaphoreType.DMA((2, SLOTS, members)),
            pltpu.SemaphoreType.DMA((2, 2, members)),
        ],
        compiler_params=pltpu.CompilerParams(
            vmem_limit_bytes=VMEM_LIMIT, collective_id=1, has_side_effects=True),
    )(m, dy, low3, e4, we, wr, be, bup, adn)


def grads_kernel(scales, *refs):
    out = refs[-1]
    at = 0
    for i, sc in enumerate(scales):
        left, right = refs[2 * i][...], refs[2 * i + 1][...]
        owners = out.shape[0]
        w = right.shape[1] // owners
        g = dot_tn(left, right) * sc
        for to in range(owners):
            out[to, :, at : at + w] = g[:, to * w : (to + 1) * w].astype(bf16)
        at += w


def grads(owners, pairs):
    rk = pairs[0][0].shape[1]
    width = sum(p[1].shape[1] for p in pairs) // owners
    vm = pl.BlockSpec(memory_space=pltpu.VMEM)
    return pl.pallas_call(
        lambda *refs: grads_kernel([p[2] for p in pairs], *refs),
        in_specs=[vm] * (2 * len(pairs)),
        out_specs=vm,
        out_shape=jax.ShapeDtypeStruct((owners, rk, width), bf16),
        compiler_params=pltpu.CompilerParams(vmem_limit_bytes=VMEM_LIMIT),
    )(*[x for p in pairs for x in p[:2]])


def exchange(v, axis, bit):
    return lax.ppermute(v, axis, [(i, i ^ bit) for i in range(lax.axis_size(axis))])


def reduce_share(parts, turn):
    me = lax.axis_index("shard")
    count = parts.shape[0].bit_length() - 1
    left = list(range(count))[::-1]
    cur = parts.reshape((2,) * count + parts.shape[1:])
    order = [0] + (list(range(1, count)) if turn == 0 else list(range(1, count))[::-1])
    for i, bit in enumerate(order):
        pos = left.index(bit)
        mine = (me >> bit) & 1
        send = lax.dynamic_index_in_dim(cur, 1 - mine, pos, keepdims=False)
        keep = lax.dynamic_index_in_dim(cur, mine, pos, keepdims=False)
        cur = keep.astype(f32) + exchange(send, "shard", 1 << bit).astype(f32)
        left.remove(bit)
        if i + 1 < count:
            cur = cur.astype(bf16)
    bit = 1
    while bit < lax.axis_size("rep"):
        low = cur.astype(bf16)
        cur = low.astype(f32) + exchange(low, "rep", bit).astype(f32)
        bit *= 2
    return cur


def norm_parts(v):
    center = v - jnp.mean(v, axis=-1, keepdims=True)
    inv = lax.rsqrt(jnp.mean(center * center, axis=-1, keepdims=True) + eps)
    return center * inv, inv


def norm_back(n, inv, gain, dn):
    w = gain * dn
    return (w - jnp.mean(w, axis=-1, keepdims=True)
            - n * jnp.mean(w * n, axis=-1, keepdims=True)) * inv


def local(tokens, out_grad, token_perm, seq_lens, adapter_ids,
          attn_g, attn_b, wq, bq, wkv, bv, wmix, bmix, mlp_g, mlp_b, wexp, bexp, wred, bred,
          q_dn, q_up, kv_dn, kv_up, mix_dn, mix_up, exp_dn, exp_up, red_dn, red_up):
    members = lax.axis_size("shard")
    replicas = lax.axis_size("rep")
    me = lax.axis_index("shard")
    rep = lax.axis_index("rep")
    length, d = tokens.shape
    cap = 3 * length // (2 * members)
    slots = members * cap
    block = me * replicas + rep
    experts, rank = q_dn.shape[:2]
    rk = experts * rank
    seqs = seq_lens.shape[1]
    projs = adapter_ids.shape[2]
    hd = bv.shape[0] * members
    heads = d // hd
    ff = wexp.shape[1]
    chunks = 8
    sub = ff // members // chunks
    fc = sub * members

    smalls = [attn_g, attn_b, bq, bmix, mlp_g, mlp_b, bred, bexp, bv]
    small = lax.all_gather(jnp.concatenate(smalls)[None], "shard", axis=0, tiled=True)
    wide = []
    at = 0
    for part in smalls:
        wide.append(small[:, at : at + part.shape[0]])
        at += part.shape[0]
    attn_gain, attn_bias, q_bias, mix_bias, mlp_gain, mlp_bias, red_bias = (
        w.reshape(-1).astype(f32) for w in wide[:7])
    be = wide[7].reshape(members, chunks, sub).transpose(1, 0, 2).reshape(chunks, 1, fc)
    v_bias = wide[8].reshape(-1).astype(f32)
    table = jnp.concatenate([seq_lens[0], adapter_ids[0].reshape(-1)])[None]
    table = lax.all_gather(table, "shard", axis=0, tiled=True)
    lens, ids = table[:, :seqs], table[:, seqs:].reshape(members, seqs, projs)

    attn_w = lax.all_gather(jnp.concatenate([wq, wkv, wmix], axis=1), "shard", axis=0, tiled=True)
    wq_f, wkv_f, wmix_f = attn_w[:, :d], attn_w[:, d : d + 2 * hd], attn_w[:, d + 2 * hd :]
    we_c = wexp.reshape(wexp.shape[0], members, chunks, sub).transpose(2, 0, 1, 3)
    we_c = we_c.reshape(chunks, wexp.shape[0], fc)
    wr_c = wred.reshape(chunks, sub, d)

    group = lax.dynamic_index_in_dim(
        token_perm.reshape(members, replicas, length), rep, 1, keepdims=False)
    src = group // (length * replicas)
    places = jnp.arange(length, dtype=jnp.int32)
    same = (src[:, :, None] == src[:, None, :]) & (places[None, None, :] < places[None, :, None])
    order = jnp.sum(same.astype(jnp.int32), axis=2)
    key_slot = (src * cap + order).reshape(members, 1, length)
    ends = jnp.sum(jnp.where(jnp.arange(seqs)[:, None] >= jnp.arange(seqs)[None, :],
                             lens[:, None, :], 0), axis=2)
    seg = jnp.sum((places[None, :, None] >= ends[:, None, :]).astype(jnp.int32), axis=2)
    start = jnp.sum(jnp.where(places[None, :, None] >= ends[:, None, :], lens[:, None, :], 0), axis=2)
    hit = (src == me)[:, None, :] & (order[:, None, :] == jnp.arange(cap)[None, :, None])

    def pick(values, empty):
        return jnp.sum(jnp.where(hit, values[:, None, :] - empty, 0), axis=2) + empty

    tok = pick(group - block * length, -1)
    lo = pick(start, 1)
    hi = pick(jnp.broadcast_to(places, group.shape), 0)
    span = jnp.stack([lo, hi], axis=2)
    slot_seg = pick(seg, 0)
    put = (tok.reshape(slots, 1) == places[None, :]).astype(bf16)
    seg_hits = slot_seg[:, :, None] == jnp.arange(seqs)[None, None, :]
    slot_ids = jnp.sum(jnp.where(seg_hits[:, :, :, None], ids[:, None, :, :], 0), axis=2)
    chosen = dot_tn(put, slot_ids.reshape(slots, projs).astype(bf16)).astype(jnp.int32)
    owner = jnp.arange(rk, dtype=jnp.int32) // rank
    masks = [(owner[None, :] == chosen[:, p : p + 1]).astype(f32) for p in range(projs)]

    flat = lambda s: s.reshape(rk, s.shape[2])
    q_dn, q_up, kv_dn, kv_up, mix_dn, mix_up, exp_dn, exp_up, red_dn, red_up = map(
        flat, (q_dn, q_up, kv_dn, kv_up, mix_dn, mix_up, exp_dn, exp_up, red_dn, red_up))
    by_chunk = lambda s: s.reshape(rk, members, chunks, sub).transpose(2, 0, 1, 3).reshape(chunks, rk, fc)

    x = tokens.astype(f32)
    nx, inv_x = norm_parts(x)
    a = (nx * attn_gain + attn_bias).astype(bf16)
    both = dot_nt(a, jnp.concatenate([q_dn, kv_dn], axis=0))
    low0 = (both[:, :rk] * masks[0]).astype(bf16)
    low1 = (both[:, rk:] * masks[1]).astype(bf16)
    q = (dot_nn(a, wq_f) + q_bias + scale_lora * dot_nn(low0, q_up)).astype(bf16)
    kv_bias = jnp.concatenate([jnp.zeros((hd,), f32), v_bias])
    kv = (dot_nn(a, wkv_f) + kv_bias + scale_lora * dot_nn(low1, kv_up)).astype(bf16)
    kvp = dot_nn(put, kv).astype(bf16).reshape(members, cap, 2 * hd)
    kvs = lax.all_gather(kvp, "shard", axis=0, tiled=False)
    qpad = dot_nn(put, q).astype(bf16).reshape(members, cap, d)
    opad, kd = attn_fwd(heads, key_slot, span, qpad, kvs)
    o = dot_tn(put, opad.reshape(slots, d)).astype(bf16)
    low2 = (dot_nt(o, mix_dn) * masks[2]).astype(bf16)
    resid = x + dot_nn(o, wmix_f) + mix_bias + scale_lora * dot_nn(low2, mix_up)

    nr, inv_r = norm_parts(resid)
    m = (nr * mlp_gain + mlp_bias).astype(bf16)
    low3 = (dot_nt(m, exp_dn) * masks[3]).astype(bf16)
    e4 = (scale_lora * dot_nt(out_grad, red_up) * masks[4]).astype(bf16)
    y, dm, low4, e3, g_exp_up, g_red_dn, _, _ = mlp(
        members, m, out_grad, low3, e4, we_c, wr_c, be, by_chunk(exp_up), by_chunk(red_dn))
    r_exp_up = reduce_share(g_exp_up, 0)
    r_red_dn = reduce_share(g_red_dn, 1)
    low4 = (low4 * masks[4]).astype(bf16)
    layer_out = (resid + y + red_bias + scale_lora * dot_nn(low4, red_up)).astype(bf16)
    e3 = (scale_lora * e3 * masks[3]).astype(bf16)
    dm = dm + dot_nn(e3, exp_dn)
    dres = out_grad.astype(f32) + norm_back(nr, inv_r, mlp_gain, dm)

    def stack(g):
        return g.reshape(experts, rank, g.shape[1])

    def stack_chunks(g):
        return stack(g.transpose(1, 0, 2).reshape(rk, chunks * sub))

    dresl = dres.astype(bf16)
    e2 = (scale_lora * dot_nt(dresl, mix_up) * masks[2]).astype(bf16)
    do = (dot_nt(dresl, wmix_f) + dot_nn(e2, mix_dn)).astype(bf16)
    r_down = reduce_share(grads(members, [(e3, m, 1.0), (e2, o, 1.0)]), 0)
    r_up = reduce_share(grads(members, [(low4, out_grad, scale_lora), (low2, dresl, scale_lora)]), 1)
    dopad = dot_nn(put, do).astype(bf16).reshape(members, cap, d)
    dqpad, dslots = attn_bwd(heads, key_slot, span, qpad, dopad, kd)
    got = lax.all_to_all(dslots, "shard", split_axis=0, concat_axis=0, tiled=True)
    dkvp = jnp.sum(got.astype(f32), axis=0).astype(bf16).reshape(slots, 2 * hd)
    dq = dot_tn(put, dqpad.reshape(slots, d)).astype(bf16)
    dkv = dot_tn(put, dkvp).astype(bf16)
    e0 = (scale_lora * dot_nt(dq, q_up) * masks[0]).astype(bf16)
    e1 = (scale_lora * dot_nt(dkv, kv_up) * masks[1]).astype(bf16)
    da = (dot_nt(dq, wq_f) + dot_nn(e0, q_dn)) + (dot_nt(dkv, wkv_f) + dot_nn(e1, kv_dn))
    tokens_grad = (dres + norm_back(nx, inv_x, attn_gain, da)).astype(bf16)
    r_qkv_down = reduce_share(grads(members, [(e0, a, 1.0), (e1, a, 1.0)]), 0)
    r_qkv_up = reduce_share(grads(members, [(low0, dq, scale_lora), (low1, dkv, scale_lora)]), 1)
    w = d // members
    return (layer_out, tokens_grad, stack(r_qkv_down[:, :w]), stack(r_qkv_up[:, :w]), stack(r_qkv_down[:, w:]),
            stack(r_qkv_up[:, w:]), stack(r_down[:, w:]), stack(r_up[:, w:]), stack(r_down[:, :w]),
            stack_chunks(r_exp_up), stack_chunks(r_red_dn), stack(r_up[:, :w]))


def solution(mesh):
    both = ("shard", "rep")
    row, vec = P("shard", None), P("shard")
    in_specs = (
        P(both, None), P(both, None), P(), P(both, None), P(both, None, None),
        vec, vec, row, vec, row, vec, row, vec, vec, vec, row, vec, row, vec,
    ) + (P(),) * 10
    out_specs = (P(both, None), P(both, None)) + (P(None, None, "shard"),) * 10
    return jax.shard_map(local, mesh=mesh, in_specs=in_specs, out_specs=out_specs, check_vma=False)
```

```python
import jax
import jax.numpy as jnp
from jax import lax
from jax.experimental import pallas as pl
from jax.experimental.pallas import tpu as pltpu
from jax.sharding import PartitionSpec as P

scale_lora = 0.5
eps = 1e-05
f32 = jnp.float32
bf16 = jnp.bfloat16
neg_big = -1e30
gelu_c = 0.7978845608028654
VMEM_LIMIT = 60 * 1024 * 1024


def dot_nn(a, b):
    return lax.dot_general(a, b, (((1,), (0,)), ((), ())), preferred_element_type=f32)


def dot_nt(a, b):
    return lax.dot_general(a, b, (((1,), (1,)), ((), ())), preferred_element_type=f32)


def dot_tn(a, b):
    return lax.dot_general(a, b, (((0,), (0,)), ((), ())), preferred_element_type=f32)


def key_onehot(slot_row, slots):
    ids = lax.broadcasted_iota(jnp.int32, (slots, slot_row.shape[1]), 0)
    return jnp.where(ids == slot_row, 1.0, 0.0).astype(bf16)


def to_rows(x, heads):
    hd = x.shape[1] // heads
    return jnp.concatenate([x[:, h * hd : (h + 1) * hd] for h in range(heads)], axis=0)


def to_cols(x, heads):
    c = x.shape[0] // heads
    return jnp.concatenate([x[h * c : (h + 1) * c] for h in range(heads)], axis=1)


def softmax_rows(qr, kd, span, heads):
    rows, keys = qr.shape[0], kd.shape[0]
    c = rows // heads
    u = lax.broadcasted_iota(jnp.int32, (c, keys), 1).astype(f32)
    allowed = (u >= span[:, 0:1]) & (u <= span[:, 1:2])
    s = dot_nt(qr, kd) * (kd.shape[1] ** (-0.5))
    s = jnp.where(allowed[None], s.reshape(heads, c, keys), neg_big)
    top = jnp.max(s, axis=2, keepdims=True)
    e = jnp.exp(s - top)
    p = e / jnp.sum(e, axis=2, keepdims=True)
    return p.reshape(rows, keys)


def attn_bwd_kernel(heads, slot_ref, span_ref, q_ref, do_ref, kd_ref, dq_ref, ds_ref):
    m, _, c, w = ds_ref.shape
    hd = w // 2
    kvd = kd_ref[0]
    kd, vd = kvd[:, :hd], kvd[:, hd:]
    qr = to_rows(q_ref[0], heads)
    dor = to_rows(do_ref[0], heads)
    p = softmax_rows(qr, kd, span_ref[0], heads)
    dp = dot_nt(dor, vd)
    rd = jnp.sum(dp * p, axis=1, keepdims=True)
    ds = (p * (dp - rd)).astype(bf16)
    sc = hd ** (-0.5)
    dq = (dot_nn(ds, kd) * sc).astype(bf16)
    dq_ref[0] = to_cols(dq, heads)
    dk = dot_tn(ds, qr) * sc
    dv = dot_tn(p.astype(bf16), dor)
    dkv = jnp.concatenate([dk, dv], axis=1).astype(bf16)
    oh = key_onehot(slot_ref[0], m * c)
    ds_ref[...] = dot_nn(oh, dkv).astype(bf16).reshape(ds_ref.shape)


def attn_bwd(heads, slot, span, qpad, dopad, kd):
    m, c, d = qpad.shape
    length, w = kd.shape[1], kd.shape[2]
    return pl.pallas_call(
        lambda *refs: attn_bwd_kernel(heads, *refs),
        grid=(m,),
        in_specs=[
            pl.BlockSpec((1, 1, length), lambda k: (k, 0, 0)),
            pl.BlockSpec((1, c, 128), lambda k: (k, 0, 0)),
            pl.BlockSpec((1, c, d), lambda k: (k, 0, 0)),
            pl.BlockSpec((1, c, d), lambda k: (k, 0, 0)),
            pl.BlockSpec((1, length, w), lambda k: (k, 0, 0)),
        ],
        out_specs=[
            pl.BlockSpec((1, c, d), lambda k: (k, 0, 0)),
            pl.BlockSpec((m, 1, c, w), lambda k: (0, k, 0, 0)),
        ],
        out_shape=[
            jax.ShapeDtypeStruct((m, c, d), bf16),
            jax.ShapeDtypeStruct((m, m, c, w), bf16),
        ],
        compiler_params=pltpu.CompilerParams(vmem_limit_bytes=VMEM_LIMIT),
    )(slot, span, qpad, dopad, kd)


MESH = pl.DeviceIdType.MESH


class Gather:
    def __init__(self, members, own, full, slots, send_sem, recv_sem):
        self.members = members
        self.me, self.rep = lax.axis_index("shard"), lax.axis_index("rep")
        self.own, self.full = own, full
        self.base = [sum(slots[:i]) for i in range(len(slots))]
        self.send_sem, self.recv_sem = send_sem, recv_sem
        self.bits = [1 << i for i in range(1, members.bit_length() - 1)]
        self.planes = list(range(0, members, 2))
        self.sent = {}

    def place(self, kind, slot, offset):
        return self.full[kind].at[slot, self.me ^ offset]

    def copy(self, kind, slot, offset, there, to, to_slot):
        mine = self.sent.setdefault((kind, slot), {})
        at = mine.setdefault((offset, there, to_slot), len(mine))
        src = self.own[kind](slot) if offset == 0 else self.place(kind, slot, offset)
        pltpu.make_async_remote_copy(
            src, self.full[kind].at[to_slot, self.me ^ offset],
            self.send_sem.at[self.base[kind] + slot, at],
            self.recv_sem.at[self.base[kind] + to_slot, there],
            device_id=to, device_id_type=MESH).start()

    def wait(self, kind, slot, offset):
        piece = self.place(kind, slot, offset)
        pltpu.make_async_copy(piece, piece, self.recv_sem.at[self.base[kind] + slot, offset]).wait()

    def order(self, kind):
        return self.bits if kind % 2 == 0 else self.bits[::-1]

    def stage(self, kind, offset):
        return max(i for i, b in enumerate(self.order(kind)) if offset & b)

    def issue(self, slot, kinds, plane=True):
        for kind in kinds:
            if plane:
                for b in self.order(kind):
                    self.copy(kind, slot, 0, b, (self.me ^ b, self.rep), slot)
            self.copy(kind, slot, 0, 1, (self.me ^ 1, self.rep), slot)

    def arrive(self, slot, kinds, direct, swap_to=None):
        for kind in kinds:
            order = self.order(kind)
            some = [o for o in self.planes if o and (bin(o).count("1") == 1) == direct]
            some.sort(key=lambda o: self.stage(kind, o))
            for o in some:
                self.wait(kind, slot, o)
                for i in range(self.stage(kind, o) + 1, len(order)):
                    self.copy(kind, slot, o, o ^ order[i], (self.me ^ order[i], self.rep), slot)
                if swap_to is not None:
                    self.copy(kind, slot, o, o, (self.me, self.rep ^ 1), swap_to)
                self.copy(kind, slot, o, o ^ 1, (self.me ^ 1, self.rep), slot)

    def swapped(self, slot, kinds):
        for kind in kinds:
            for o in self.planes[1:]:
                self.wait(kind, slot, o)
                self.copy(kind, slot, o, o ^ 1, (self.me ^ 1, self.rep), slot)

    def ready(self, slot, kinds):
        for kind in kinds:
            for o in range(1, self.members, 2):
                self.wait(kind, slot, o)

    def finish(self):
        for (kind, slot), mine in self.sent.items():
            piece = self.place(kind, slot, 0)
            for at in mine.values():
                pltpu.make_async_copy(piece, piece, self.send_sem.at[self.base[kind] + slot, at]).wait()


U, V, C = (0, 1, 2), (3, 4, 5), (6, 7)
SLOTS = 8
WE, WR, AT, AB, KV = range(5)
BOTH, HALVES = (WE, WR), (AT, AB)
WQ, WMIX = 0, 1
SEND, NEAR, FAR, SWAP = range(4)
MLP_ORDER = (0, 3, 4, 1, 2, 6, 5, 7)
SERVE = {
    "p0": ((SEND, KV, 0),),
    "stage": ((SEND, WR, 0),),
    "norm_0": ((NEAR, KV, 0),),
    "idx_1": ((SEND, AT, 0),),
    "idx_5": ((NEAR, WR, 0),),
    "idx_6": ((FAR, KV, 0),),
    "wqneed": ((NEAR, AT, 0), (FAR, WR, 0), (SEND, AB, 0), (SWAP, WR, 3), (FAR, AT, 0), (SEND, WE, 0), (NEAR, AB, 0), (SEND, AB, 1), (NEAR, WE, 0), (FAR, AB, 0),),
    "q_1": ((SEND, WE, 1),),
    "att_0": ((NEAR, AB, 1),),
    "att_1": ((FAR, WE, 0),),
    "att_3": ((SEND, AT, 1),),
    "att_5": ((NEAR, WE, 1),),
    "att_6": ((SWAP, WE, 3),),
    "mixneed": ((FAR, AB, 1), (SEND, WR, 1), (NEAR, AT, 1), (FAR, WE, 1), (SEND, WE, 2), (NEAR, WR, 1), (SWAP, WE, 4), (FAR, AT, 1),),
    "mix_0": ((SEND, WR, 2),),
    "mix_1": ((FAR, WR, 1),),
    "norm2_0": ((NEAR, WE, 2), (SEND, WE, 6),),
    "mlp_0_0": ((NEAR, WR, 2),),
    "mlp_0_1": ((SWAP, WR, 4),),
    "mlp_1_0": ((FAR, WE, 2), (SEND, WR, 6),),
    "mlp_2_0": ((FAR, WR, 2), (NEAR, WE, 6), (SEND, WR, 7),),
    "mlp_3_0": ((NEAR, WR, 6),),
    "mlp_4_0": ((FAR, WE, 6), (SEND, WE, 7),),
    "mlp_4_1": ((FAR, WR, 6),),
    "mlp_5_0": ((NEAR, WR, 7), (SWAP, WE, 5),),
    "mlp_5_1": ((NEAR, WE, 7), (SWAP, WR, 5),),
    "mlp_6_0": ((FAR, WR, 7), (FAR, WE, 7),),
}


def chunk_of(slot, parity):
    slot = jnp.int32(slot)
    low = jnp.where(slot < 3, slot, slot + 2)
    high = jnp.where(slot < 3, slot + 5, slot - 3)
    return jnp.where(slot >= 6, slot - 3, jnp.where(parity == 0, low, high))


def norm_parts(v):
    center = v - jnp.mean(v, axis=-1, keepdims=True)
    inv = lax.rsqrt(jnp.mean(center * center, axis=-1, keepdims=True) + eps)
    return center * inv, inv


def norm_back(n, inv, gain, dn):
    w = gain * dn
    return (w - jnp.mean(w, axis=-1, keepdims=True)
            - n * jnp.mean(w * n, axis=-1, keepdims=True)) * inv


class Sizes:
    def __init__(self, members, replicas, length, d, ff, hd, rk, rank, seqs, projs):
        self.members, self.replicas, self.length, self.d, self.ff = members, replicas, length, d, ff
        self.hd, self.rk, self.rank, self.seqs, self.projs = hd, rk, rank, seqs, projs
        self.heads = d // hd
        self.cap = 3 * length // (2 * members)
        self.slots = members * self.cap
        self.w = 2 * hd
        self.rows = d // members
        self.sub = ff // members // SLOTS
        self.fc = self.sub * members
        self.aligned = self.sub % 128 == 0
        self.small_cols = -(-max(self.rows + self.sub, seqs * (projs + 1)) // 128) * 128


FWD_IN = ("x", "dy", "small", "group", "group_t", "q_dn", "q_up", "kv_dn", "kv_up", "mix_dn", "mix_up",
          "exp_dn", "exp_up", "red_dn", "red_up", "wq", "wkv", "wmix", "wexp", "wred")
FWD_OUT = ("dres", "put", "slot", "info", "chosen", "low0", "low1", "low2", "low4", "e3",
           "a", "q", "o", "m", "resid", "kd", "gup", "gdn", "layer", "kvs", "ge", "gr", "ga", "gb", "gk")
FWD_SCRATCH = ("y", "we_v", "wr_v", "a_v", "q_v", "kvp", "kvb", "kd_st", "gup_st", "gdn_st", "sm",
               "lowr", "er", "low3", "e4",
               "send_sem", "recv_sem", "sm_send", "sm_recv", "kv_send", "kv_recv", "stage_sem", "store_sem",
               "load_sem", "kvb_sem", "kd_sem", "g_sem", "out_sem")


def fwd_kernel(z, *refs):
    r = dict(zip(FWD_IN + FWD_OUT + FWD_SCRATCH, refs))
    members, rows, fc, sub, d, hd = z.members, z.rows, z.fc, z.sub, z.d, z.hd
    length, cap, w, heads, rk = z.length, z.cap, z.w, z.heads, z.rk
    me, rep = lax.axis_index("shard"), lax.axis_index("rep")
    parity = lax.rem(rep, 2)
    half = rows // 2
    att = (r["wq"], r["wmix"])
    g = Gather(
        members,
        [lambda s: r["ge"].at[s, me],
         lambda s: r["wred"].at[chunk_of(s, parity)],
         lambda s: att[s].at[0:half],
         lambda s: att[s].at[half:rows],
         lambda s: r["wkv"]],
        [r["ge"], r["gr"], r["ga"], r["gb"], r["gk"]],
        [SLOTS, SLOTS, 2, 2, 1], r["send_sem"], r["recv_sem"])
    we_v, wr_v, sm, y, dm = r["we_v"], r["wr_v"], r["sm"], r["y"], r["dres"]

    def serve(point):
        for op, kind, slot in SERVE.get(point, ()):
            swap_to = slot + 3 if slot in U and kind in BOTH else None
            if op == SEND:
                g.issue(slot, (kind,))
            elif op == SWAP:
                g.swapped(slot, (kind,))
            else:
                g.arrive(slot, (kind,), op == NEAR, swap_to)

    barrier = pltpu.get_barrier_semaphore()
    others = [(me ^ o, rep) for o in range(1, members)] + [(me, rep ^ 1)]
    for to in others:
        pl.semaphore_signal(barrier, inc=1, device_id=to, device_id_type=MESH)

    def stage_copies(slot):
        j = chunk_of(slot, parity)
        to = we_v.at[0, slot]
        if not z.aligned:
            return [pltpu.make_async_copy(r["wexp"].at[j], to, r["stage_sem"].at[slot])]
        return [pltpu.make_async_copy(
            r["wexp"].at[:, pl.ds(pl.multiple_of(s * (z.ff // members) + j * sub, sub), sub)],
            to.at[:, s * sub : (s + 1) * sub], r["stage_sem"].at[slot]) for s in range(members)]

    def stored(slot):
        return pltpu.make_async_copy(we_v.at[0, slot], r["ge"].at[slot, me], r["store_sem"].at[slot])

    def staged(slot):
        pltpu.make_async_copy(we_v.at[0, slot], we_v.at[0, slot], r["stage_sem"].at[slot]).wait()
        stored(slot).start()

    for slot in range(SLOTS):
        for cp in stage_copies(slot):
            cp.start()
    pl.semaphore_wait(barrier, len(others))

    def small_copy(o):
        return pltpu.make_async_remote_copy(
            r["small"], sm.at[me], r["sm_send"].at[o], r["sm_recv"].at[o],
            device_id=(me ^ o, rep), device_id_type=MESH)

    for o in range(1, members):
        small_copy(o).start()
    serve("p0")
    sm[me] = r["small"][...]
    for slot in range(SLOTS):
        staged(slot)
    for slot in range(SLOTS):
        stored(slot).wait()
    serve("stage")
    for o in range(1, members):
        pltpu.make_async_copy(sm.at[me ^ o], sm.at[me ^ o], r["sm_recv"].at[o]).wait()

    def vec(row):
        return jnp.concatenate([sm[s, row : row + 1, 0:rows] for s in range(members)], axis=1)

    def norm_rows(src, gain, bias, dst, part):
        gv, bv = vec(gain), vec(bias)

        def body(i, _):
            at = pl.ds(pl.multiple_of(i * 128, 128), 128)
            n, _inv = norm_parts(src[at, :].astype(f32))
            dst[at, :] = (n * gv + bv).astype(bf16)
            return 0

        lax.fori_loop(part * length // 256, (part + 1) * length // 256, body, 0)

    for part in range(2):
        serve("norm_%d" % part)
        norm_rows(r["x"], 0, 1, r["a_v"], part)

    t_row = lax.broadcasted_iota(jnp.int32, (1, length), 1)
    before_t = lax.broadcasted_iota(jnp.int32, (length, length), 0) < lax.broadcasted_iota(
        jnp.int32, (length, length), 1)
    c_ids = lax.broadcasted_iota(jnp.int32, (cap, length), 0)
    lane = lax.broadcasted_iota(jnp.int32, (cap, 128), 1)
    span = length * z.replicas
    first = (me * z.replicas + rep) * length
    tf = t_row.astype(f32)
    chosen = jnp.zeros((length, 128), f32)
    for k in range(members):
        serve("idx_%d" % k)
        row = r["group"][k]
        src = lax.div(row, span)
        src_col = lax.div(r["group_t"][:, k : k + 1], span)
        earlier = jnp.where((src_col == src) & before_t, 1.0, 0.0)
        slot_row = src * cap + jnp.sum(earlier, axis=0, keepdims=True).astype(jnp.int32)
        r["slot"][k] = slot_row
        hit = slot_row == c_ids + me * cap

        def pick(values):
            return jnp.sum(jnp.where(hit, values, 0.0), axis=1, keepdims=True)

        full = pick(jnp.ones_like(tf))
        tok = pick((row - first + 1).astype(f32)) - 1.0
        put = jnp.where(tok == tf, 1.0, 0.0).astype(bf16)
        r["put"][k] = put
        end = jnp.zeros((1, 1), f32)
        start = jnp.zeros_like(tf)
        ids = [jnp.zeros_like(tf) for _ in range(z.projs)]
        for j in range(z.seqs):
            n = sm[k, 8:9, j : j + 1]
            inside = (tf >= end) & (tf < end + n)
            end = end + n
            start = start + jnp.where(tf >= end, n, 0.0)
            for p in range(z.projs):
                at = z.seqs + j * z.projs + p
                ids[p] = ids[p] + jnp.where(inside, sm[k, 8:9, at : at + 1], 0.0)
        info = jnp.where(lane == 0, pick(start) + (1.0 - full), 0.0)
        info = jnp.where(lane == 1, pick(tf), info)
        for p in range(z.projs):
            info = jnp.where(lane == 2 + p, pick(ids[p]), info)
        r["info"][k] = info
        chosen = chosen + dot_tn(put, info.astype(bf16))
    r["chosen"][...] = chosen
    rank_of = lax.broadcasted_iota(jnp.int32, (length, rk), 1) // z.rank

    def mask(p):
        return jnp.where(rank_of.astype(f32) == r["chosen"][:, 2 + p : 3 + p], 1.0, 0.0)

    a_v, q_v = r["a_v"], r["q_v"]
    o_v = q_v
    serve("low")
    r["low0"][...] = (dot_nt(a_v[...], r["q_dn"][...]) * mask(0)).astype(bf16)
    r["low1"][...] = (dot_nt(a_v[...], r["kv_dn"][...]) * mask(1)).astype(bf16)
    out_a = pltpu.make_async_copy(a_v, r["a"], r["out_sem"].at[0])
    out_a.start()

    serve("kvneed")
    g.ready(0, (KV,))
    kv_loads = [pltpu.make_async_copy(
        r["wkv"] if o == 0 else g.place(KV, 0, o), we_v.at[1, me ^ o, :, 0:w], r["kv_send"].at[o]) for o in range(members)]
    for cp in kv_loads:
        cp.start()
    for cp in kv_loads:
        cp.wait()
    back_kv = pltpu.make_async_copy(we_v.at[1, me, :, 0:w], g.place(KV, 0, 0), r["kv_send"].at[0])
    back_kv.start()
    vb = jnp.concatenate([sm[s, 7:8, 0 : hd // members] for s in range(members)], axis=1)
    kv_bias = jnp.concatenate([jnp.zeros((1, hd), f32), vb], axis=1)
    kv = (dot_nn(a_v[...], we_v[1, :, :, 0:w].reshape(d, w)) + kv_bias
          + scale_lora * dot_nn(r["low1"][...], r["kv_up"][...])).astype(bf16)
    for k in range(members):
        r["kvp"][k] = dot_nn(r["put"][k], kv).astype(bf16)

    def kv_copy(o):
        return pltpu.make_async_remote_copy(
            r["kvp"], r["kvs"].at[me], r["kv_send"].at[o], r["kv_recv"].at[o],
            device_id=(me ^ o, rep), device_id_type=MESH)

    back_kv.wait()
    own_kv = pltpu.make_async_copy(r["kvp"], r["kvs"].at[me], r["kv_send"].at[0])
    for o in range(1, members):
        kv_copy(o).start()
    own_kv.start()

    for slot in V:
        g.issue(slot, BOTH, False)
    serve("afterkvx")

    def wide_load(which):
        g.ready(which, HALVES)
        out = []
        for kind in HALVES:
            for o in range(members):
                src = g.own[kind](which) if o == 0 else g.place(kind, which, o)
                for c in range(d // fc):
                    out.append(pltpu.make_async_copy(
                        src.at[:, c * fc : (c + 1) * fc],
                        we_v.at[c, me ^ o, (kind - AT) * half : (kind - AT + 1) * half],
                        r["load_sem"].at[kind - AT, c, o]))
        for cp in out:
            cp.start()
        for cp in out:
            cp.wait()
        back = [pltpu.make_async_copy(
            we_v.at[c, me, (kind - AT) * half : (kind - AT + 1) * half],
            g.place(kind, which, 0).at[:, c * fc : (c + 1) * fc],
            r["load_sem"].at[kind - AT, c, 0]) for kind in HALVES for c in range(d // fc)]
        for cp in back:
            cp.start()
        return back

    serve("wqneed")
    back_q = wide_load(WQ)
    q_bias = vec(2)
    for c in range(d // fc):
        serve("q_%d" % c)
        at = slice(c * fc, (c + 1) * fc)
        q_v[:, at] = (dot_nn(a_v[...], we_v[c].reshape(d, fc)) + q_bias[:, at]
                      + scale_lora * dot_nn(r["low0"][...], r["q_up"][:, at])).astype(bf16)
    out_q = pltpu.make_async_copy(q_v, r["q"], r["out_sem"].at[1])
    out_q.start()

    for cp in back_q:
        cp.wait()

    serve("kvxwait")

    for o in range(1, members):
        pltpu.make_async_copy(r["kvs"].at[me ^ o], r["kvs"].at[me ^ o], r["kv_recv"].at[o]).wait()
    own_kv.wait()
    dm[...] = jnp.zeros_like(dm)

    def kvb_load(k, buf):
        return pltpu.make_async_copy(r["kvs"].at[:, k], r["kvb"].at[buf], r["kvb_sem"].at[buf])

    def kd_out(k, buf):
        return pltpu.make_async_copy(r["kd_st"].at[buf], r["kd"].at[k], r["kd_sem"].at[buf])

    kvb_load(0, 0).start()
    groups = 2

    def attend(k, _):
        buf = lax.rem(k, 2)

        @pl.when(k + 1 < members)
        def _():
            kvb_load(k + 1, 1 - buf).start()

        for i in range(members):
            if "att_%d" % i in SERVE:
                pl.when(k == i)(lambda i=i: serve("att_%d" % i))
        kvb_load(k, buf).wait()
        oh = key_onehot(r["slot"][k], z.slots)
        kvd = dot_tn(oh, r["kvb"][buf].reshape(z.slots, w)).astype(bf16)

        @pl.when(k >= 2)
        def _():
            kd_out(k, buf).wait()

        r["kd_st"][buf] = kvd
        kd_out(k, buf).start()
        put = r["put"][k]
        qp = dot_nn(put, q_v[...]).astype(bf16)
        info = r["info"][k]
        outs = []
        per = heads // groups
        for h in range(groups):
            qr = to_rows(qp[:, h * per * hd : (h + 1) * per * hd], per)
            p = softmax_rows(qr, kvd[:, :hd], info, per).astype(bf16)
            outs.append(to_cols(dot_nn(p, kvd[:, hd:]).astype(bf16), per))
        dm[...] += dot_tn(put, jnp.concatenate(outs, axis=1))
        return 0

    lax.fori_loop(0, members, attend, 0)
    out_q.wait()
    o_v[...] = dm[...].astype(bf16)
    out_o = pltpu.make_async_copy(o_v, r["o"], r["out_sem"].at[2])
    out_o.start()
    r["low2"][...] = (dot_nt(o_v[...], r["mix_dn"][...]) * mask(2)).astype(bf16)
    serve("mixneed")
    back_m = wide_load(WMIX)
    mix_bias = vec(3)
    for c in range(d // fc):
        serve("mix_%d" % c)
        at = slice(c * fc, (c + 1) * fc)
        y[:, at] = (r["x"][:, at].astype(f32) + dot_nn(o_v[...], we_v[c].reshape(d, fc)) + mix_bias[:, at]
                    + scale_lora * dot_nn(r["low2"][...], r["mix_up"][:, at]))

    def load(slot, buf):
        out = [pltpu.make_async_copy(r["ge"].at[slot], we_v.at[buf], r["load_sem"].at[0, buf, 0])]
        for o in range(members):
            src = g.own[WR](slot) if o == 0 else g.place(WR, slot, o)
            out.append(pltpu.make_async_copy(src, wr_v.at[buf, me ^ o], r["load_sem"].at[1, buf, o]))
        return out

    def fetch(slot, buf):
        g.ready(slot, BOTH)
        for cp in load(slot, buf):
            cp.start()

    for cp in back_m:
        cp.wait()
    out_r = pltpu.make_async_copy(y, r["resid"], r["out_sem"].at[3])
    out_r.start()
    out_a.wait()
    m_v = a_v
    for part in range(2):
        serve("norm2_%d" % part)
        norm_rows(y, 4, 5, m_v, part)
    serve("low3")
    out_m = pltpu.make_async_copy(m_v, r["m"], r["out_sem"].at[0])
    out_m.start()
    r["low3"][...] = (dot_nt(m_v[...], r["exp_dn"][...]) * mask(3)).astype(bf16)
    r["e4"][...] = (scale_lora * dot_nt(r["dy"][...], r["red_up"][...]) * mask(4)).astype(bf16)
    dm[...] = jnp.zeros_like(dm)
    r["lowr"][...] = jnp.zeros_like(r["lowr"])
    r["er"][...] = jnp.zeros_like(r["er"])
    out_r.wait()
    y[...] += vec(6)

    def g_out(j, buf):
        return (pltpu.make_async_copy(r["gup_st"].at[buf], r["gup"].at[:, j], r["g_sem"].at[0, buf]),
                pltpu.make_async_copy(r["gdn_st"].at[buf], r["gdn"].at[:, j], r["g_sem"].at[1, buf]))

    serve("mlp_f0")
    fetch(MLP_ORDER[0], 0)

    def step(n, _):
        for i in range(SLOTS):
            if "mlp_%d_0" % i in SERVE:
                pl.when(n == i)(lambda i=i: serve("mlp_%d_0" % i))
        buf = lax.rem(n, 2)
        slot = jnp.int32(0)
        for i, q in enumerate(MLP_ORDER):
            slot = jnp.where(n == i, q, slot)
        for cp in load(slot, buf):
            cp.wait()
        j = chunk_of(slot, parity)
        we = we_v[buf].reshape(d, fc)
        wr = wr_v[buf].reshape(fc, d)
        if z.aligned:
            def cut(ref):
                return jnp.concatenate([ref[:, pl.ds(pl.multiple_of(s * (z.ff // members) + j * sub, sub), sub)]
                                        for s in range(members)], axis=1)
            bup, adn = cut(r["exp_up"]), cut(r["red_dn"])
        else:
            bup, adn = r["exp_up"][j], r["red_dn"][j]
        be = jnp.concatenate([sm[s, 0:SLOTS, rows : rows + sub] for s in range(members)], axis=1)
        be = jnp.sum(jnp.where(lax.broadcasted_iota(jnp.int32, (SLOTS, fc), 0) == j, be, 0.0), axis=0, keepdims=True)
        hid = dot_nn(m_v[...], we) + be
        hid = hid + scale_lora * dot_nn(r["low3"][...], bup)
        cube = hid * hid * hid
        t = jnp.tanh(gelu_c * (hid + 0.044715 * cube))
        act = (0.5 * hid * (1.0 + t)).astype(bf16)
        slope = 0.5 * (1.0 + t) + 0.5 * hid * (1.0 - t * t) * (
            gelu_c * (1.0 + 3.0 * 0.044715 * hid * hid)
        )
        dact = dot_nt(r["dy"][...], wr) + dot_nn(r["e4"][...], adn)
        dh = (dact * slope).astype(bf16)
        for i in range(SLOTS):
            def middle(i=i):
                serve("mlp_%d_1" % i)
                if i + 1 < SLOTS:
                    fetch(MLP_ORDER[i + 1], (i + 1) % 2)
            pl.when(n == i)(middle)
        y[...] += dot_nn(act, wr)
        dm[...] += dot_nt(dh, we)
        r["lowr"][...] += dot_nt(act, adn)
        r["er"][...] += dot_nt(dh, bup)
        gup = (scale_lora * dot_tn(r["low3"][...], dh)).astype(bf16)
        gdn = dot_tn(r["e4"][...], act).astype(bf16)

        @pl.when(n >= 2)
        def _():
            for cp in g_out(j, buf):
                cp.wait()

        for to in range(members):
            r["gup_st"][buf, to] = gup[:, to * sub : (to + 1) * sub]
            r["gdn_st"][buf, to] = gdn[:, to * sub : (to + 1) * sub]
        for cp in g_out(j, buf):
            cp.start()
        return 0

    lax.fori_loop(0, SLOTS, step, 0)

    low4 = (r["lowr"][...] * mask(4)).astype(bf16)
    r["low4"][...] = low4
    out_o.wait()
    layer_v = q_v
    for c in range(d // fc):
        at = slice(c * fc, (c + 1) * fc)
        layer_v[:, at] = (y[:, at] + scale_lora * dot_nn(low4, r["red_up"][:, at])).astype(bf16)
    out_l = pltpu.make_async_copy(layer_v, r["layer"], r["out_sem"].at[1])
    out_l.start()
    back_r = pltpu.make_async_copy(r["resid"], y, r["out_sem"].at[3])
    back_r.start()
    e3 = (scale_lora * r["er"][...] * mask(3)).astype(bf16)
    r["e3"][...] = e3
    gain = vec(4)
    back_r.wait()

    def last(i, _):
        at = pl.ds(pl.multiple_of(i * 128, 128), 128)
        n, inv = norm_parts(y[at, :])
        dn = dm[at, :] + dot_nn(r["e3"][at, :], r["exp_dn"][...])
        dm[at, :] = r["dy"][at, :].astype(f32) + norm_back(n, inv, gain, dn)
        return 0

    lax.fori_loop(0, length // 128, last, 0)
    out_l.wait()
    out_m.wait()
    for buf in range(2):
        kd_out(buf, buf).wait()
        for cp in g_out(buf, buf):
            cp.wait()
    for o in range(1, members):
        small_copy(o).wait_send()
        kv_copy(o).wait_send()
    g.finish()


def forward(z, args):
    vm = pl.BlockSpec(memory_space=pltpu.VMEM)
    hbm = pl.BlockSpec(memory_space=pl.ANY)
    m, n, d, rk, w = z.members, z.length, z.d, z.rk, z.w
    s = jax.ShapeDtypeStruct
    half = z.rows // 2
    outs = dict(
        dres=s((n, d), f32), put=s((m, z.cap, n), bf16), slot=s((m, 1, n), jnp.int32),
        info=s((m, z.cap, 128), f32), chosen=s((n, 128), f32),
        low0=s((n, rk), bf16), low1=s((n, rk), bf16), low2=s((n, rk), bf16), low4=s((n, rk), bf16), e3=s((n, rk), bf16),
        a=s((n, d), bf16), q=s((n, d), bf16), o=s((n, d), bf16), m=s((n, d), bf16), resid=s((n, d), f32),
        kd=s((m, n, w), bf16), gup=s((m, SLOTS, rk, z.sub), bf16), gdn=s((m, SLOTS, rk, z.sub), bf16),
        layer=s((n, d), bf16), kvs=s((m, m, z.cap, w), bf16),
        ge=s((SLOTS, m, z.rows, z.fc), bf16), gr=s((SLOTS, m, z.sub, d), bf16),
        ga=s((2, m, half, d), bf16), gb=s((2, m, half, d), bf16), gk=s((1, m, z.rows, w), bf16))
    in_vmem = FWD_OUT[:10]
    sends = m - 1 + m // 2
    dma = pltpu.SemaphoreType.DMA
    items = 2 * SLOTS + 5
    scratch = dict(
        y=pltpu.VMEM((n, d), f32), we_v=pltpu.VMEM((2, m, z.rows, z.fc), bf16), wr_v=pltpu.VMEM((2, m, z.sub, d), bf16),
        a_v=pltpu.VMEM((n, d), bf16), q_v=pltpu.VMEM((n, d), bf16),
        kvp=pltpu.VMEM((m, z.cap, w), bf16), kvb=pltpu.VMEM((2, m, z.cap, w), bf16),
        kd_st=pltpu.VMEM((2, n, w), bf16), gup_st=pltpu.VMEM((2, m, rk, z.sub), bf16),
        gdn_st=pltpu.VMEM((2, m, rk, z.sub), bf16), sm=pltpu.VMEM((m, 16, z.small_cols), f32),
        lowr=pltpu.VMEM((n, rk), f32), er=pltpu.VMEM((n, rk), f32), low3=pltpu.VMEM((n, rk), bf16), e4=pltpu.VMEM((n, rk), bf16),
        send_sem=dma((items, sends)), recv_sem=dma((items, m)), sm_send=dma((m,)), sm_recv=dma((m,)),
        kv_send=dma((m,)), kv_recv=dma((m,)), stage_sem=dma((SLOTS,)), store_sem=dma((SLOTS,)),
        load_sem=dma((2, 2, m)), kvb_sem=dma((2,)), kd_sem=dma((2,)), g_sem=dma((2, 2)), out_sem=dma((4,)))
    got = pl.pallas_call(
        lambda *refs: fwd_kernel(z, *refs),
        in_specs=[hbm if k.startswith("w") else vm for k in FWD_IN],
        out_specs=[vm if k in in_vmem else hbm for k in FWD_OUT],
        out_shape=[outs[k] for k in FWD_OUT],
        scratch_shapes=[scratch[k] for k in FWD_SCRATCH],
        compiler_params=pltpu.CompilerParams(
            vmem_limit_bytes=FWD_VMEM, collective_id=1, has_side_effects=True),
    )(*[args[k] for k in FWD_IN])
    return dict(zip(FWD_OUT, got))


FWD_VMEM = 62 * 1024 * 1024


def grads_kernel(scales, *refs):
    out = refs[-1]
    at = 0
    for i, sc in enumerate(scales):
        left, right = refs[2 * i][...], refs[2 * i + 1][...]
        owners = out.shape[0]
        w = right.shape[1] // owners
        g = dot_tn(left, right) * sc
        for to in range(owners):
            out[to, :, at : at + w] = g[:, to * w : (to + 1) * w].astype(bf16)
        at += w


def grads(owners, pairs):
    rk = pairs[0][0].shape[1]
    width = sum(p[1].shape[1] for p in pairs) // owners
    vm = pl.BlockSpec(memory_space=pltpu.VMEM)
    return pl.pallas_call(
        lambda *refs: grads_kernel([p[2] for p in pairs], *refs),
        in_specs=[vm] * (2 * len(pairs)),
        out_specs=vm,
        out_shape=jax.ShapeDtypeStruct((owners, rk, width), bf16),
        compiler_params=pltpu.CompilerParams(vmem_limit_bytes=VMEM_LIMIT),
    )(*[x for p in pairs for x in p[:2]])


def exchange(v, axis, bit):
    return lax.ppermute(v, axis, [(i, i ^ bit) for i in range(lax.axis_size(axis))])


def reduce_share(parts, turn):
    me = lax.axis_index("shard")
    count = parts.shape[0].bit_length() - 1
    left = list(range(count))[::-1]
    cur = parts.reshape((2,) * count + parts.shape[1:])
    order = [0] + (list(range(1, count)) if turn == 0 else list(range(1, count))[::-1])
    for i, bit in enumerate(order):
        pos = left.index(bit)
        mine = (me >> bit) & 1
        send = lax.dynamic_index_in_dim(cur, 1 - mine, pos, keepdims=False)
        keep = lax.dynamic_index_in_dim(cur, mine, pos, keepdims=False)
        cur = keep.astype(f32) + exchange(send, "shard", 1 << bit).astype(f32)
        left.remove(bit)
        if i + 1 < count:
            cur = cur.astype(bf16)
    bit = 1
    while bit < lax.axis_size("rep"):
        low = cur.astype(bf16)
        cur = low.astype(f32) + exchange(low, "rep", bit).astype(f32)
        bit *= 2
    return cur


def local(tokens, out_grad, token_perm, seq_lens, adapter_ids,
          attn_g, attn_b, wq, bq, wkv, bv, wmix, bmix, mlp_g, mlp_b, wexp, bexp, wred, bred,
          q_dn, q_up, kv_dn, kv_up, mix_dn, mix_up, exp_dn, exp_up, red_dn, red_up):
    members = lax.axis_size("shard")
    replicas = lax.axis_size("rep")
    rep = lax.axis_index("rep")
    length, d = tokens.shape
    experts, rank = q_dn.shape[:2]
    rk = experts * rank
    z = Sizes(members, replicas, length, d, wexp.shape[1], bv.shape[0] * members, rk, rank,
              seq_lens.shape[1], adapter_ids.shape[2])
    flat = lambda s: s.reshape(rk, s.shape[2])
    q_dn, q_up, kv_dn, kv_up, mix_dn, mix_up, exp_dn, exp_up, red_dn, red_up = map(
        flat, (q_dn, q_up, kv_dn, kv_up, mix_dn, mix_up, exp_dn, exp_up, red_dn, red_up))
    group = lax.dynamic_index_in_dim(
        token_perm.reshape(members, replicas, length), rep, 1, keepdims=False)

    def pad(rows, cols):
        return jnp.pad(rows.astype(f32), ((0, 0), (0, cols - rows.shape[1])))

    vecs = jnp.concatenate([v[None] for v in (attn_g, attn_b, bq, bmix, mlp_g, mlp_b, bred)]
                           + [pad(bv[None], z.rows).astype(bf16)], axis=0)
    top = pad(jnp.concatenate([vecs, bexp.reshape(SLOTS, z.sub)], axis=1), z.small_cols)
    table = pad(jnp.concatenate([seq_lens[0], adapter_ids[0].reshape(-1)])[None], z.small_cols)
    small = jnp.concatenate([top, table, jnp.zeros((7, z.small_cols), f32)], axis=0)
    by_chunk = lambda s: s.reshape(s.shape[0], members, SLOTS, z.sub).transpose(2, 0, 1, 3).reshape(
        SLOTS, s.shape[0], z.fc)
    chunked = (lambda s: s) if z.aligned else by_chunk
    got = forward(z, dict(
        x=tokens, dy=out_grad, small=small, group=group.reshape(members, 1, length), group_t=group.T,
        q_dn=q_dn, q_up=q_up, kv_dn=kv_dn, kv_up=kv_up, mix_dn=mix_dn, mix_up=mix_up, exp_dn=exp_dn,
        exp_up=chunked(exp_up), red_dn=chunked(red_dn), red_up=red_up,
        wq=wq, wkv=wkv, wmix=wmix, wexp=chunked(wexp), wred=wred.reshape(SLOTS, z.sub, d)))
    r_exp_up = reduce_share(got["gup"], 0)
    r_red_dn = reduce_share(got["gdn"], 1)
    wq_f, wmix_f = (jnp.stack([got["ga"][i], got["gb"][i]], axis=1).reshape(d, d) for i in (WQ, WMIX))
    wkv_f = got["gk"].reshape(d, z.w)
    attn_gain = lax.all_gather(attn_g, "shard", axis=0, tiled=True).astype(f32)
    owner = jnp.arange(rk, dtype=jnp.int32) // rank
    masks = [(owner[None, :].astype(f32) == got["chosen"][:, 2 + p : 3 + p]).astype(f32) for p in range(3)]
    put = got["put"].reshape(z.slots, length)
    low0, low1, low2, low4, e3 = (got[k] for k in ("low0", "low1", "low2", "low4", "e3"))
    a, o, m, dres, layer_out = (got[k] for k in ("a", "o", "m", "dres", "layer"))
    x = tokens.astype(f32)
    nx, inv_x = norm_parts(x)
    qpad = dot_nn(put, got["q"]).astype(bf16).reshape(members, z.cap, d)

    def stack(g):
        return g.reshape(experts, rank, g.shape[1])

    def stack_chunks(g):
        return stack(g.transpose(1, 0, 2).reshape(rk, SLOTS * z.sub))

    dresl = dres.astype(bf16)
    e2 = (scale_lora * dot_nt(dresl, mix_up) * masks[2]).astype(bf16)
    do = (dot_nt(dresl, wmix_f) + dot_nn(e2, mix_dn)).astype(bf16)
    r_down = reduce_share(grads(members, [(e3, m, 1.0), (e2, o, 1.0)]), 0)
    r_up = reduce_share(grads(members, [(low4, out_grad, scale_lora), (low2, dresl, scale_lora)]), 1)
    dopad = dot_nn(put, do).astype(bf16).reshape(members, z.cap, d)
    dqpad, dslots = attn_bwd(z.heads, got["slot"], got["info"], qpad, dopad, got["kd"])
    back = lax.all_to_all(dslots, "shard", split_axis=0, concat_axis=0, tiled=True)
    dkvp = jnp.sum(back.astype(f32), axis=0).astype(bf16).reshape(z.slots, z.w)
    dq = dot_tn(put, dqpad.reshape(z.slots, d)).astype(bf16)
    dkv = dot_tn(put, dkvp).astype(bf16)
    e0 = (scale_lora * dot_nt(dq, q_up) * masks[0]).astype(bf16)
    e1 = (scale_lora * dot_nt(dkv, kv_up) * masks[1]).astype(bf16)
    da = (dot_nt(dq, wq_f) + dot_nn(e0, q_dn)) + (dot_nt(dkv, wkv_f) + dot_nn(e1, kv_dn))
    tokens_grad = (dres + norm_back(nx, inv_x, attn_gain, da)).astype(bf16)
    r_qkv_down = reduce_share(grads(members, [(e0, a, 1.0), (e1, a, 1.0)]), 0)
    r_qkv_up = reduce_share(grads(members, [(low0, dq, scale_lora), (low1, dkv, scale_lora)]), 1)
    c = d // members
    return (layer_out, tokens_grad, stack(r_qkv_down[:, :c]), stack(r_qkv_up[:, :c]), stack(r_qkv_down[:, c:]),
            stack(r_qkv_up[:, c:]), stack(r_down[:, c:]), stack(r_up[:, c:]), stack(r_down[:, :c]),
            stack_chunks(r_exp_up), stack_chunks(r_red_dn), stack(r_up[:, :c]))


def solution(mesh):
    both = ("shard", "rep")
    row, vec = P("shard", None), P("shard")
    in_specs = (
        P(both, None), P(both, None), P(), P(both, None), P(both, None, None),
        vec, vec, row, vec, row, vec, row, vec, vec, vec, row, vec, row, vec,
    ) + (P(),) * 10
    out_specs = (P(both, None), P(both, None)) + (P(None, None, "shard"),) * 10
    return jax.shard_map(local, mesh=mesh, in_specs=in_specs, out_specs=out_specs, check_vma=False)
```

```python
import jax
import jax.numpy as jnp
from jax import lax
from jax.experimental import pallas as pl
from jax.experimental.pallas import tpu as pltpu
from jax.sharding import PartitionSpec as P

scale_lora = 0.5
eps = 1e-05
f32 = jnp.float32
bf16 = jnp.bfloat16
neg_big = -1e30
gelu_c = 0.7978845608028654
VMEM_LIMIT = 60 * 1024 * 1024


def dot_nn(a, b):
    return lax.dot_general(a, b, (((1,), (0,)), ((), ())), preferred_element_type=f32)


def dot_nt(a, b):
    return lax.dot_general(a, b, (((1,), (1,)), ((), ())), preferred_element_type=f32)


def dot_tn(a, b):
    return lax.dot_general(a, b, (((0,), (0,)), ((), ())), preferred_element_type=f32)


def key_onehot(slot_row, slots):
    ids = lax.broadcasted_iota(jnp.int32, (slots, slot_row.shape[1]), 0)
    return jnp.where(ids == slot_row, 1.0, 0.0).astype(bf16)


def to_rows(x, heads):
    hd = x.shape[1] // heads
    return jnp.concatenate([x[:, h * hd : (h + 1) * hd] for h in range(heads)], axis=0)


def to_cols(x, heads):
    c = x.shape[0] // heads
    return jnp.concatenate([x[h * c : (h + 1) * c] for h in range(heads)], axis=1)


def softmax_rows(qr, kd, span, heads):
    rows, keys = qr.shape[0], kd.shape[0]
    c = rows // heads
    u = lax.broadcasted_iota(jnp.int32, (c, keys), 1).astype(f32)
    allowed = (u >= span[:, 0:1]) & (u <= span[:, 1:2])
    s = dot_nt(qr, kd) * (kd.shape[1] ** (-0.5))
    s = jnp.where(allowed[None], s.reshape(heads, c, keys), neg_big)
    top = jnp.max(s, axis=2, keepdims=True)
    e = jnp.exp(s - top)
    p = e / jnp.sum(e, axis=2, keepdims=True)
    return p.reshape(rows, keys)


MESH = pl.DeviceIdType.MESH


class Gather:
    def __init__(self, members, own, full, slots, send_sem, recv_sem):
        self.members = members
        self.me, self.rep = lax.axis_index("shard"), lax.axis_index("rep")
        self.own, self.full = own, full
        self.base = [sum(slots[:i]) for i in range(len(slots))]
        self.send_sem, self.recv_sem = send_sem, recv_sem
        self.bits = [1 << i for i in range(1, members.bit_length() - 1)]
        self.planes = list(range(0, members, 2))
        self.sent = {}

    def place(self, kind, slot, offset):
        return self.full[kind].at[slot, self.me ^ offset]

    def copy(self, kind, slot, offset, there, to, to_slot):
        mine = self.sent.setdefault((kind, slot), {})
        at = mine.setdefault((offset, there, to_slot), len(mine))
        src = self.own[kind](slot) if offset == 0 else self.place(kind, slot, offset)
        pltpu.make_async_remote_copy(
            src, self.full[kind].at[to_slot, self.me ^ offset],
            self.send_sem.at[self.base[kind] + slot, at],
            self.recv_sem.at[self.base[kind] + to_slot, there],
            device_id=to, device_id_type=MESH).start()

    def wait(self, kind, slot, offset):
        piece = self.place(kind, slot, offset)
        pltpu.make_async_copy(piece, piece, self.recv_sem.at[self.base[kind] + slot, offset]).wait()

    def order(self, kind):
        return self.bits if kind % 2 == 0 else self.bits[::-1]

    def stage(self, kind, offset):
        return max(i for i, b in enumerate(self.order(kind)) if offset & b)

    def issue(self, slot, kinds, plane=True):
        for kind in kinds:
            if plane:
                for b in self.order(kind):
                    self.copy(kind, slot, 0, b, (self.me ^ b, self.rep), slot)
            self.copy(kind, slot, 0, 1, (self.me ^ 1, self.rep), slot)

    def arrive(self, slot, kinds, direct, swap_to=None):
        for kind in kinds:
            order = self.order(kind)
            some = [o for o in self.planes if o and (bin(o).count("1") == 1) == direct]
            some.sort(key=lambda o: self.stage(kind, o))
            for o in some:
                self.wait(kind, slot, o)
                for i in range(self.stage(kind, o) + 1, len(order)):
                    self.copy(kind, slot, o, o ^ order[i], (self.me ^ order[i], self.rep), slot)
                if swap_to is not None:
                    self.copy(kind, slot, o, o, (self.me, self.rep ^ 1), swap_to)
                self.copy(kind, slot, o, o ^ 1, (self.me ^ 1, self.rep), slot)

    def swapped(self, slot, kinds):
        for kind in kinds:
            for o in self.planes[1:]:
                self.wait(kind, slot, o)
                self.copy(kind, slot, o, o ^ 1, (self.me ^ 1, self.rep), slot)

    def ready(self, slot, kinds):
        for kind in kinds:
            for o in range(1, self.members, 2):
                self.wait(kind, slot, o)

    def finish(self):
        for (kind, slot), mine in self.sent.items():
            piece = self.place(kind, slot, 0)
            for at in mine.values():
                pltpu.make_async_copy(piece, piece, self.send_sem.at[self.base[kind] + slot, at]).wait()


U, V, C = (0, 1, 2), (3, 4, 5), (6, 7)
SLOTS = 8
WE, WR, AT, AB, KV = range(5)
BOTH, HALVES = (WE, WR), (AT, AB)
WQ, WMIX = 0, 1
SEND, NEAR, FAR, SWAP = range(4)
MLP_ORDER = (0, 3, 4, 1, 2, 6, 5, 7)
SERVE = {
    "p0": ((SEND, KV, 0),),
    "stage": ((SEND, WR, 0),),
    "norm_0": ((NEAR, KV, 0),),
    "idx_1": ((SEND, AT, 0),),
    "idx_5": ((NEAR, WR, 0),),
    "idx_6": ((FAR, KV, 0),),
    "wqneed": ((NEAR, AT, 0), (FAR, WR, 0), (SEND, AB, 0), (SWAP, WR, 3), (FAR, AT, 0), (SEND, WE, 0), (NEAR, AB, 0), (SEND, AB, 1), (NEAR, WE, 0), (FAR, AB, 0),),
    "q_1": ((SEND, WE, 1),),
    "att_0": ((NEAR, AB, 1),),
    "att_1": ((FAR, WE, 0),),
    "att_3": ((SEND, AT, 1),),
    "att_5": ((NEAR, WE, 1),),
    "att_6": ((SWAP, WE, 3),),
    "mixneed": ((FAR, AB, 1), (SEND, WR, 1), (NEAR, AT, 1), (FAR, WE, 1), (SEND, WE, 2), (NEAR, WR, 1), (SWAP, WE, 4), (FAR, AT, 1),),
    "mix_0": ((SEND, WR, 2),),
    "mix_1": ((FAR, WR, 1),),
    "norm2_0": ((NEAR, WE, 2), (SEND, WE, 6),),
    "mlp_0_0": ((NEAR, WR, 2),),
    "mlp_0_1": ((SWAP, WR, 4),),
    "mlp_1_0": ((FAR, WE, 2), (SEND, WR, 6),),
    "mlp_2_0": ((FAR, WR, 2), (NEAR, WE, 6), (SEND, WR, 7),),
    "mlp_3_0": ((NEAR, WR, 6),),
    "mlp_4_0": ((FAR, WE, 6), (SEND, WE, 7),),
    "mlp_4_1": ((FAR, WR, 6),),
    "mlp_5_0": ((NEAR, WR, 7), (SWAP, WE, 5),),
    "mlp_5_1": ((NEAR, WE, 7), (SWAP, WR, 5),),
    "mlp_6_0": ((FAR, WR, 7), (FAR, WE, 7),),
}


def chunk_of(slot, parity):
    slot = jnp.int32(slot)
    low = jnp.where(slot < 3, slot, slot + 2)
    high = jnp.where(slot < 3, slot + 5, slot - 3)
    return jnp.where(slot >= 6, slot - 3, jnp.where(parity == 0, low, high))


def norm_parts(v):
    center = v - jnp.mean(v, axis=-1, keepdims=True)
    inv = lax.rsqrt(jnp.mean(center * center, axis=-1, keepdims=True) + eps)
    return center * inv, inv


def norm_back(n, inv, gain, dn):
    w = gain * dn
    return (w - jnp.mean(w, axis=-1, keepdims=True)
            - n * jnp.mean(w * n, axis=-1, keepdims=True)) * inv


class Sizes:
    def __init__(self, members, replicas, length, d, ff, hd, rk, rank, seqs, projs):
        self.members, self.replicas, self.length, self.d, self.ff = members, replicas, length, d, ff
        self.hd, self.rk, self.rank, self.seqs, self.projs = hd, rk, rank, seqs, projs
        self.heads = d // hd
        self.cap = 3 * length // (2 * members)
        self.slots = members * self.cap
        self.w = 2 * hd
        self.rows = d // members
        self.sub = ff // members // SLOTS
        self.fc = self.sub * members
        self.aligned = self.sub % 128 == 0
        self.small_cols = -(-max(self.rows + self.sub, seqs * (projs + 1)) // 128) * 128


FWD_IN = ("x", "dy", "small", "group", "group_t", "q_dn", "q_up", "kv_dn", "kv_up", "mix_dn", "mix_up",
          "exp_dn", "exp_up", "red_dn", "red_up", "wq", "wkv", "wmix", "wexp", "wred")
FWD_OUT = ("dres", "put", "slot", "info", "chosen", "low0", "low1", "low2", "low4", "e3", "gain",
           "a", "q", "o", "m", "resid", "kd", "gup", "gdn", "layer", "kvs", "ge", "gr", "ga", "gb", "gk")
FWD_SCRATCH = ("y", "we_v", "wr_v", "a_v", "q_v", "kvp", "kvb", "kd_st", "gup_st", "gdn_st", "sm",
               "lowr", "er", "low3", "e4",
               "send_sem", "recv_sem", "sm_send", "sm_recv", "kv_send", "kv_recv", "stage_sem", "store_sem",
               "load_sem", "kvb_sem", "kd_sem", "g_sem", "out_sem")


def fwd_kernel(z, *refs):
    r = dict(zip(FWD_IN + FWD_OUT + FWD_SCRATCH, refs))
    members, rows, fc, sub, d, hd = z.members, z.rows, z.fc, z.sub, z.d, z.hd
    length, cap, w, heads, rk = z.length, z.cap, z.w, z.heads, z.rk
    me, rep = lax.axis_index("shard"), lax.axis_index("rep")
    parity = lax.rem(rep, 2)
    half = rows // 2
    att = (r["wq"], r["wmix"])
    g = Gather(
        members,
        [lambda s: r["ge"].at[s, me],
         lambda s: r["wred"].at[chunk_of(s, parity)],
         lambda s: att[s].at[0:half],
         lambda s: att[s].at[half:rows],
         lambda s: r["wkv"]],
        [r["ge"], r["gr"], r["ga"], r["gb"], r["gk"]],
        [SLOTS, SLOTS, 2, 2, 1], r["send_sem"], r["recv_sem"])
    we_v, wr_v, sm, y, dm = r["we_v"], r["wr_v"], r["sm"], r["y"], r["dres"]

    def serve(point):
        for op, kind, slot in SERVE.get(point, ()):
            swap_to = slot + 3 if slot in U and kind in BOTH else None
            if op == SEND:
                g.issue(slot, (kind,))
            elif op == SWAP:
                g.swapped(slot, (kind,))
            else:
                g.arrive(slot, (kind,), op == NEAR, swap_to)

    barrier = pltpu.get_barrier_semaphore()
    others = [(me ^ o, rep) for o in range(1, members)] + [(me, rep ^ 1)]
    for to in others:
        pl.semaphore_signal(barrier, inc=1, device_id=to, device_id_type=MESH)

    def stage_copies(slot):
        j = chunk_of(slot, parity)
        to = we_v.at[0, slot]
        if not z.aligned:
            return [pltpu.make_async_copy(r["wexp"].at[j], to, r["stage_sem"].at[slot])]
        return [pltpu.make_async_copy(
            r["wexp"].at[:, pl.ds(pl.multiple_of(s * (z.ff // members) + j * sub, sub), sub)],
            to.at[:, s * sub : (s + 1) * sub], r["stage_sem"].at[slot]) for s in range(members)]

    def stored(slot):
        return pltpu.make_async_copy(we_v.at[0, slot], r["ge"].at[slot, me], r["store_sem"].at[slot])

    def staged(slot):
        pltpu.make_async_copy(we_v.at[0, slot], we_v.at[0, slot], r["stage_sem"].at[slot]).wait()
        stored(slot).start()

    for slot in range(SLOTS):
        for cp in stage_copies(slot):
            cp.start()
    pl.semaphore_wait(barrier, len(others))

    def small_copy(o):
        return pltpu.make_async_remote_copy(
            r["small"], sm.at[me], r["sm_send"].at[o], r["sm_recv"].at[o],
            device_id=(me ^ o, rep), device_id_type=MESH)

    for o in range(1, members):
        small_copy(o).start()
    serve("p0")
    sm[me] = r["small"][...]
    for slot in range(SLOTS):
        staged(slot)
    for slot in range(SLOTS):
        stored(slot).wait()
    serve("stage")
    for o in range(1, members):
        pltpu.make_async_copy(sm.at[me ^ o], sm.at[me ^ o], r["sm_recv"].at[o]).wait()

    def vec(row):
        return jnp.concatenate([sm[s, row : row + 1, 0:rows] for s in range(members)], axis=1)

    def norm_rows(src, gain, bias, dst, part):
        gv, bv = vec(gain), vec(bias)

        def body(i, _):
            at = pl.ds(pl.multiple_of(i * 128, 128), 128)
            n, _inv = norm_parts(src[at, :].astype(f32))
            dst[at, :] = (n * gv + bv).astype(bf16)
            return 0

        lax.fori_loop(part * length // 256, (part + 1) * length // 256, body, 0)

    for part in range(2):
        serve("norm_%d" % part)
        norm_rows(r["x"], 0, 1, r["a_v"], part)

    r["gain"][...] = vec(0)

    t_row = lax.broadcasted_iota(jnp.int32, (1, length), 1)
    before_t = lax.broadcasted_iota(jnp.int32, (length, length), 0) < lax.broadcasted_iota(
        jnp.int32, (length, length), 1)
    c_ids = lax.broadcasted_iota(jnp.int32, (cap, length), 0)
    lane = lax.broadcasted_iota(jnp.int32, (cap, 128), 1)
    span = length * z.replicas
    first = (me * z.replicas + rep) * length
    tf = t_row.astype(f32)
    chosen = jnp.zeros((length, 128), f32)
    for k in range(members):
        serve("idx_%d" % k)
        row = r["group"][k]
        src = lax.div(row, span)
        src_col = lax.div(r["group_t"][:, k : k + 1], span)
        earlier = jnp.where((src_col == src) & before_t, 1.0, 0.0)
        slot_row = src * cap + jnp.sum(earlier, axis=0, keepdims=True).astype(jnp.int32)
        r["slot"][k] = slot_row
        hit = slot_row == c_ids + me * cap

        def pick(values):
            return jnp.sum(jnp.where(hit, values, 0.0), axis=1, keepdims=True)

        full = pick(jnp.ones_like(tf))
        tok = pick((row - first + 1).astype(f32)) - 1.0
        put = jnp.where(tok == tf, 1.0, 0.0).astype(bf16)
        r["put"][k] = put
        end = jnp.zeros((1, 1), f32)
        start = jnp.zeros_like(tf)
        ids = [jnp.zeros_like(tf) for _ in range(z.projs)]
        for j in range(z.seqs):
            n = sm[k, 8:9, j : j + 1]
            inside = (tf >= end) & (tf < end + n)
            end = end + n
            start = start + jnp.where(tf >= end, n, 0.0)
            for p in range(z.projs):
                at = z.seqs + j * z.projs + p
                ids[p] = ids[p] + jnp.where(inside, sm[k, 8:9, at : at + 1], 0.0)
        info = jnp.where(lane == 0, pick(start) + (1.0 - full), 0.0)
        info = jnp.where(lane == 1, pick(tf), info)
        for p in range(z.projs):
            info = jnp.where(lane == 2 + p, pick(ids[p]), info)
        r["info"][k] = info
        chosen = chosen + dot_tn(put, info.astype(bf16))
    r["chosen"][...] = chosen
    rank_of = lax.broadcasted_iota(jnp.int32, (length, rk), 1) // z.rank

    def mask(p):
        return jnp.where(rank_of.astype(f32) == r["chosen"][:, 2 + p : 3 + p], 1.0, 0.0)

    a_v, q_v = r["a_v"], r["q_v"]
    o_v = q_v
    serve("low")
    r["low0"][...] = (dot_nt(a_v[...], r["q_dn"][...]) * mask(0)).astype(bf16)
    r["low1"][...] = (dot_nt(a_v[...], r["kv_dn"][...]) * mask(1)).astype(bf16)
    out_a = pltpu.make_async_copy(a_v, r["a"], r["out_sem"].at[0])
    out_a.start()

    serve("kvneed")
    g.ready(0, (KV,))
    kv_loads = [pltpu.make_async_copy(
        r["wkv"] if o == 0 else g.place(KV, 0, o), we_v.at[1, me ^ o, :, 0:w], r["kv_send"].at[o]) for o in range(members)]
    for cp in kv_loads:
        cp.start()
    for cp in kv_loads:
        cp.wait()
    back_kv = pltpu.make_async_copy(we_v.at[1, me, :, 0:w], g.place(KV, 0, 0), r["kv_send"].at[0])
    back_kv.start()
    vb = jnp.concatenate([sm[s, 7:8, 0 : hd // members] for s in range(members)], axis=1)
    kv_bias = jnp.concatenate([jnp.zeros((1, hd), f32), vb], axis=1)
    kv = (dot_nn(a_v[...], we_v[1, :, :, 0:w].reshape(d, w)) + kv_bias
          + scale_lora * dot_nn(r["low1"][...], r["kv_up"][...])).astype(bf16)
    for k in range(members):
        r["kvp"][k] = dot_nn(r["put"][k], kv).astype(bf16)

    def kv_copy(o):
        return pltpu.make_async_remote_copy(
            r["kvp"], r["kvs"].at[me], r["kv_send"].at[o], r["kv_recv"].at[o],
            device_id=(me ^ o, rep), device_id_type=MESH)

    back_kv.wait()
    own_kv = pltpu.make_async_copy(r["kvp"], r["kvs"].at[me], r["kv_send"].at[0])
    for o in range(1, members):
        kv_copy(o).start()
    own_kv.start()

    for slot in V:
        g.issue(slot, BOTH, False)
    serve("afterkvx")

    def wide_load(which):
        g.ready(which, HALVES)
        out = []
        for kind in HALVES:
            for o in range(members):
                src = g.own[kind](which) if o == 0 else g.place(kind, which, o)
                for c in range(d // fc):
                    out.append(pltpu.make_async_copy(
                        src.at[:, c * fc : (c + 1) * fc],
                        we_v.at[c, me ^ o, (kind - AT) * half : (kind - AT + 1) * half],
                        r["load_sem"].at[kind - AT, c, o]))
        for cp in out:
            cp.start()
        for cp in out:
            cp.wait()
        back = [pltpu.make_async_copy(
            we_v.at[c, me, (kind - AT) * half : (kind - AT + 1) * half],
            g.place(kind, which, 0).at[:, c * fc : (c + 1) * fc],
            r["load_sem"].at[kind - AT, c, 0]) for kind in HALVES for c in range(d // fc)]
        for cp in back:
            cp.start()
        return back

    serve("wqneed")
    back_q = wide_load(WQ)
    q_bias = vec(2)
    for c in range(d // fc):
        serve("q_%d" % c)
        at = slice(c * fc, (c + 1) * fc)
        q_v[:, at] = (dot_nn(a_v[...], we_v[c].reshape(d, fc)) + q_bias[:, at]
                      + scale_lora * dot_nn(r["low0"][...], r["q_up"][:, at])).astype(bf16)
    out_q = pltpu.make_async_copy(q_v, r["q"], r["out_sem"].at[1])
    out_q.start()

    for cp in back_q:
        cp.wait()

    serve("kvxwait")

    for o in range(1, members):
        pltpu.make_async_copy(r["kvs"].at[me ^ o], r["kvs"].at[me ^ o], r["kv_recv"].at[o]).wait()
    own_kv.wait()
    dm[...] = jnp.zeros_like(dm)

    def kvb_load(k, buf):
        return pltpu.make_async_copy(r["kvs"].at[:, k], r["kvb"].at[buf], r["kvb_sem"].at[buf])

    def kd_out(k, buf):
        return pltpu.make_async_copy(r["kd_st"].at[buf], r["kd"].at[k], r["kd_sem"].at[buf])

    kvb_load(0, 0).start()
    groups = 2

    def attend(k, _):
        buf = lax.rem(k, 2)

        @pl.when(k + 1 < members)
        def _():
            kvb_load(k + 1, 1 - buf).start()

        for i in range(members):
            if "att_%d" % i in SERVE:
                pl.when(k == i)(lambda i=i: serve("att_%d" % i))
        kvb_load(k, buf).wait()
        oh = key_onehot(r["slot"][k], z.slots)
        kvd = dot_tn(oh, r["kvb"][buf].reshape(z.slots, w)).astype(bf16)

        @pl.when(k >= 2)
        def _():
            kd_out(k, buf).wait()

        r["kd_st"][buf] = kvd
        kd_out(k, buf).start()
        put = r["put"][k]
        qp = dot_nn(put, q_v[...]).astype(bf16)
        info = r["info"][k]
        outs = []
        per = heads // groups
        for h in range(groups):
            qr = to_rows(qp[:, h * per * hd : (h + 1) * per * hd], per)
            p = softmax_rows(qr, kvd[:, :hd], info, per).astype(bf16)
            outs.append(to_cols(dot_nn(p, kvd[:, hd:]).astype(bf16), per))
        dm[...] += dot_tn(put, jnp.concatenate(outs, axis=1))
        return 0

    lax.fori_loop(0, members, attend, 0)
    out_q.wait()
    o_v[...] = dm[...].astype(bf16)
    out_o = pltpu.make_async_copy(o_v, r["o"], r["out_sem"].at[2])
    out_o.start()
    r["low2"][...] = (dot_nt(o_v[...], r["mix_dn"][...]) * mask(2)).astype(bf16)
    serve("mixneed")
    back_m = wide_load(WMIX)
    mix_bias = vec(3)
    for c in range(d // fc):
        serve("mix_%d" % c)
        at = slice(c * fc, (c + 1) * fc)
        y[:, at] = (r["x"][:, at].astype(f32) + dot_nn(o_v[...], we_v[c].reshape(d, fc)) + mix_bias[:, at]
                    + scale_lora * dot_nn(r["low2"][...], r["mix_up"][:, at]))

    def load(slot, buf):
        out = [pltpu.make_async_copy(r["ge"].at[slot], we_v.at[buf], r["load_sem"].at[0, buf, 0])]
        for o in range(members):
            src = g.own[WR](slot) if o == 0 else g.place(WR, slot, o)
            out.append(pltpu.make_async_copy(src, wr_v.at[buf, me ^ o], r["load_sem"].at[1, buf, o]))
        return out

    def fetch(slot, buf):
        g.ready(slot, BOTH)
        for cp in load(slot, buf):
            cp.start()

    for cp in back_m:
        cp.wait()
    out_r = pltpu.make_async_copy(y, r["resid"], r["out_sem"].at[3])
    out_r.start()
    out_a.wait()
    m_v = a_v
    for part in range(2):
        serve("norm2_%d" % part)
        norm_rows(y, 4, 5, m_v, part)
    serve("low3")
    out_m = pltpu.make_async_copy(m_v, r["m"], r["out_sem"].at[0])
    out_m.start()
    r["low3"][...] = (dot_nt(m_v[...], r["exp_dn"][...]) * mask(3)).astype(bf16)
    r["e4"][...] = (scale_lora * dot_nt(r["dy"][...], r["red_up"][...]) * mask(4)).astype(bf16)
    dm[...] = jnp.zeros_like(dm)
    r["lowr"][...] = jnp.zeros_like(r["lowr"])
    r["er"][...] = jnp.zeros_like(r["er"])
    out_r.wait()
    y[...] += vec(6)

    def g_out(j, buf):
        return (pltpu.make_async_copy(r["gup_st"].at[buf], r["gup"].at[:, j], r["g_sem"].at[0, buf]),
                pltpu.make_async_copy(r["gdn_st"].at[buf], r["gdn"].at[:, j], r["g_sem"].at[1, buf]))

    serve("mlp_f0")
    fetch(MLP_ORDER[0], 0)

    def step(n, _):
        for i in range(SLOTS):
            if "mlp_%d_0" % i in SERVE:
                pl.when(n == i)(lambda i=i: serve("mlp_%d_0" % i))
        buf = lax.rem(n, 2)
        slot = jnp.int32(0)
        for i, q in enumerate(MLP_ORDER):
            slot = jnp.where(n == i, q, slot)
        for cp in load(slot, buf):
            cp.wait()
        j = chunk_of(slot, parity)
        we = we_v[buf].reshape(d, fc)
        wr = wr_v[buf].reshape(fc, d)
        if z.aligned:
            def cut(ref):
                return jnp.concatenate([ref[:, pl.ds(pl.multiple_of(s * (z.ff // members) + j * sub, sub), sub)]
                                        for s in range(members)], axis=1)
            bup, adn = cut(r["exp_up"]), cut(r["red_dn"])
        else:
            bup, adn = r["exp_up"][j], r["red_dn"][j]
        be = jnp.concatenate([sm[s, 0:SLOTS, rows : rows + sub] for s in range(members)], axis=1)
        be = jnp.sum(jnp.where(lax.broadcasted_iota(jnp.int32, (SLOTS, fc), 0) == j, be, 0.0), axis=0, keepdims=True)
        hid = dot_nn(m_v[...], we) + be
        hid = hid + scale_lora * dot_nn(r["low3"][...], bup)
        cube = hid * hid * hid
        t = jnp.tanh(gelu_c * (hid + 0.044715 * cube))
        act = (0.5 * hid * (1.0 + t)).astype(bf16)
        slope = 0.5 * (1.0 + t) + 0.5 * hid * (1.0 - t * t) * (
            gelu_c * (1.0 + 3.0 * 0.044715 * hid * hid)
        )
        dact = dot_nt(r["dy"][...], wr) + dot_nn(r["e4"][...], adn)
        dh = (dact * slope).astype(bf16)
        for i in range(SLOTS):
            def middle(i=i):
                serve("mlp_%d_1" % i)
                if i + 1 < SLOTS:
                    fetch(MLP_ORDER[i + 1], (i + 1) % 2)
            pl.when(n == i)(middle)
        y[...] += dot_nn(act, wr)
        dm[...] += dot_nt(dh, we)
        r["lowr"][...] += dot_nt(act, adn)
        r["er"][...] += dot_nt(dh, bup)
        gup = (scale_lora * dot_tn(r["low3"][...], dh)).astype(bf16)
        gdn = dot_tn(r["e4"][...], act).astype(bf16)

        @pl.when(n >= 2)
        def _():
            for cp in g_out(j, buf):
                cp.wait()

        for to in range(members):
            r["gup_st"][buf, to] = gup[:, to * sub : (to + 1) * sub]
            r["gdn_st"][buf, to] = gdn[:, to * sub : (to + 1) * sub]
        for cp in g_out(j, buf):
            cp.start()
        return 0

    lax.fori_loop(0, SLOTS, step, 0)

    low4 = (r["lowr"][...] * mask(4)).astype(bf16)
    r["low4"][...] = low4
    out_o.wait()
    layer_v = q_v
    for c in range(d // fc):
        at = slice(c * fc, (c + 1) * fc)
        layer_v[:, at] = (y[:, at] + scale_lora * dot_nn(low4, r["red_up"][:, at])).astype(bf16)
    out_l = pltpu.make_async_copy(layer_v, r["layer"], r["out_sem"].at[1])
    out_l.start()
    back_r = pltpu.make_async_copy(r["resid"], y, r["out_sem"].at[3])
    back_r.start()
    e3 = (scale_lora * r["er"][...] * mask(3)).astype(bf16)
    r["e3"][...] = e3
    gain = vec(4)
    back_r.wait()

    def last(i, _):
        at = pl.ds(pl.multiple_of(i * 128, 128), 128)
        n, inv = norm_parts(y[at, :])
        dn = dm[at, :] + dot_nn(r["e3"][at, :], r["exp_dn"][...])
        dm[at, :] = r["dy"][at, :].astype(f32) + norm_back(n, inv, gain, dn)
        return 0

    lax.fori_loop(0, length // 128, last, 0)
    out_l.wait()
    out_m.wait()
    for buf in range(2):
        kd_out(buf, buf).wait()
        for cp in g_out(buf, buf):
            cp.wait()
    for o in range(1, members):
        small_copy(o).wait_send()
        kv_copy(o).wait_send()
    g.finish()


def forward(z, args):
    vm = pl.BlockSpec(memory_space=pltpu.VMEM)
    hbm = pl.BlockSpec(memory_space=pl.ANY)
    m, n, d, rk, w = z.members, z.length, z.d, z.rk, z.w
    s = jax.ShapeDtypeStruct
    half = z.rows // 2
    outs = dict(
        dres=s((n, d), f32), put=s((m, z.cap, n), bf16), slot=s((m, 1, n), jnp.int32),
        info=s((m, z.cap, 128), f32), chosen=s((n, 128), f32),
        low0=s((n, rk), bf16), low1=s((n, rk), bf16), low2=s((n, rk), bf16), low4=s((n, rk), bf16), e3=s((n, rk), bf16), gain=s((1, d), f32),
        a=s((n, d), bf16), q=s((n, d), bf16), o=s((n, d), bf16), m=s((n, d), bf16), resid=s((n, d), f32),
        kd=s((m, n, w), bf16), gup=s((m, SLOTS, rk, z.sub), bf16), gdn=s((m, SLOTS, rk, z.sub), bf16),
        layer=s((n, d), bf16), kvs=s((m, m, z.cap, w), bf16),
        ge=s((SLOTS, m, z.rows, z.fc), bf16), gr=s((SLOTS, m, z.sub, d), bf16),
        ga=s((2, m, half, d), bf16), gb=s((2, m, half, d), bf16), gk=s((1, m, z.rows, w), bf16))
    in_vmem = FWD_OUT[:11]
    sends = m - 1 + m // 2
    dma = pltpu.SemaphoreType.DMA
    items = 2 * SLOTS + 5
    scratch = dict(
        y=pltpu.VMEM((n, d), f32), we_v=pltpu.VMEM((2, m, z.rows, z.fc), bf16), wr_v=pltpu.VMEM((2, m, z.sub, d), bf16),
        a_v=pltpu.VMEM((n, d), bf16), q_v=pltpu.VMEM((n, d), bf16),
        kvp=pltpu.VMEM((m, z.cap, w), bf16), kvb=pltpu.VMEM((2, m, z.cap, w), bf16),
        kd_st=pltpu.VMEM((2, n, w), bf16), gup_st=pltpu.VMEM((2, m, rk, z.sub), bf16),
        gdn_st=pltpu.VMEM((2, m, rk, z.sub), bf16), sm=pltpu.VMEM((m, 16, z.small_cols), f32),
        lowr=pltpu.VMEM((n, rk), f32), er=pltpu.VMEM((n, rk), f32), low3=pltpu.VMEM((n, rk), bf16), e4=pltpu.VMEM((n, rk), bf16),
        send_sem=dma((items, sends)), recv_sem=dma((items, m)), sm_send=dma((m,)), sm_recv=dma((m,)),
        kv_send=dma((m,)), kv_recv=dma((m,)), stage_sem=dma((SLOTS,)), store_sem=dma((SLOTS,)),
        load_sem=dma((2, 2, m)), kvb_sem=dma((2,)), kd_sem=dma((2,)), g_sem=dma((2, 2)), out_sem=dma((4,)))
    got = pl.pallas_call(
        lambda *refs: fwd_kernel(z, *refs),
        in_specs=[hbm if k.startswith("w") else vm for k in FWD_IN],
        out_specs=[vm if k in in_vmem else hbm for k in FWD_OUT],
        out_shape=[outs[k] for k in FWD_OUT],
        scratch_shapes=[scratch[k] for k in FWD_SCRATCH],
        compiler_params=pltpu.CompilerParams(
            vmem_limit_bytes=FWD_VMEM, collective_id=1, has_side_effects=True),
    )(*[args[k] for k in FWD_IN])
    return dict(zip(FWD_OUT, got))


FWD_VMEM = 62 * 1024 * 1024


class Job:
    def __init__(self, members, replicas, work, got, out, send_sem, recv_sem, turn):
        self.me, self.rep = lax.axis_index("shard"), lax.axis_index("rep")
        self.work, self.got, self.out = work, got, out
        self.send_sem, self.recv_sem = send_sem, recv_sem
        bits = [1 << i for i in range(members.bit_length() - 1)]
        bits = bits if turn == 0 else bits[:1] + bits[1:][::-1]
        self.stages = []
        at, decided = 0, 0
        for b in bits:
            free = [f for f in range(members) if not f & (decided | b)]
            self.stages.append((b, True, at, free, decided))
            at += len(free)
            decided |= b
        b = 1
        while b < replicas:
            self.stages.append((b, False, at, [0], decided))
            at += 1
            b *= 2

    def copy(self, i, n):
        b, shard, at, free, decided = self.stages[i]
        if shard:
            src = self.work.at[free[n] | (self.me & decided) | ((self.me ^ b) & b)]
            to = (self.me ^ b, self.rep)
        else:
            src, to = self.work.at[self.me], (self.me, self.rep ^ b)
        return pltpu.make_async_remote_copy(
            src, self.got.at[at + n], self.send_sem.at[at + n], self.recv_sem.at[at + n],
            device_id=to, device_id_type=MESH)

    def start(self, i):
        for n in range(len(self.stages[i][3])):
            self.copy(i, n).start()

    def add(self, i):
        b, shard, at, free, decided = self.stages[i]
        for n, f in enumerate(free):
            cp = self.copy(i, n)
            cp.wait_recv()
            cp.wait_send()
            keep = f | (self.me & decided) | (self.me & b) if shard else self.me
            total = self.work[keep].astype(f32) + self.got[at + n].astype(f32)
            if i + 1 < len(self.stages):
                self.work[keep] = total.astype(bf16)
            else:
                blocks, _, lanes = total.shape
                for j in range(blocks):
                    self.out[:, j * lanes : (j + 1) * lanes] = total[j]

    def move(self, i):
        self.add(i)
        if i + 1 < len(self.stages):
            self.start(i + 1)


BWD_IN = ("dres", "put", "slot", "info", "chosen", "low0", "low1", "low2", "low4", "e3", "gain",
          "mix_dn", "mix_up", "q_dn", "q_up", "kv_dn", "kv_up",
          "ga", "gb", "gk", "q", "a", "o", "m", "dy", "x", "kd", "gup", "gdn")
JOBS = ("ja", "jb", "jc", "jd", "je", "jf")
BWD_OUT = ("dx",) + tuple(j + "_out" for j in JOBS)
BWD_SCRATCH = ("w_v", "wk_v", "t1", "t2", "q_v", "do_v", "dq", "kd_st", "ds_st", "dk_r") + tuple(
    j + s for j in JOBS for s in ("_w", "_g", "_s", "_r")) + (
    "w_sem", "t_sem", "g_sem", "kd_sem", "dk_send", "dk_recv", "out_sem")


def job_shapes(z):
    wide = z.rows // min(128, z.rows)
    lanes = min(128, z.rows)
    chunks = (SLOTS, z.sub) if z.aligned else (SLOTS * z.sub // 128, 128)
    return dict(ja=chunks, jb=chunks, jc=(2 * wide, lanes), jd=(2 * wide, lanes),
                je=(2 * wide, lanes), jf=(wide + 1, lanes))


def bwd_kernel(z, *refs):
    r = dict(zip(BWD_IN + BWD_OUT + BWD_SCRATCH, refs))
    members, replicas, rows, fc, d, hd = z.members, z.replicas, z.rows, z.fc, z.d, z.hd
    length, cap, w, heads, rk = z.length, z.cap, z.w, z.heads, z.rk
    me, rep = lax.axis_index("shard"), lax.axis_index("rep")
    half = rows // 2
    halves = d // fc
    w_v, t1, t2, q_v, do_v, dq, dres = (r[k] for k in ("w_v", "t1", "t2", "q_v", "do_v", "dq", "dres"))
    ja, jb, jc, jd, je, jf = (
        Job(members, replicas, r[j + "_w"], r[j + "_g"], r[j + "_out"], r[j + "_s"], r[j + "_r"], i % 2)
        for i, j in enumerate(JOBS))
    last = len(ja.stages) - 1

    barrier = pltpu.get_barrier_semaphore()
    others = [(me ^ o, rep) for o in range(1, members)]
    b = 1
    while b < replicas:
        others.append((me, rep ^ b))
        b *= 2
    for to in others:
        pl.semaphore_signal(barrier, inc=1, device_id=to, device_id_type=MESH)

    def local(src, dst, sem):
        return pltpu.make_async_copy(src, dst, sem)

    def wide(which):
        return [local(r[k].at[which, :, :, c * fc : (c + 1) * fc],
                      w_v.at[c, :, h * half : (h + 1) * half], r["w_sem"].at[h, c])
                for h, k in enumerate(("ga", "gb")) for c in range(halves)]

    load_up = local(r["gup"], r["ja_w"], r["g_sem"].at[0])
    load_dn = local(r["gdn"], r["jb_w"], r["g_sem"].at[1])
    load_up.start()
    load_dn.start()
    mix = wide(WMIX)
    for cp in mix:
        cp.start()
    load_m = local(r["m"], t1, r["t_sem"].at[0])
    load_dy = local(r["dy"], t2, r["t_sem"].at[1])
    load_q = local(r["q"], q_v, r["t_sem"].at[2])
    load_k = local(r["gk"].at[0], r["wk_v"], r["t_sem"].at[3])
    for cp in (load_m, load_dy, load_q, load_k):
        cp.start()
    pl.semaphore_wait(barrier, len(others))
    load_up.wait()
    ja.start(0)
    load_dn.wait()
    jb.start(0)

    rank_of = (lax.broadcasted_iota(jnp.int32, (length, rk), 1) // z.rank).astype(f32)

    def mask(p):
        return jnp.where(rank_of == r["chosen"][:, 2 + p : 3 + p], 1.0, 0.0)

    def terms(job, block, left, right, sc):
        lanes = job.work.shape[3]
        g = dot_tn(left, right) * sc
        width = right.shape[1] // members
        for to in range(members):
            for i in range(-(-width // lanes)):
                part = g[:, to * width + i * lanes : to * width + min((i + 1) * lanes, width)]
                if part.shape[1] < lanes:
                    part = jnp.concatenate([part, jnp.zeros((rk, lanes - part.shape[1]), f32)], axis=1)
                job.work[to, block + i] = part.astype(bf16)

    per = r["jc_w"].shape[1] // 2

    dresl = do_v
    dresl[...] = dres[...].astype(bf16)
    e2 = (scale_lora * dot_nt(dresl[...], r["mix_up"][...]) * mask(2)).astype(bf16)
    terms(jd, per, r["low2"][...], dresl[...], scale_lora)
    load_m.wait()
    terms(jc, 0, r["e3"][...], t1[...], 1.0)
    load_o = local(r["o"], t1, r["t_sem"].at[0])
    load_o.start()
    load_dy.wait()
    terms(jd, 0, r["low4"][...], t2[...], scale_lora)
    load_x = local(r["x"], t2, r["t_sem"].at[1])
    load_x.start()
    jd.start(0)
    for cp in mix:
        cp.wait()
    ja.move(0)
    dq[...] = dot_nt(dresl[:, 0:fc], w_v[0].reshape(d, fc)) + dot_nn(e2, r["mix_dn"][...])
    jb.move(0)
    for c in range(1, halves):
        dq[...] += dot_nt(dresl[:, c * fc : (c + 1) * fc], w_v[c].reshape(d, fc))
    do_v[...] = dq[...].astype(bf16)
    query = wide(WQ)
    for cp in query:
        cp.start()
    load_o.wait()
    terms(jc, per, e2, t1[...], 1.0)
    jc.start(0)
    load_a = local(r["a"], t1, r["t_sem"].at[0])
    load_a.start()
    jd.move(0)
    dq[...] = jnp.zeros_like(dq)
    load_q.wait()

    def kd_load(k, buf):
        return local(r["kd"].at[k], r["kd_st"].at[buf], r["kd_sem"].at[buf])

    def ds_copy(k, buf, o):
        return pltpu.make_async_remote_copy(
            r["ds_st"].at[buf, me ^ o], r["dk_r"].at[me, k], r["dk_send"].at[buf, o], r["dk_recv"].at[o],
            device_id=(me ^ o, rep), device_id_type=MESH)

    kd_load(0, 0).start()
    groups = 4
    sc = hd ** (-0.5)
    acts = {0: lambda: jc.move(0), 1: lambda: ja.move(1), 2: lambda: (jb.move(1), jd.move(1))[0], 3: lambda: (ja.move(2), jc.move(1))[0],
            4: lambda: (jb.move(2), jd.move(2))[0], 5: lambda: (ja.move(3), jc.move(2))[0],
            6: lambda: (jb.move(3), jd.move(3))[0], 7: lambda: jc.move(3)}

    def attend(k, _):
        buf = lax.rem(k, 2)

        @pl.when(k + 1 < members)
        def _():
            kd_load(k + 1, 1 - buf).start()

        for i, act in acts.items():
            pl.when(k == i)(act)
        kd_load(k, buf).wait()
        kvd = r["kd_st"][buf]
        kd, vd = kvd[:, :hd], kvd[:, hd:]
        put = r["put"][k]
        qp = dot_nn(put, q_v[...]).astype(bf16)
        dop = dot_nn(put, do_v[...]).astype(bf16)
        info = r["info"][k]
        n = heads // groups
        dqs = []
        dk = jnp.zeros((length, hd), f32)
        dv = jnp.zeros((length, hd), f32)
        for h in range(groups):
            at = slice(h * n * hd, (h + 1) * n * hd)
            qr, dor = to_rows(qp[:, at], n), to_rows(dop[:, at], n)
            p = softmax_rows(qr, kd, info, n)
            dp = dot_nt(dor, vd)
            ds = (p * (dp - jnp.sum(dp * p, axis=1, keepdims=True))).astype(bf16)
            dqs.append(to_cols((dot_nn(ds, kd) * sc).astype(bf16), n))
            dk = dk + dot_tn(ds, qr)
            dv = dv + dot_tn(p.astype(bf16), dor)
        dq[...] += dot_tn(put, jnp.concatenate(dqs, axis=1))
        dkv = jnp.concatenate([dk * sc, dv], axis=1).astype(bf16)
        slots = dot_nn(key_onehot(r["slot"][k], z.slots), dkv).astype(bf16).reshape(members, cap, w)

        @pl.when(k >= 2)
        def _():
            for o in range(1, members):
                ds_copy(k, buf, o).wait_send()

        r["ds_st"][buf] = slots
        r["dk_r"][me, k] = r["ds_st"][buf, me]
        for o in range(1, members):
            ds_copy(k, buf, o).start()
        return 0

    lax.fori_loop(0, members, attend, 0)

    q_v[...] = dq[...].astype(bf16)
    e0 = (scale_lora * dot_nt(q_v[...], r["q_up"][...]) * mask(0)).astype(bf16)
    load_a.wait()
    terms(je, 0, e0, t1[...], 1.0)
    terms(jf, 0, r["low0"][...], q_v[...], scale_lora)
    for o in range(1, members):
        local(r["dk_r"].at[me ^ o], r["dk_r"].at[me ^ o], r["dk_recv"].at[o]).wait()
    dkv = jnp.zeros((length, w), f32)
    for k in range(members):
        total = r["dk_r"][0, k].astype(f32)
        for s in range(1, members):
            total = total + r["dk_r"][s, k].astype(f32)
        dkv = dkv + dot_tn(r["put"][k], total.astype(bf16))
    dkv = dkv.astype(bf16)
    e1 = (scale_lora * dot_nt(dkv, r["kv_up"][...]) * mask(1)).astype(bf16)
    terms(je, per, e1, t1[...], 1.0)
    terms(jf, per, r["low1"][...], dkv, scale_lora)
    je.start(0)
    jf.start(0)
    load_k.wait()
    dq[...] = (dot_nn(e0, r["q_dn"][...]) + dot_nn(e1, r["kv_dn"][...])
               + dot_nt(dkv, r["wk_v"][...].reshape(d, w)))
    je.move(0)
    jf.move(0)
    for cp in query:
        cp.wait()
    for c in range(halves):
        dq[...] += dot_nt(q_v[:, c * fc : (c + 1) * fc], w_v[c].reshape(d, fc))
    load_x.wait()
    gain = r["gain"][...]

    def back(i, _):
        at = pl.ds(pl.multiple_of(i * 128, 128), 128)
        n, inv = norm_parts(t2[at, :].astype(f32))
        do_v[at, :] = (dres[at, :] + norm_back(n, inv, gain, dq[at, :])).astype(bf16)
        return 0

    je.move(1)
    jf.move(1)
    lax.fori_loop(0, length // 128, back, 0)
    out = local(do_v, r["dx"], r["out_sem"])
    out.start()
    for i in range(2, last + 1):
        for job in (je, jf):
            job.move(i)
    for job in (ja, jb, jc, jd):
        for i in range(4, last + 1):
            job.move(i)
    out.wait()
    for buf in range(2):
        for o in range(1, members):
            ds_copy(buf, buf, o).wait_send()


def backward(z, args):
    vm = pl.BlockSpec(memory_space=pltpu.VMEM)
    hbm = pl.BlockSpec(memory_space=pl.ANY)
    m, n, d, rk, w = z.members, z.length, z.d, z.rk, z.w
    s = jax.ShapeDtypeStruct
    dma = pltpu.SemaphoreType.DMA
    shapes = job_shapes(z)
    legs = m - 1 + z.replicas.bit_length() - 1
    outs = dict(dx=s((n, d), bf16))
    scratch = dict(
        w_v=pltpu.VMEM((d // z.fc, m, z.rows, z.fc), bf16), wk_v=pltpu.VMEM((m, z.rows, w), bf16),
        t1=pltpu.VMEM((n, d), bf16), t2=pltpu.VMEM((n, d), bf16), q_v=pltpu.VMEM((n, d), bf16), do_v=pltpu.VMEM((n, d), bf16),
        dq=pltpu.VMEM((n, d), f32), kd_st=pltpu.VMEM((2, n, w), bf16), ds_st=pltpu.VMEM((2, m, z.cap, w), bf16),
        dk_r=pltpu.VMEM((m, m, z.cap, w), bf16),
        w_sem=dma((2, d // z.fc)), t_sem=dma((4,)), g_sem=dma((2,)), kd_sem=dma((2,)), dk_send=dma((2, m)),
        dk_recv=dma((m,)), out_sem=dma(()))
    for j, (blocks, lanes) in shapes.items():
        outs[j + "_out"] = s((rk, blocks * lanes), f32)
        scratch[j + "_w"] = pltpu.VMEM((m, blocks, rk, lanes), bf16)
        scratch[j + "_g"] = pltpu.VMEM((legs, blocks, rk, lanes), bf16)
        scratch[j + "_s"] = dma((legs,))
        scratch[j + "_r"] = dma((legs,))
    first_hbm = BWD_IN.index("ga")
    got = pl.pallas_call(
        lambda *refs: bwd_kernel(z, *refs),
        in_specs=[vm] * first_hbm + [hbm] * (len(BWD_IN) - first_hbm),
        out_specs=[hbm] + [vm] * len(JOBS),
        out_shape=[outs[k] for k in BWD_OUT],
        scratch_shapes=[scratch[k] for k in BWD_SCRATCH],
        compiler_params=pltpu.CompilerParams(
            vmem_limit_bytes=FWD_VMEM, collective_id=2, has_side_effects=True),
    )(*[args[k] for k in BWD_IN])
    return dict(zip(BWD_OUT, got))


def local(tokens, out_grad, token_perm, seq_lens, adapter_ids,
          attn_g, attn_b, wq, bq, wkv, bv, wmix, bmix, mlp_g, mlp_b, wexp, bexp, wred, bred,
          q_dn, q_up, kv_dn, kv_up, mix_dn, mix_up, exp_dn, exp_up, red_dn, red_up):
    members = lax.axis_size("shard")
    replicas = lax.axis_size("rep")
    rep = lax.axis_index("rep")
    length, d = tokens.shape
    experts, rank = q_dn.shape[:2]
    rk = experts * rank
    z = Sizes(members, replicas, length, d, wexp.shape[1], bv.shape[0] * members, rk, rank,
              seq_lens.shape[1], adapter_ids.shape[2])
    flat = lambda s: s.reshape(rk, s.shape[2])
    q_dn, q_up, kv_dn, kv_up, mix_dn, mix_up, exp_dn, exp_up, red_dn, red_up = map(
        flat, (q_dn, q_up, kv_dn, kv_up, mix_dn, mix_up, exp_dn, exp_up, red_dn, red_up))
    group = lax.dynamic_index_in_dim(
        token_perm.reshape(members, replicas, length), rep, 1, keepdims=False)

    def pad(rows, cols):
        return jnp.pad(rows.astype(f32), ((0, 0), (0, cols - rows.shape[1])))

    vecs = jnp.concatenate([v[None] for v in (attn_g, attn_b, bq, bmix, mlp_g, mlp_b, bred)]
                           + [pad(bv[None], z.rows).astype(bf16)], axis=0)
    top = pad(jnp.concatenate([vecs, bexp.reshape(SLOTS, z.sub)], axis=1), z.small_cols)
    table = pad(jnp.concatenate([seq_lens[0], adapter_ids[0].reshape(-1)])[None], z.small_cols)
    small = jnp.concatenate([top, table, jnp.zeros((7, z.small_cols), f32)], axis=0)
    by_chunk = lambda s: s.reshape(s.shape[0], members, SLOTS, z.sub).transpose(2, 0, 1, 3).reshape(
        SLOTS, s.shape[0], z.fc)
    chunked = (lambda s: s) if z.aligned else by_chunk
    got = forward(z, dict(
        x=tokens, dy=out_grad, small=small, group=group.reshape(members, 1, length), group_t=group.T,
        q_dn=q_dn, q_up=q_up, kv_dn=kv_dn, kv_up=kv_up, mix_dn=mix_dn, mix_up=mix_up, exp_dn=exp_dn,
        exp_up=chunked(exp_up), red_dn=chunked(red_dn), red_up=red_up,
        wq=wq, wkv=wkv, wmix=wmix, wexp=chunked(wexp), wred=wred.reshape(SLOTS, z.sub, d)))
    if not z.aligned:
        pack = 128 // z.sub
        for k in ("gup", "gdn"):
            got[k] = got[k].reshape(members, SLOTS // pack, pack, rk, z.sub).transpose(0, 1, 3, 2, 4).reshape(
                members, SLOTS // pack, rk, 128)
    back = backward(z, dict(
        got, mix_dn=mix_dn, mix_up=mix_up, q_dn=q_dn, q_up=q_up, kv_dn=kv_dn, kv_up=kv_up, dy=out_grad, x=tokens))
    c = d // members
    outs = [back[j + "_out"] for j in JOBS]

    def stack(g):
        return g.reshape(experts, rank, g.shape[1])

    g_exp_up, g_red_dn, one, two, three, four = outs
    return (got["layer"], back["dx"], stack(three[:, :c]), stack(four[:, :c]), stack(three[:, c:]),
            stack(four[:, c : c + z.w // members]), stack(one[:, c:]), stack(two[:, c:]), stack(one[:, :c]),
            stack(g_exp_up), stack(g_red_dn), stack(two[:, :c]))


def solution(mesh):
    both = ("shard", "rep")
    row, vec = P("shard", None), P("shard")
    in_specs = (
        P(both, None), P(both, None), P(), P(both, None), P(both, None, None),
        vec, vec, row, vec, row, vec, row, vec, vec, vec, row, vec, row, vec,
    ) + (P(),) * 10
    out_specs = (P(both, None), P(both, None)) + (P(None, None, "shard"),) * 10
    return jax.shard_map(local, mesh=mesh, in_specs=in_specs, out_specs=out_specs, check_vma=False)
```

```python
import jax
import jax.numpy as jnp
from jax import lax
from jax.experimental import pallas as pl
from jax.experimental.pallas import tpu as pltpu
from jax.sharding import PartitionSpec as P
from typing import NamedTuple

scale_lora = 0.5
eps = 1e-05
f32 = jnp.float32
bf16 = jnp.bfloat16
neg_big = -1e30
log2_e = 1.4426950408889634
gelu_c = 0.7978845608028654
VMEM_LIMIT = 60 * 1024 * 1024


def dot_nn(a, b):
    return lax.dot_general(a, b, (((1,), (0,)), ((), ())), preferred_element_type=f32)


def dot_nt(a, b):
    return lax.dot_general(a, b, (((1,), (1,)), ((), ())), preferred_element_type=f32)


def dot_tn(a, b):
    return lax.dot_general(a, b, (((0,), (0,)), ((), ())), preferred_element_type=f32)


def key_onehot(slot_row, slots):
    ids = lax.broadcasted_iota(jnp.int32, (slots, slot_row.shape[1]), 0)
    return jnp.where(ids == slot_row, 1.0, 0.0).astype(bf16)


def to_rows(x, heads):
    hd = x.shape[1] // heads
    return jnp.concatenate([x[:, h * hd : (h + 1) * hd] for h in range(heads)], axis=0)


def to_cols(x, heads):
    c = x.shape[0] // heads
    return jnp.concatenate([x[h * c : (h + 1) * c] for h in range(heads)], axis=1)


def softmax_rows(qr, kd, span, heads):
    rows, keys = qr.shape[0], kd.shape[0]
    c = rows // heads
    u = lax.broadcasted_iota(jnp.int32, (c, keys), 1).astype(f32)
    allowed = (u >= span[:, 0:1]) & (u <= span[:, 1:2])
    s = jnp.where(allowed[None], dot_nt(qr, kd).reshape(heads, c, keys), neg_big)
    top = jnp.max(s, axis=2, keepdims=True)
    e = jnp.exp2((s - top) * (kd.shape[1] ** (-0.5) * log2_e))
    p = e * (1.0 / jnp.sum(e, axis=2, keepdims=True))
    return p.reshape(rows, keys)


MESH = pl.DeviceIdType.MESH


class Gather:
    def __init__(self, members, own, full, slots, send_sem, recv_sem):
        self.members = members
        self.me, self.rep = lax.axis_index("shard"), lax.axis_index("rep")
        self.own, self.full = own, full
        self.base = [sum(slots[:i]) for i in range(len(slots))]
        self.send_sem, self.recv_sem = send_sem, recv_sem
        self.bits = [1 << i for i in range(1, members.bit_length() - 1)]
        self.planes = list(range(0, members, 2))
        self.sent = {}

    def place(self, kind, slot, offset):
        return self.full[kind].at[slot, self.me ^ offset]

    def copy(self, kind, slot, offset, there, to, to_slot):
        mine = self.sent.setdefault((kind, slot), {})
        at = mine.setdefault((offset, there, to_slot), len(mine))
        src = self.own[kind](slot) if offset == 0 else self.place(kind, slot, offset)
        pltpu.make_async_remote_copy(
            src, self.full[kind].at[to_slot, self.me ^ offset],
            self.send_sem.at[self.base[kind] + slot, at],
            self.recv_sem.at[self.base[kind] + to_slot, there],
            device_id=to, device_id_type=MESH).start()

    def wait(self, kind, slot, offset):
        piece = self.place(kind, slot, offset)
        pltpu.make_async_copy(piece, piece, self.recv_sem.at[self.base[kind] + slot, offset]).wait()

    def order(self, kind):
        return self.bits if kind % 2 == 0 else self.bits[::-1]

    def stage(self, kind, offset):
        return max(i for i, b in enumerate(self.order(kind)) if offset & b)

    def issue(self, slot, kinds, plane=True):
        for kind in kinds:
            if plane:
                for b in self.order(kind):
                    self.copy(kind, slot, 0, b, (self.me ^ b, self.rep), slot)
            self.copy(kind, slot, 0, 1, (self.me ^ 1, self.rep), slot)

    def arrive(self, slot, kinds, direct, swap_to=None):
        for kind in kinds:
            order = self.order(kind)
            some = [o for o in self.planes if o and (bin(o).count("1") == 1) == direct]
            some.sort(key=lambda o: self.stage(kind, o))
            for o in some:
                self.wait(kind, slot, o)
                for i in range(self.stage(kind, o) + 1, len(order)):
                    self.copy(kind, slot, o, o ^ order[i], (self.me ^ order[i], self.rep), slot)
                if swap_to is not None:
                    self.copy(kind, slot, o, o, (self.me, self.rep ^ 1), swap_to)
                self.copy(kind, slot, o, o ^ 1, (self.me ^ 1, self.rep), slot)

    def swapped(self, slot, kinds):
        for kind in kinds:
            for o in self.planes[1:]:
                self.wait(kind, slot, o)
                self.copy(kind, slot, o, o ^ 1, (self.me ^ 1, self.rep), slot)

    def ready(self, slot, kinds):
        for kind in kinds:
            for o in range(1, self.members, 2):
                self.wait(kind, slot, o)

    def finish(self):
        for (kind, slot), mine in self.sent.items():
            piece = self.place(kind, slot, 0)
            for at in mine.values():
                pltpu.make_async_copy(piece, piece, self.send_sem.at[self.base[kind] + slot, at]).wait()


U, V, C = (0, 1, 2), (3, 4, 5), (6, 7)
SLOTS = 8
WE, WR, AT, AB, KV = range(5)
BOTH, HALVES = (WE, WR), (AT, AB)
WQ, WMIX = 0, 1
SEND, NEAR, FAR, SWAP = range(4)
MLP_ORDER = (0, 1, 4, 3, 2, 6, 5, 7)
SERVE = {
    0: ((SEND, KV, 0),),
    1: ((SEND, WR, 0),),
    10: ((NEAR, KV, 0),),
    21: ((SEND, WE, 0),),
    24: ((NEAR, WR, 0),),
    25: ((FAR, KV, 0),),
    2: ((SEND, AT, 0),),
    4: ((NEAR, WE, 0),),
    5: ((FAR, WR, 0), (NEAR, AT, 0), (SEND, AB, 0), (FAR, WE, 0), (SEND, WE, 1), (SWAP, WR, 3), (FAR, AT, 0), (SEND, AB, 1), (SWAP, WE, 3), (NEAR, AB, 0), (NEAR, WE, 1), (SEND, AT, 1), (FAR, AB, 0),),
    15: ((NEAR, AB, 1),),
    41: ((FAR, WE, 1), (SEND, WR, 1),),
    43: ((FAR, AB, 1),),
    44: ((NEAR, AT, 1), (SEND, WE, 2), (SWAP, WE, 4),),
    46: ((NEAR, WR, 1),),
    7: ((FAR, AT, 1),),
    16: ((SEND, WR, 2),),
    17: ((FAR, WR, 1),),
    12: ((NEAR, WE, 2),),
    13: ((SEND, WR, 6),),
    60: ((NEAR, WR, 2),),
    61: ((SWAP, WR, 4),),
    62: ((FAR, WE, 2), (SEND, WE, 6),),
    63: ((FAR, WR, 2),),
    64: ((NEAR, WR, 6), (SEND, WE, 7),),
    66: ((NEAR, WE, 6),),
    67: ((FAR, WR, 6), (SEND, WR, 7),),
    69: ((NEAR, WE, 7), (FAR, WE, 6), (SWAP, WE, 5),),
    70: ((NEAR, WR, 7), (SWAP, WR, 5),),
    72: ((FAR, WE, 7), (FAR, WR, 7),),
}


def chunk_of(slot, parity):
    slot = jnp.int32(slot)
    low = jnp.where(slot < 3, slot, slot + 2)
    high = jnp.where(slot < 3, slot + 5, slot - 3)
    return jnp.where(slot >= 6, slot - 3, jnp.where(parity == 0, low, high))


def norm_parts(v):
    center = v - jnp.mean(v, axis=-1, keepdims=True)
    inv = lax.rsqrt(jnp.mean(center * center, axis=-1, keepdims=True) + eps)
    return center * inv, inv


def norm_back(n, inv, gain, dn):
    w = gain * dn
    return (w - jnp.mean(w, axis=-1, keepdims=True)
            - n * jnp.mean(w * n, axis=-1, keepdims=True)) * inv


class Sizes:
    def __init__(self, members, replicas, length, d, ff, hd, rk, rank, seqs, projs):
        self.members, self.replicas, self.length, self.d, self.ff = members, replicas, length, d, ff
        self.hd, self.rk, self.rank, self.seqs, self.projs = hd, rk, rank, seqs, projs
        self.heads = d // hd
        self.cap = 3 * length // (2 * members)
        self.slots = members * self.cap
        self.w = 2 * hd
        self.rows = d // members
        self.sub = ff // members // SLOTS
        self.fc = self.sub * members
        self.aligned = self.sub % 128 == 0
        self.be_at = 7 * self.rows
        self.vb_at = self.be_at + ff // members
        self.len_at = self.vb_at + hd // members
        self.ids_at = self.len_at + seqs
        self.small_cols = -(-(self.ids_at + seqs * projs) // 128) * 128


class FwdIn(NamedTuple):
    x: object
    small: object
    group: object
    q_dn: object
    q_up: object
    kv_dn: object
    kv_up: object
    dy: object
    mix_dn: object
    mix_up: object
    exp_dn: object
    exp_up: object
    red_dn: object
    red_up: object
    wq: object
    wkv: object
    wmix: object
    wexp: object
    wred: object


class FwdOut(NamedTuple):
    dres: object
    put: object
    slot: object
    info: object
    chosen: object
    low0: object
    low1: object
    low2: object
    low4: object
    e3: object
    gain: object
    a: object
    q: object
    o: object
    m: object
    resid: object
    kd: object
    gup: object
    gdn: object
    layer: object
    kvs: object
    ge: object
    gr: object
    ga: object
    gb: object
    gk: object


class FwdScratch(NamedTuple):
    y: object
    dy_v: object
    mix_dn_v: object
    mix_up_v: object
    exp_dn_v: object
    exp_up_v: object
    red_dn_v: object
    red_up_v: object
    late_sem: object
    we_v: object
    wr_v: object
    a_v: object
    q_v: object
    kvp: object
    kvb: object
    kd_st: object
    gup_st: object
    gdn_st: object
    sm: object
    lowr: object
    er: object
    low3: object
    e4: object
    send_sem: object
    recv_sem: object
    sm_send: object
    sm_recv: object
    kv_send: object
    kv_recv: object
    stage_sem: object
    store_sem: object
    load_sem: object
    kvb_sem: object
    kd_sem: object
    g_sem: object
    out_sem: object


class FwdRefs(NamedTuple):
    x: object
    small: object
    group: object
    q_dn: object
    q_up: object
    kv_dn: object
    kv_up: object
    dy: object
    mix_dn: object
    mix_up: object
    exp_dn: object
    exp_up: object
    red_dn: object
    red_up: object
    wq: object
    wkv: object
    wmix: object
    wexp: object
    wred: object
    dres: object
    put: object
    slot: object
    info: object
    chosen: object
    low0: object
    low1: object
    low2: object
    low4: object
    e3: object
    gain: object
    a: object
    q: object
    o: object
    m: object
    resid: object
    kd: object
    gup: object
    gdn: object
    layer: object
    kvs: object
    ge: object
    gr: object
    ga: object
    gb: object
    gk: object
    y: object
    dy_v: object
    mix_dn_v: object
    mix_up_v: object
    exp_dn_v: object
    exp_up_v: object
    red_dn_v: object
    red_up_v: object
    late_sem: object
    we_v: object
    wr_v: object
    a_v: object
    q_v: object
    kvp: object
    kvb: object
    kd_st: object
    gup_st: object
    gdn_st: object
    sm: object
    lowr: object
    er: object
    low3: object
    e4: object
    send_sem: object
    recv_sem: object
    sm_send: object
    sm_recv: object
    kv_send: object
    kv_recv: object
    stage_sem: object
    store_sem: object
    load_sem: object
    kvb_sem: object
    kd_sem: object
    g_sem: object
    out_sem: object


def fwd_kernel(z, *refs):
    r = FwdRefs(*refs)
    members, rows, fc, sub, d, hd = z.members, z.rows, z.fc, z.sub, z.d, z.hd
    length, cap, w, heads, rk = z.length, z.cap, z.w, z.heads, z.rk
    me, rep = lax.axis_index("shard"), lax.axis_index("rep")
    parity = lax.rem(rep, 2)
    half = rows // 2
    att = (r.wq, r.wmix)
    g = Gather(
        members,
        [lambda s: r.ge.at[s, me],
         lambda s: r.wred.at[chunk_of(s, parity)],
         lambda s: att[s].at[0:half],
         lambda s: att[s].at[half:rows],
         lambda s: r.wkv],
        [r.ge, r.gr, r.ga, r.gb, r.gk],
        [SLOTS, SLOTS, 2, 2, 1], r.send_sem, r.recv_sem)
    we_v, wr_v, sm, y, dm = r.we_v, r.wr_v, r.sm, r.y, r.dres

    def serve(point):
        for op, kind, slot in SERVE.get(point, ()):
            swap_to = slot + 3 if slot in U and kind in BOTH else None
            if op == SEND:
                g.issue(slot, (kind,))
            elif op == SWAP:
                g.swapped(slot, (kind,))
            else:
                g.arrive(slot, (kind,), op == NEAR, swap_to)

    barrier = pltpu.get_barrier_semaphore()
    others = [(me ^ o, rep) for o in range(1, members)] + [(me, rep ^ 1)]
    for to in others:
        pl.semaphore_signal(barrier, inc=1, device_id=to, device_id_type=MESH)

    def stage_copies(slot):
        j = chunk_of(slot, parity)
        to = we_v.at[0, slot]
        if not z.aligned:
            return [pltpu.make_async_copy(r.wexp.at[j], to, r.stage_sem.at[slot])]
        return [pltpu.make_async_copy(
            r.wexp.at[:, pl.ds(pl.multiple_of(s * (z.ff // members) + j * sub, sub), sub)],
            to.at[:, s * sub : (s + 1) * sub], r.stage_sem.at[slot]) for s in range(members)]

    def stored(slot):
        return pltpu.make_async_copy(we_v.at[0, slot], r.ge.at[slot, me], r.store_sem.at[slot])

    def staged(slot):
        pltpu.make_async_copy(we_v.at[0, slot], we_v.at[0, slot], r.stage_sem.at[slot]).wait()
        stored(slot).start()

    for slot in range(SLOTS):
        for cp in stage_copies(slot):
            cp.start()
    pl.semaphore_wait(barrier, len(others))

    def small_copy(o):
        return pltpu.make_async_remote_copy(
            sm.at[me], sm.at[me], r.sm_send.at[o], r.sm_recv.at[o],
            device_id=(me ^ o, rep), device_id_type=MESH)

    serve(0)
    coming = [pltpu.make_async_copy(src, dst, r.late_sem.at[i]) for i, (src, dst) in enumerate((
        (r.mix_dn, r.mix_dn_v), (r.mix_up, r.mix_up_v), (r.dy, r.dy_v), (r.exp_dn, r.exp_dn_v),
        (r.exp_up, r.exp_up_v), (r.red_dn, r.red_dn_v), (r.red_up, r.red_up_v)))]
    for cp in coming:
        cp.start()
    r = r._replace(dy=r.dy_v, mix_dn=r.mix_dn_v, mix_up=r.mix_up_v, exp_dn=r.exp_dn_v, exp_up=r.exp_up_v,
                   red_dn=r.red_dn_v, red_up=r.red_up_v)
    sm[me] = r.small[...]
    for o in range(1, members):
        small_copy(o).start()
    for slot in range(SLOTS):
        staged(slot)
    for slot in range(SLOTS):
        stored(slot).wait()
    serve(1)
    for o in range(1, members):
        pltpu.make_async_copy(sm.at[me ^ o], sm.at[me ^ o], r.sm_recv.at[o]).wait()

    def vec(row):
        return jnp.concatenate([sm[s, :, row * rows : (row + 1) * rows] for s in range(members)], axis=1)

    def norm_rows(src, gain, bias, dst, part):
        gv, bv = vec(gain), vec(bias)

        def body(i, _):
            at = pl.ds(pl.multiple_of(i * 128, 128), 128)
            n, _inv = norm_parts(src[at, :].astype(f32))
            dst[at, :] = (n * gv + bv).astype(bf16)
            return 0

        lax.fori_loop(part * length // 256, (part + 1) * length // 256, body, 0)

    for part in range(2):
        serve(10 + part)
        norm_rows(r.x, 0, 1, r.a_v, part)

    r.gain[...] = vec(0)

    t_row = lax.broadcasted_iota(jnp.int32, (1, length), 1)
    before_t = lax.broadcasted_iota(jnp.int32, (length, length), 0) < lax.broadcasted_iota(
        jnp.int32, (length, length), 1)
    c_ids = lax.broadcasted_iota(jnp.int32, (cap, length), 0)
    lane = lax.broadcasted_iota(jnp.int32, (cap, 128), 1)
    span = length * z.replicas
    first = (me * z.replicas + rep) * length
    tf = t_row.astype(f32)
    src_cols = lax.div(r.group[...], span).astype(f32).T
    chosen = jnp.zeros((length, 128), f32)
    for k in range(members):
        serve(20 + k)
        row = r.group[k : k + 1, :]
        src = lax.div(row, span)
        earlier = jnp.where((src_cols[:, k : k + 1] == src.astype(f32)) & before_t, 1.0, 0.0)
        slot_row = src * cap + jnp.sum(earlier, axis=0, keepdims=True).astype(jnp.int32)
        r.slot[k] = slot_row
        hit = slot_row == c_ids + me * cap

        def pick(values):
            return jnp.sum(jnp.where(hit, values, 0.0), axis=1, keepdims=True)

        full = pick(jnp.ones_like(tf))
        tok = pick((row - first + 1).astype(f32)) - 1.0
        put = jnp.where(tok == tf, 1.0, 0.0).astype(bf16)
        r.put[k] = put
        end = jnp.zeros((1, 1), f32)
        start = jnp.zeros_like(tf)
        ids = [jnp.zeros_like(tf) for _ in range(z.projs)]
        for j in range(z.seqs):
            n = sm[k, :, z.len_at + j : z.len_at + j + 1]
            inside = (tf >= end) & (tf < end + n)
            end = end + n
            start = start + jnp.where(tf >= end, n, 0.0)
            for p in range(z.projs):
                at = z.ids_at + j * z.projs + p
                ids[p] = ids[p] + jnp.where(inside, sm[k, :, at : at + 1], 0.0)
        info = jnp.where(lane == 0, pick(start) + (1.0 - full), 0.0)
        info = jnp.where(lane == 1, pick(tf), info)
        for p in range(z.projs):
            info = jnp.where(lane == 2 + p, pick(ids[p]), info)
        r.info[k] = info
        chosen = chosen + dot_tn(put, info.astype(bf16))
    r.chosen[...] = chosen
    rank_of = lax.broadcasted_iota(jnp.int32, (length, rk), 1) // z.rank

    def mask(p):
        return jnp.where(rank_of.astype(f32) == r.chosen[:, 2 + p : 3 + p], 1.0, 0.0)

    a_v, q_v = r.a_v, r.q_v
    o_v = q_v
    serve(2)
    r.low0[...] = (dot_nt(a_v[...], r.q_dn[...]) * mask(0)).astype(bf16)
    r.low1[...] = (dot_nt(a_v[...], r.kv_dn[...]) * mask(1)).astype(bf16)
    out_a = pltpu.make_async_copy(a_v, r.a, r.out_sem.at[0])
    out_a.start()

    serve(3)
    g.ready(0, (KV,))
    kv_loads = [pltpu.make_async_copy(
        r.wkv if o == 0 else g.place(KV, 0, o), we_v.at[1, me ^ o, :, 0:w], r.kv_send.at[o]) for o in range(members)]
    for cp in kv_loads:
        cp.start()
    for cp in kv_loads:
        cp.wait()
    back_kv = pltpu.make_async_copy(we_v.at[1, me, :, 0:w], g.place(KV, 0, 0), r.kv_send.at[0])
    back_kv.start()
    vb = jnp.concatenate([sm[s, :, z.vb_at : z.vb_at + hd // members] for s in range(members)], axis=1)
    kv_bias = jnp.concatenate([jnp.zeros((1, hd), f32), vb], axis=1)
    kv = (dot_nn(a_v[...], we_v[1, :, :, 0:w].reshape(d, w)) + kv_bias
          + scale_lora * dot_nn(r.low1[...], r.kv_up[...])).astype(bf16)
    for k in range(members):
        r.kvp[k] = dot_nn(r.put[k], kv).astype(bf16)

    def kv_copy(o):
        return pltpu.make_async_remote_copy(
            r.kvp, r.kvs.at[me], r.kv_send.at[o], r.kv_recv.at[o],
            device_id=(me ^ o, rep), device_id_type=MESH)

    back_kv.wait()
    own_kv = pltpu.make_async_copy(r.kvp, r.kvs.at[me], r.kv_send.at[0])
    for o in range(1, members):
        kv_copy(o).start()
    own_kv.start()

    for slot in V:
        g.issue(slot, BOTH, False)
    serve(4)

    def wide_load(which):
        g.ready(which, HALVES)
        out = []
        for kind in HALVES:
            for o in range(members):
                src = g.own[kind](which) if o == 0 else g.place(kind, which, o)
                for c in range(d // fc):
                    out.append(pltpu.make_async_copy(
                        src.at[:, c * fc : (c + 1) * fc],
                        we_v.at[c, me ^ o, (kind - AT) * half : (kind - AT + 1) * half],
                        r.load_sem.at[kind - AT, c, o]))
        for cp in out:
            cp.start()
        for cp in out:
            cp.wait()
        back = [pltpu.make_async_copy(
            we_v.at[c, me, (kind - AT) * half : (kind - AT + 1) * half],
            g.place(kind, which, 0).at[:, c * fc : (c + 1) * fc],
            r.load_sem.at[kind - AT, c, 0]) for kind in HALVES for c in range(d // fc)]
        for cp in back:
            cp.start()
        return back

    serve(5)
    back_q = wide_load(WQ)
    q_bias = vec(2)
    for c in range(d // fc):
        serve(14 + c)
        at = slice(c * fc, (c + 1) * fc)
        q_v[:, at] = (dot_nn(a_v[...], we_v[c].reshape(d, fc)) + q_bias[:, at]
                      + scale_lora * dot_nn(r.low0[...], r.q_up[:, at])).astype(bf16)
    out_q = pltpu.make_async_copy(q_v, r.q, r.out_sem.at[1])
    out_q.start()

    for cp in back_q:
        cp.wait()

    serve(6)

    for o in range(1, members):
        pltpu.make_async_copy(r.kvs.at[me ^ o], r.kvs.at[me ^ o], r.kv_recv.at[o]).wait()
    own_kv.wait()
    for cp in coming:
        cp.wait()
    dm[...] = jnp.zeros_like(dm)

    def kvb_load(k, buf):
        return pltpu.make_async_copy(r.kvs.at[:, k], r.kvb.at[buf], r.kvb_sem.at[buf])

    def kd_out(k, buf):
        return pltpu.make_async_copy(r.kd_st.at[buf], r.kd.at[k], r.kd_sem.at[buf])

    kvb_load(0, 0).start()
    groups = 2

    def attend(k, _):
        buf = lax.rem(k, 2)

        @pl.when(k + 1 < members)
        def _():
            kvb_load(k + 1, 1 - buf).start()

        for i in range(min(members, 16)):
            if 40 + i in SERVE:
                pl.when(k == i)(lambda i=i: serve(40 + i))
        kvb_load(k, buf).wait()
        oh = key_onehot(r.slot[k], z.slots)
        kvd = dot_tn(oh, r.kvb[buf].reshape(z.slots, w)).astype(bf16)

        @pl.when(k >= 2)
        def _():
            kd_out(k, buf).wait()

        r.kd_st[buf] = kvd
        kd_out(k, buf).start()
        put = r.put[k]
        qp = dot_nn(put, q_v[...]).astype(bf16)
        info = r.info[k]
        outs = []
        per = heads // groups
        for h in range(groups):
            qr = to_rows(qp[:, h * per * hd : (h + 1) * per * hd], per)
            p = softmax_rows(qr, kvd[:, :hd], info, per).astype(bf16)
            outs.append(to_cols(dot_nn(p, kvd[:, hd:]).astype(bf16), per))
        dm[...] += dot_tn(put, jnp.concatenate(outs, axis=1))
        return 0

    lax.fori_loop(0, members, attend, 0)
    out_q.wait()
    o_v[...] = dm[...].astype(bf16)
    out_o = pltpu.make_async_copy(o_v, r.o, r.out_sem.at[2])
    out_o.start()
    r.low2[...] = (dot_nt(o_v[...], r.mix_dn[...]) * mask(2)).astype(bf16)
    serve(7)
    back_m = wide_load(WMIX)
    mix_bias = vec(3)
    for c in range(d // fc):
        serve(16 + c)
        at = slice(c * fc, (c + 1) * fc)
        y[:, at] = (r.x[:, at].astype(f32) + dot_nn(o_v[...], we_v[c].reshape(d, fc)) + mix_bias[:, at]
                    + scale_lora * dot_nn(r.low2[...], r.mix_up[:, at]))

    def load(slot, buf):
        out = [pltpu.make_async_copy(r.ge.at[slot], we_v.at[buf], r.load_sem.at[0, buf, 0])]
        for o in range(members):
            src = g.own[WR](slot) if o == 0 else g.place(WR, slot, o)
            out.append(pltpu.make_async_copy(src, wr_v.at[buf, me ^ o], r.load_sem.at[1, buf, o]))
        return out

    def fetch(slot, buf):
        g.ready(slot, BOTH)
        for cp in load(slot, buf):
            cp.start()

    for cp in back_m:
        cp.wait()
    out_r = pltpu.make_async_copy(y, r.resid, r.out_sem.at[3])
    out_r.start()
    out_a.wait()
    m_v = a_v
    for part in range(2):
        serve(12 + part)
        norm_rows(y, 4, 5, m_v, part)
    serve(8)
    out_m = pltpu.make_async_copy(m_v, r.m, r.out_sem.at[0])
    out_m.start()
    r.low3[...] = (dot_nt(m_v[...], r.exp_dn[...]) * mask(3)).astype(bf16)
    r.e4[...] = (scale_lora * dot_nt(r.dy[...], r.red_up[...]) * mask(4)).astype(bf16)
    dm[...] = jnp.zeros_like(dm)
    r.lowr[...] = jnp.zeros_like(r.lowr)
    r.er[...] = jnp.zeros_like(r.er)
    out_r.wait()
    y[...] += vec(6)

    def g_out(j, buf):
        return (pltpu.make_async_copy(r.gup_st.at[buf], r.gup.at[:, j], r.g_sem.at[0, buf]),
                pltpu.make_async_copy(r.gdn_st.at[buf], r.gdn.at[:, j], r.g_sem.at[1, buf]))

    serve(9)
    fetch(MLP_ORDER[0], 0)

    def step(n, _):
        for i in range(SLOTS):
            if 60 + 2 * i in SERVE:
                pl.when(n == i)(lambda i=i: serve(60 + 2 * i))
        buf = lax.rem(n, 2)
        slot = jnp.int32(0)
        for i, q in enumerate(MLP_ORDER):
            slot = jnp.where(n == i, q, slot)
        for cp in load(slot, buf):
            cp.wait()
        j = chunk_of(slot, parity)
        we = we_v[buf].reshape(d, fc)
        wr = wr_v[buf].reshape(fc, d)
        if z.aligned:
            def cut(ref):
                return jnp.concatenate([ref[:, pl.ds(pl.multiple_of(s * (z.ff // members) + j * sub, sub), sub)]
                                        for s in range(members)], axis=1)
            bup, adn = cut(r.exp_up), cut(r.red_dn)
        else:
            bup, adn = r.exp_up[j], r.red_dn[j]
        be = jnp.zeros((1, fc), f32)
        for i in range(SLOTS):
            lo = z.be_at + i * sub
            row = jnp.concatenate([sm[s, :, lo : lo + sub] for s in range(members)], axis=1)
            be = jnp.where(j == i, row, be)
        hid = dot_nn(m_v[...], we) + be
        hid = hid + scale_lora * dot_nn(r.low3[...], bup)
        cube = hid * hid * hid
        t = jnp.tanh(gelu_c * (hid + 0.044715 * cube))
        act = (0.5 * hid * (1.0 + t)).astype(bf16)
        slope = 0.5 * (1.0 + t) + 0.5 * hid * (1.0 - t * t) * (
            gelu_c * (1.0 + 3.0 * 0.044715 * hid * hid)
        )
        dact = dot_nt(r.dy[...], wr) + dot_nn(r.e4[...], adn)
        dh = (dact * slope).astype(bf16)
        for i in range(SLOTS):
            def middle(i=i):
                serve(61 + 2 * i)
                if i + 1 < SLOTS:
                    fetch(MLP_ORDER[i + 1], (i + 1) % 2)
            pl.when(n == i)(middle)
        y[...] += dot_nn(act, wr)
        dm[...] += dot_nt(dh, we)
        r.lowr[...] += dot_nt(act, adn)
        r.er[...] += dot_nt(dh, bup)
        gup = (scale_lora * dot_tn(r.low3[...], dh)).astype(bf16)
        gdn = dot_tn(r.e4[...], act).astype(bf16)

        @pl.when(n >= 2)
        def _():
            for cp in g_out(j, buf):
                cp.wait()

        for to in range(members):
            r.gup_st[buf, to] = gup[:, to * sub : (to + 1) * sub]
            r.gdn_st[buf, to] = gdn[:, to * sub : (to + 1) * sub]
        for cp in g_out(j, buf):
            cp.start()
        return 0

    lax.fori_loop(0, SLOTS, step, 0)

    low4 = (r.lowr[...] * mask(4)).astype(bf16)
    r.low4[...] = low4
    out_o.wait()
    layer_v = q_v
    for c in range(d // fc):
        at = slice(c * fc, (c + 1) * fc)
        layer_v[:, at] = (y[:, at] + scale_lora * dot_nn(low4, r.red_up[:, at])).astype(bf16)
    out_l = pltpu.make_async_copy(layer_v, r.layer, r.out_sem.at[1])
    out_l.start()
    back_r = pltpu.make_async_copy(r.resid, y, r.out_sem.at[3])
    back_r.start()
    e3 = (scale_lora * r.er[...] * mask(3)).astype(bf16)
    r.e3[...] = e3
    gain = vec(4)
    back_r.wait()

    def last(i, _):
        at = pl.ds(pl.multiple_of(i * 128, 128), 128)
        n, inv = norm_parts(y[at, :])
        dn = dm[at, :] + dot_nn(r.e3[at, :], r.exp_dn[...])
        dm[at, :] = r.dy[at, :].astype(f32) + norm_back(n, inv, gain, dn)
        return 0

    lax.fori_loop(0, length // 128, last, 0)
    out_l.wait()
    out_m.wait()
    for buf in range(2):
        kd_out(buf, buf).wait()
        for cp in g_out(buf, buf):
            cp.wait()
    for o in range(1, members):
        small_copy(o).wait_send()
        kv_copy(o).wait_send()
    g.finish()


def forward(z, args):
    vm = pl.BlockSpec(memory_space=pltpu.VMEM)
    hbm = pl.BlockSpec(memory_space=pl.ANY)
    m, n, d, rk, w = z.members, z.length, z.d, z.rk, z.w
    s = jax.ShapeDtypeStruct
    half = z.rows // 2
    outs = dict(
        dres=s((n, d), f32), put=s((m, z.cap, n), bf16), slot=s((m, 1, n), jnp.int32),
        info=s((m, z.cap, 128), f32), chosen=s((n, 128), f32),
        low0=s((n, rk), bf16), low1=s((n, rk), bf16), low2=s((n, rk), bf16), low4=s((n, rk), bf16), e3=s((n, rk), bf16), gain=s((1, d), f32),
        a=s((n, d), bf16), q=s((n, d), bf16), o=s((n, d), bf16), m=s((n, d), bf16), resid=s((n, d), f32),
        kd=s((m, n, w), bf16), gup=s((m, SLOTS, rk, z.sub), bf16), gdn=s((m, SLOTS, rk, z.sub), bf16),
        layer=s((n, d), bf16), kvs=s((m, m, z.cap, w), bf16),
        ge=s((SLOTS, m, z.rows, z.fc), bf16), gr=s((SLOTS, m, z.sub, d), bf16),
        ga=s((2, m, half, d), bf16), gb=s((2, m, half, d), bf16), gk=s((1, m, z.rows, w), bf16))
    in_vmem = 11
    sends = m - 1 + m // 2
    dma = pltpu.SemaphoreType.DMA
    items = 2 * SLOTS + 5
    scratch = dict(
        y=pltpu.VMEM((n, d), f32), dy_v=pltpu.VMEM((n, d), bf16), mix_dn_v=pltpu.VMEM((rk, d), bf16),
        mix_up_v=pltpu.VMEM((rk, d), bf16), exp_dn_v=pltpu.VMEM((rk, d), bf16),
        exp_up_v=pltpu.VMEM(args.exp_up.shape, bf16), red_dn_v=pltpu.VMEM(args.exp_up.shape, bf16),
        red_up_v=pltpu.VMEM((rk, d), bf16), late_sem=dma((7,)), we_v=pltpu.VMEM((2, m, z.rows, z.fc), bf16), wr_v=pltpu.VMEM((2, m, z.sub, d), bf16),
        a_v=pltpu.VMEM((n, d), bf16), q_v=pltpu.VMEM((n, d), bf16),
        kvp=pltpu.VMEM((m, z.cap, w), bf16), kvb=pltpu.VMEM((2, m, z.cap, w), bf16),
        kd_st=pltpu.VMEM((2, n, w), bf16), gup_st=pltpu.VMEM((2, m, rk, z.sub), bf16),
        gdn_st=pltpu.VMEM((2, m, rk, z.sub), bf16), sm=pltpu.VMEM((m, 1, z.small_cols), f32),
        lowr=pltpu.VMEM((n, rk), f32), er=pltpu.VMEM((n, rk), f32), low3=pltpu.VMEM((n, rk), bf16), e4=pltpu.VMEM((n, rk), bf16),
        send_sem=dma((items, sends)), recv_sem=dma((items, m)), sm_send=dma((m,)), sm_recv=dma((m,)),
        kv_send=dma((m,)), kv_recv=dma((m,)), stage_sem=dma((SLOTS,)), store_sem=dma((SLOTS,)),
        load_sem=dma((2, 2, m)), kvb_sem=dma((2,)), kd_sem=dma((2,)), g_sem=dma((2, 2)), out_sem=dma((4,)))
    got = pl.pallas_call(
        lambda *refs: fwd_kernel(z, *refs),
        in_specs=[vm] * 7 + [hbm] * 12,
        out_specs=[vm] * in_vmem + [hbm] * (len(FwdOut._fields) - in_vmem),
        out_shape=list(FwdOut(**outs)),
        scratch_shapes=list(FwdScratch(**scratch)),
        compiler_params=pltpu.CompilerParams(
            vmem_limit_bytes=FWD_VMEM, collective_id=1, has_side_effects=True),
    )(*args)
    return FwdOut(*got)


FWD_VMEM = 62 * 1024 * 1024


class Job:
    def __init__(self, members, replicas, work, got, out, send_sem, recv_sem, turn):
        self.me, self.rep = lax.axis_index("shard"), lax.axis_index("rep")
        self.work, self.got, self.out = work, got, out
        self.send_sem, self.recv_sem = send_sem, recv_sem
        bits = [1 << i for i in range(members.bit_length() - 1)]
        bits = bits if turn == 0 else bits[:1] + bits[1:][::-1]
        self.shard_stages = len(bits)
        self.stages = []
        at, decided = 0, 0
        for b in bits:
            free = [f for f in range(members) if not f & (decided | b)]
            self.stages.append((b, at, free, decided))
            at += len(free)
            decided |= b
        rk = work.shape[2]
        turns = [1 << i for i in range(replicas.bit_length() - 1)]
        sizes = [rk >> (i + 1) for i in range(len(turns))]
        row = 0
        for b, size in list(zip(turns, sizes)) + list(zip(turns, sizes))[::-1]:
            if row + size > rk:
                at, row = at + 1, 0
            self.stages.append((b, at, row, size))
            row += size
        self.sem_at = [s[1] for s in self.stages[: len(bits)]] + [
            self.stages[len(bits) - 1][1] + 1 + i for i in range(2 * len(turns))]
        self.count = len(self.stages)

    def rows(self, i):
        b, _, _, size = self.stages[i]
        start = jnp.int32(0)
        for b2, _, _, size2 in self.stages[self.shard_stages : self.shard_stages + self.turns()]:
            if b2 < b:
                start = start + lax.rem(lax.div(self.rep, b2), 2) * size2
        mine = lax.rem(lax.div(self.rep, b), 2)
        near = pl.ds(pl.multiple_of(start + mine * size, size), size)
        far = pl.ds(pl.multiple_of(start + (1 - mine) * size, size), size)
        return near, far

    def turns(self):
        return (self.count - self.shard_stages) // 2

    def copy(self, i, n=0):
        if i < self.shard_stages:
            b, at, free, decided = self.stages[i]
            src = self.work.at[free[n] | (self.me & decided) | ((self.me ^ b) & b)]
            dst, to = self.got.at[at + n], (self.me ^ b, self.rep)
        else:
            b, at, row, size = self.stages[i]
            near, far = self.rows(i)
            src = self.work.at[self.me, :, far if i < self.shard_stages + self.turns() else near]
            dst, to = self.got.at[at, :, row : row + size], (self.me, self.rep ^ b)
        sem = self.sem_at[i] + n
        return pltpu.make_async_remote_copy(
            src, dst, self.send_sem.at[sem], self.recv_sem.at[sem], device_id=to, device_id_type=MESH)

    def start(self, i):
        for n in range(len(self.stages[i][2]) if i < self.shard_stages else 1):
            self.copy(i, n).start()

    def add(self, i):
        if i < self.shard_stages:
            b, at, free, decided = self.stages[i]
            for n, f in enumerate(free):
                cp = self.copy(i, n)
                cp.wait_recv()
                cp.wait_send()
                keep = f | (self.me & decided) | (self.me & b)
                self.work[keep] = (self.work[keep].astype(f32) + self.got[at + n].astype(f32)).astype(bf16)
            return
        b, at, row, size = self.stages[i]
        cp = self.copy(i)
        cp.wait_recv()
        cp.wait_send()
        near, far = self.rows(i)
        came = self.got[at, :, row : row + size]
        if i < self.shard_stages + self.turns():
            kept = self.work[self.me, :, near].astype(f32) + came.astype(f32)
            self.work[self.me, :, near] = kept.astype(bf16)
        else:
            self.work[self.me, :, far] = came
        if i + 1 == self.count:
            blocks, lanes = self.work.shape[1], self.work.shape[3]
            for j in range(blocks):
                self.out[:, j * lanes : (j + 1) * lanes] = self.work[self.me, j].astype(f32)

    def move(self, i):
        self.add(i)
        if i + 1 < self.count:
            self.start(i + 1)


class BwdIn(NamedTuple):
    dres: object
    put: object
    slot: object
    info: object
    chosen: object
    low0: object
    low1: object
    low2: object
    low4: object
    e3: object
    gain: object
    mix_dn: object
    mix_up: object
    q_dn: object
    q_up: object
    kv_dn: object
    kv_up: object
    ga: object
    gb: object
    gk: object
    q: object
    a: object
    o: object
    m: object
    dy: object
    x: object
    kd: object
    gup: object
    gdn: object


class BwdOut(NamedTuple):
    dx: object
    ja_out: object
    jb_out: object
    jc_out: object
    jd_out: object
    je_out: object
    jf_out: object
    jg_out: object


class BwdScratch(NamedTuple):
    w_v: object
    wk_v: object
    t1: object
    t2: object
    q_v: object
    do_v: object
    dq: object
    kd_st: object
    ds_st: object
    dk_r: object
    w_sem: object
    t_sem: object
    g_sem: object
    kd_sem: object
    dk_send: object
    dk_recv: object
    out_sem: object
    ja_w: object
    ja_g: object
    ja_s: object
    ja_r: object
    jb_w: object
    jb_g: object
    jb_s: object
    jb_r: object
    jc_w: object
    jc_g: object
    jc_s: object
    jc_r: object
    jd_w: object
    jd_g: object
    jd_s: object
    jd_r: object
    je_w: object
    je_g: object
    je_s: object
    je_r: object
    jf_w: object
    jf_g: object
    jf_s: object
    jf_r: object
    jg_w: object
    jg_g: object
    jg_s: object
    jg_r: object


class BwdRefs(NamedTuple):
    dres: object
    put: object
    slot: object
    info: object
    chosen: object
    low0: object
    low1: object
    low2: object
    low4: object
    e3: object
    gain: object
    mix_dn: object
    mix_up: object
    q_dn: object
    q_up: object
    kv_dn: object
    kv_up: object
    ga: object
    gb: object
    gk: object
    q: object
    a: object
    o: object
    m: object
    dy: object
    x: object
    kd: object
    gup: object
    gdn: object
    dx: object
    ja_out: object
    jb_out: object
    jc_out: object
    jd_out: object
    je_out: object
    jf_out: object
    jg_out: object
    w_v: object
    wk_v: object
    t1: object
    t2: object
    q_v: object
    do_v: object
    dq: object
    kd_st: object
    ds_st: object
    dk_r: object
    w_sem: object
    t_sem: object
    g_sem: object
    kd_sem: object
    dk_send: object
    dk_recv: object
    out_sem: object
    ja_w: object
    ja_g: object
    ja_s: object
    ja_r: object
    jb_w: object
    jb_g: object
    jb_s: object
    jb_r: object
    jc_w: object
    jc_g: object
    jc_s: object
    jc_r: object
    jd_w: object
    jd_g: object
    jd_s: object
    jd_r: object
    je_w: object
    je_g: object
    je_s: object
    je_r: object
    jf_w: object
    jf_g: object
    jf_s: object
    jf_r: object
    jg_w: object
    jg_g: object
    jg_s: object
    jg_r: object


def job_shapes(z):
    wide = z.rows // min(128, z.rows)
    lanes = min(128, z.rows)
    chunks = (SLOTS, z.sub) if z.aligned else (SLOTS * z.sub // 128, 128)
    return (chunks, chunks, (2 * wide, lanes), (2 * wide, lanes), (wide, lanes), (wide, lanes), (wide + 1, lanes))


def bwd_kernel(z, *refs):
    r = BwdRefs(*refs)
    members, replicas, rows, fc, d, hd = z.members, z.replicas, z.rows, z.fc, z.d, z.hd
    length, cap, w, heads, rk = z.length, z.cap, z.w, z.heads, z.rk
    me, rep = lax.axis_index("shard"), lax.axis_index("rep")
    half = rows // 2
    halves = d // fc
    w_v, t1, t2, q_v, do_v, dq, dres = r.w_v, r.t1, r.t2, r.q_v, r.do_v, r.dq, r.dres
    outs = refs[len(BwdIn._fields) + 1 : len(BwdIn._fields) + len(BwdOut._fields)]
    held = refs[-4 * len(outs) :]
    ja, jb, jc, jd, je, jf, jg = (
        Job(members, replicas, held[4 * i], held[4 * i + 1], out, held[4 * i + 2], held[4 * i + 3], i % 2)
        for i, out in enumerate(outs))

    barrier = pltpu.get_barrier_semaphore()
    others = [(me ^ o, rep) for o in range(1, members)]
    b = 1
    while b < replicas:
        others.append((me, rep ^ b))
        b *= 2
    for to in others:
        pl.semaphore_signal(barrier, inc=1, device_id=to, device_id_type=MESH)

    def local(src, dst, sem):
        return pltpu.make_async_copy(src, dst, sem)

    def wide(which):
        return [local(part.at[which, :, :, c * fc : (c + 1) * fc],
                      w_v.at[c, :, h * half : (h + 1) * half], r.w_sem.at[h, c])
                for h, part in enumerate((r.ga, r.gb)) for c in range(halves)]

    load_up = local(r.gup, r.ja_w, r.g_sem.at[0])
    load_dn = local(r.gdn, r.jb_w, r.g_sem.at[1])
    load_up.start()
    load_dn.start()
    mix = wide(WMIX)
    for cp in mix:
        cp.start()
    load_m = local(r.m, t1, r.t_sem.at[0])
    load_dy = local(r.dy, t2, r.t_sem.at[1])
    load_q = local(r.q, q_v, r.t_sem.at[2])
    load_k = local(r.gk.at[0], r.wk_v, r.t_sem.at[3])
    for cp in (load_m, load_dy, load_q, load_k):
        cp.start()
    pl.semaphore_wait(barrier, len(others))
    load_up.wait()
    ja.start(0)
    load_dn.wait()
    jb.start(0)

    rank_of = (lax.broadcasted_iota(jnp.int32, (length, rk), 1) // z.rank).astype(f32)

    def mask(p):
        return jnp.where(rank_of == r.chosen[:, 2 + p : 3 + p], 1.0, 0.0)

    def terms(job, block, left, right, sc):
        lanes = job.work.shape[3]
        g = dot_tn(left, right) * sc
        width = right.shape[1] // members
        for to in range(members):
            for i in range(-(-width // lanes)):
                part = g[:, to * width + i * lanes : to * width + min((i + 1) * lanes, width)]
                if part.shape[1] < lanes:
                    part = jnp.concatenate([part, jnp.zeros((rk, lanes - part.shape[1]), f32)], axis=1)
                job.work[to, block + i] = part.astype(bf16)

    per = r.jc_w.shape[1] // 2

    dresl = do_v
    dresl[...] = dres[...].astype(bf16)
    e2 = (scale_lora * dot_nt(dresl[...], r.mix_up[...]) * mask(2)).astype(bf16)
    terms(jd, per, r.low2[...], dresl[...], scale_lora)
    load_m.wait()
    terms(jc, 0, r.e3[...], t1[...], 1.0)
    load_o = local(r.o, t1, r.t_sem.at[0])
    load_o.start()
    load_dy.wait()
    terms(jd, 0, r.low4[...], t2[...], scale_lora)
    load_x = local(r.x, t2, r.t_sem.at[1])
    load_x.start()
    jd.start(0)
    for cp in mix:
        cp.wait()
    ja.move(0)
    dq[...] = dot_nt(dresl[:, 0:fc], w_v[0].reshape(d, fc)) + dot_nn(e2, r.mix_dn[...])
    jb.move(0)
    for c in range(1, halves):
        dq[...] += dot_nt(dresl[:, c * fc : (c + 1) * fc], w_v[c].reshape(d, fc))
    do_v[...] = dq[...].astype(bf16)
    query = wide(WQ)
    for cp in query:
        cp.start()
    load_o.wait()
    terms(jc, per, e2, t1[...], 1.0)
    jc.start(0)
    load_a = local(r.a, t1, r.t_sem.at[0])
    load_a.start()
    jd.move(0)
    dq[...] = jnp.zeros_like(dq)
    load_q.wait()

    def kd_load(k, buf):
        return local(r.kd.at[k], r.kd_st.at[buf], r.kd_sem.at[buf])

    def ds_copy(k, buf, o):
        return pltpu.make_async_remote_copy(
            r.ds_st.at[buf, me ^ o], r.dk_r.at[me, k], r.dk_send.at[buf, o], r.dk_recv.at[o],
            device_id=(me ^ o, rep), device_id_type=MESH)

    kd_load(0, 0).start()
    groups = 4
    sc = hd ** (-0.5)
    plan = (((jc, 0),), (), ((ja, 1), (jd, 1), (jb, 1)), ((jc, 1),), ((ja, 2), (jb, 2), (jd, 2)), ((jc, 2), (ja, 3), (jb, 3)),
            ((jd, 3), (jc, 3), (ja, 4), (jb, 4)), ((jd, 4), (jc, 4), (ja, 5), (jb, 5)))

    def act(some):
        for job, i in some:
            job.move(i)

    def attend(k, _):
        buf = lax.rem(k, 2)

        @pl.when(k + 1 < members)
        def _():
            kd_load(k + 1, 1 - buf).start()

        for i, some in enumerate(plan):
            pl.when(k == i)(lambda some=some: act(some))
        kd_load(k, buf).wait()
        kvd = r.kd_st[buf]
        kd, vd = kvd[:, :hd], kvd[:, hd:]
        put = r.put[k]
        qp = dot_nn(put, q_v[...]).astype(bf16)
        dop = dot_nn(put, do_v[...]).astype(bf16)
        info = r.info[k]
        n = heads // groups
        dqs = []
        dk = jnp.zeros((length, hd), f32)
        dv = jnp.zeros((length, hd), f32)
        for h in range(groups):
            at = slice(h * n * hd, (h + 1) * n * hd)
            qr, dor = to_rows(qp[:, at], n), to_rows(dop[:, at], n)
            p = softmax_rows(qr, kd, info, n)
            dp = dot_nt(dor, vd)
            ds = (p * (dp - jnp.sum(dp * p, axis=1, keepdims=True))).astype(bf16)
            dqs.append(to_cols((dot_nn(ds, kd) * sc).astype(bf16), n))
            dk = dk + dot_tn(ds, qr)
            dv = dv + dot_tn(p.astype(bf16), dor)
        dq[...] += dot_tn(put, jnp.concatenate(dqs, axis=1))
        dkv = jnp.concatenate([dk * sc, dv], axis=1).astype(bf16)
        slots = dot_nn(key_onehot(r.slot[k], z.slots), dkv).astype(bf16).reshape(members, cap, w)

        @pl.when(k >= 2)
        def _():
            for o in range(1, members):
                ds_copy(k, buf, o).wait_send()

        r.ds_st[buf] = slots
        r.dk_r[me, k] = r.ds_st[buf, me]
        for o in range(1, members):
            ds_copy(k, buf, o).start()
        return 0

    lax.fori_loop(0, members, attend, 0)

    following = {ja: 6, jb: 6, jc: 5, jd: 5, je: 0, jf: 0, jg: 0}

    def go(*jobs):
        for job in jobs:
            if following[job] < job.count:
                job.move(following[job])
                following[job] += 1

    go(ja, jb)
    q_v[...] = dq[...].astype(bf16)
    e0 = (scale_lora * dot_nt(q_v[...], r.q_up[...]) * mask(0)).astype(bf16)
    load_a.wait()
    terms(je, 0, e0, t1[...], 1.0)
    je.start(0)
    terms(jf, 0, r.low0[...], q_v[...], scale_lora)
    jf.start(0)
    for o in range(1, members):
        local(r.dk_r.at[me ^ o], r.dk_r.at[me ^ o], r.dk_recv.at[o]).wait()
    go(jd, jc)
    dkv = jnp.zeros((length, w), f32)
    for k in range(members):
        total = r.dk_r[0, k].astype(f32)
        for s in range(1, members):
            total = total + r.dk_r[s, k].astype(f32)
        dkv = dkv + dot_tn(r.put[k], total.astype(bf16))
    dkv = dkv.astype(bf16)
    go(je, jf)
    e1 = (scale_lora * dot_nt(dkv, r.kv_up[...]) * mask(1)).astype(bf16)
    terms(jg, 0, e1, t1[...], 1.0)
    terms(jg, per, r.low1[...], dkv, scale_lora)
    jg.start(0)
    load_k.wait()
    dq[...] = (dot_nn(e0, r.q_dn[...]) + dot_nn(e1, r.kv_dn[...])
               + dot_nt(dkv, r.wk_v[...].reshape(d, w)))
    go(jd, jc, je, jf, jg)
    for cp in query:
        cp.wait()
    for c in range(halves):
        dq[...] += dot_nt(q_v[:, c * fc : (c + 1) * fc], w_v[c].reshape(d, fc))
        go(je, jf, jg)
    load_x.wait()
    gain = r.gain[...]

    def back(i, _):
        at = pl.ds(pl.multiple_of(i * 128, 128), 128)
        n, inv = norm_parts(t2[at, :].astype(f32))
        do_v[at, :] = (dres[at, :] + norm_back(n, inv, gain, dq[at, :])).astype(bf16)
        return 0

    for part in range(2):
        lax.fori_loop(part * length // 256, (part + 1) * length // 256, back, 0)
        go(je, jf, jg)
    out = local(do_v, r.dx, r.out_sem)
    out.start()
    while any(following[job] < job.count for job in following):
        go(ja, jb, jc, jd, je, jf, jg)
    out.wait()
    for buf in range(2):
        for o in range(1, members):
            ds_copy(buf, buf, o).wait_send()


def backward(z, args):
    vm = pl.BlockSpec(memory_space=pltpu.VMEM)
    hbm = pl.BlockSpec(memory_space=pl.ANY)
    m, n, d, rk, w = z.members, z.length, z.d, z.rk, z.w
    s = jax.ShapeDtypeStruct
    dma = pltpu.SemaphoreType.DMA
    shapes = job_shapes(z)
    legs = m - 1 + 2
    sems = m - 1 + 2 * (z.replicas.bit_length() - 1)
    scratch = dict(
        w_v=pltpu.VMEM((d // z.fc, m, z.rows, z.fc), bf16), wk_v=pltpu.VMEM((m, z.rows, w), bf16),
        t1=pltpu.VMEM((n, d), bf16), t2=pltpu.VMEM((n, d), bf16), q_v=pltpu.VMEM((n, d), bf16), do_v=pltpu.VMEM((n, d), bf16),
        dq=pltpu.VMEM((n, d), f32), kd_st=pltpu.VMEM((2, n, w), bf16), ds_st=pltpu.VMEM((2, m, z.cap, w), bf16),
        dk_r=pltpu.VMEM((m, m, z.cap, w), bf16),
        w_sem=dma((2, d // z.fc)), t_sem=dma((4,)), g_sem=dma((2,)), kd_sem=dma((2,)), dk_send=dma((2, m)),
        dk_recv=dma((m,)), out_sem=dma(()))
    scratch = [scratch[k] for k in BwdScratch._fields[: len(scratch)]]
    job_outs = [s((rk, blocks * lanes), f32) for blocks, lanes in shapes]
    job_scratch = [x for blocks, lanes in shapes for x in (
        pltpu.VMEM((m, blocks, rk, lanes), bf16), pltpu.VMEM((legs, blocks, rk, lanes), bf16), dma((sems,)), dma((sems,)))]
    first_hbm = 17
    got = pl.pallas_call(
        lambda *refs: bwd_kernel(z, *refs),
        in_specs=[vm] * first_hbm + [hbm] * (len(BwdIn._fields) - first_hbm),
        out_specs=[hbm] + [vm] * len(shapes),
        out_shape=[s((n, d), bf16)] + job_outs,
        scratch_shapes=scratch + job_scratch,
        compiler_params=pltpu.CompilerParams(
            vmem_limit_bytes=FWD_VMEM, collective_id=2, has_side_effects=True),
    )(*BwdIn(**args))
    return BwdOut(*got)


def final(sums, z, experts, rank):
    c, n = z.rows, z.w // z.members
    ff = z.ff // z.members
    cuts = ((4, 0, c), (5, 0, c), (6, 0, c), (6, c, n), (2, c, c), (3, c, c), (2, 0, c), (0, 0, ff), (1, 0, ff), (3, 0, c))

    def kernel(*refs):
        for (job, at, width), out in zip(cuts, refs[len(sums):]):
            out[...] = refs[job][:, at : at + width].reshape(experts, rank, width)

    vm = pl.BlockSpec(memory_space=pltpu.VMEM)
    return pl.pallas_call(
        kernel, in_specs=[vm] * len(sums), out_specs=[vm] * len(cuts),
        out_shape=[jax.ShapeDtypeStruct((experts, rank, w), f32) for _, _, w in cuts])(*sums)


def local(tokens, out_grad, token_perm, seq_lens, adapter_ids,
          attn_g, attn_b, wq, bq, wkv, bv, wmix, bmix, mlp_g, mlp_b, wexp, bexp, wred, bred,
          q_dn, q_up, kv_dn, kv_up, mix_dn, mix_up, exp_dn, exp_up, red_dn, red_up):
    members = lax.axis_size("shard")
    replicas = lax.axis_size("rep")
    rep = lax.axis_index("rep")
    length, d = tokens.shape
    experts, rank = q_dn.shape[:2]
    rk = experts * rank
    z = Sizes(members, replicas, length, d, wexp.shape[1], bv.shape[0] * members, rk, rank,
              seq_lens.shape[1], adapter_ids.shape[2])
    flat = lambda s: s.reshape(rk, s.shape[2])
    q_dn, q_up, kv_dn, kv_up, mix_dn, mix_up, exp_dn, exp_up, red_dn, red_up = map(
        flat, (q_dn, q_up, kv_dn, kv_up, mix_dn, mix_up, exp_dn, exp_up, red_dn, red_up))
    group = lax.dynamic_index_in_dim(
        token_perm.reshape(members, replicas, length), rep, 1, keepdims=False)

    small = jnp.concatenate(
        [v.astype(f32) for v in (attn_g, attn_b, bq, bmix, mlp_g, mlp_b, bred, bexp, bv, seq_lens[0], adapter_ids.reshape(-1))]
        + [jnp.zeros((z.small_cols - z.ids_at - seq_lens.shape[1] * adapter_ids.shape[2],), f32)])[None]
    by_chunk = lambda s: s.reshape(s.shape[0], members, SLOTS, z.sub).transpose(2, 0, 1, 3).reshape(
        SLOTS, s.shape[0], z.fc)
    chunked = (lambda s: s) if z.aligned else by_chunk
    got = forward(z, FwdIn(
        x=tokens, dy=out_grad, small=small, group=group,
        q_dn=q_dn, q_up=q_up, kv_dn=kv_dn, kv_up=kv_up, mix_dn=mix_dn, mix_up=mix_up, exp_dn=exp_dn,
        exp_up=chunked(exp_up), red_dn=chunked(red_dn), red_up=red_up,
        wq=wq, wkv=wkv, wmix=wmix, wexp=chunked(wexp), wred=wred.reshape(SLOTS, z.sub, d)))
    gup, gdn = got.gup, got.gdn
    if not z.aligned:
        pack = 128 // z.sub
        gup, gdn = (g.reshape(members, SLOTS // pack, pack, rk, z.sub).transpose(0, 1, 3, 2, 4).reshape(
            members, SLOTS // pack, rk, 128) for g in (gup, gdn))
    back = backward(z, dict(
        dres=got.dres, put=got.put, slot=got.slot, info=got.info, chosen=got.chosen, low0=got.low0, low1=got.low1,
        low2=got.low2, low4=got.low4, e3=got.e3, gain=got.gain, ga=got.ga, gb=got.gb, gk=got.gk, q=got.q, a=got.a,
        o=got.o, m=got.m, kd=got.kd, gup=gup, gdn=gdn,
        mix_dn=mix_dn, mix_up=mix_up, q_dn=q_dn, q_up=q_up, kv_dn=kv_dn, kv_up=kv_up, dy=out_grad, x=tokens))
    g = final(back[1:], z, experts, rank)
    return (got.layer, back.dx, *g)


def solution(mesh):
    both = ("shard", "rep")
    row, vec = P("shard", None), P("shard")
    in_specs = (
        P(both, None), P(both, None), P(), P(both, None), P(both, None, None),
        vec, vec, row, vec, row, vec, row, vec, vec, vec, row, vec, row, vec,
    ) + (P(),) * 10
    out_specs = (P(both, None), P(both, None)) + (P(None, None, "shard"),) * 10
    return jax.shard_map(local, mesh=mesh, in_specs=in_specs, out_specs=out_specs, check_vma=False)
```

```python
import jax
import jax.numpy as jnp
from jax import lax
from jax.experimental import pallas as pl
from jax.experimental.pallas import tpu as pltpu
from jax.sharding import PartitionSpec as P
from typing import NamedTuple

scale_lora = 0.5
eps = 1e-05
f32 = jnp.float32
bf16 = jnp.bfloat16
neg_big = -1e30
log2_e = 1.4426950408889634
gelu_c = 0.7978845608028654
VMEM_LIMIT = 60 * 1024 * 1024


def dot_nn(a, b):
    return lax.dot_general(a, b, (((1,), (0,)), ((), ())), preferred_element_type=f32)


def dot_nt(a, b):
    return lax.dot_general(a, b, (((1,), (1,)), ((), ())), preferred_element_type=f32)


def dot_tn(a, b):
    return lax.dot_general(a, b, (((0,), (0,)), ((), ())), preferred_element_type=f32)


def key_onehot(slot_row, slots):
    ids = lax.broadcasted_iota(jnp.int32, (slots, slot_row.shape[1]), 0)
    return jnp.where(ids == slot_row, 1.0, 0.0).astype(bf16)


def to_rows(x, heads):
    hd = x.shape[1] // heads
    return jnp.concatenate([x[:, h * hd : (h + 1) * hd] for h in range(heads)], axis=0)


def to_cols(x, heads):
    c = x.shape[0] // heads
    return jnp.concatenate([x[h * c : (h + 1) * c] for h in range(heads)], axis=1)


def softmax_rows(qr, kd, span, heads):
    rows, keys = qr.shape[0], kd.shape[0]
    c = rows // heads
    u = lax.broadcasted_iota(jnp.int32, (c, keys), 1).astype(f32)
    allowed = (u >= span[:, 0:1]) & (u <= span[:, 1:2])
    s = jnp.where(allowed[None], dot_nt(qr, kd).reshape(heads, c, keys), neg_big)
    top = jnp.max(s, axis=2, keepdims=True)
    e = jnp.exp2((s - top) * (kd.shape[1] ** (-0.5) * log2_e))
    p = e * (1.0 / jnp.sum(e, axis=2, keepdims=True))
    return p.reshape(rows, keys)


MESH = pl.DeviceIdType.MESH


class Gather:
    def __init__(self, members, own, full, slots, send_sem, recv_sem):
        self.members = members
        self.me, self.rep = lax.axis_index("shard"), lax.axis_index("rep")
        self.own, self.full = own, full
        self.base = [sum(slots[:i]) for i in range(len(slots))]
        self.send_sem, self.recv_sem = send_sem, recv_sem
        self.bits = [1 << i for i in range(1, members.bit_length() - 1)]
        self.planes = list(range(0, members, 2))
        self.sent = {}

    def place(self, kind, slot, offset):
        return self.full[kind].at[slot, self.me ^ offset]

    def copy(self, kind, slot, offset, there, to, to_slot):
        mine = self.sent.setdefault((kind, slot), {})
        at = mine.setdefault((offset, there, to_slot), len(mine))
        src = self.own[kind](slot) if offset == 0 else self.place(kind, slot, offset)
        pltpu.make_async_remote_copy(
            src, self.full[kind].at[to_slot, self.me ^ offset],
            self.send_sem.at[self.base[kind] + slot, at],
            self.recv_sem.at[self.base[kind] + to_slot, there],
            device_id=to, device_id_type=MESH).start()

    def wait(self, kind, slot, offset):
        piece = self.place(kind, slot, offset)
        pltpu.make_async_copy(piece, piece, self.recv_sem.at[self.base[kind] + slot, offset]).wait()

    def order(self, kind):
        return self.bits if kind % 2 == 0 else self.bits[::-1]

    def stage(self, kind, offset):
        return max(i for i, b in enumerate(self.order(kind)) if offset & b)

    def issue(self, slot, kinds, plane=True):
        for kind in kinds:
            if plane:
                for b in self.order(kind):
                    self.copy(kind, slot, 0, b, (self.me ^ b, self.rep), slot)
            self.copy(kind, slot, 0, 1, (self.me ^ 1, self.rep), slot)

    def arrive(self, slot, kinds, direct, swap_to=None):
        for kind in kinds:
            order = self.order(kind)
            some = [o for o in self.planes if o and (bin(o).count("1") == 1) == direct]
            some.sort(key=lambda o: self.stage(kind, o))
            for o in some:
                self.wait(kind, slot, o)
                for i in range(self.stage(kind, o) + 1, len(order)):
                    self.copy(kind, slot, o, o ^ order[i], (self.me ^ order[i], self.rep), slot)
                if swap_to is not None:
                    self.copy(kind, slot, o, o, (self.me, self.rep ^ 1), swap_to)
                self.copy(kind, slot, o, o ^ 1, (self.me ^ 1, self.rep), slot)

    def swapped(self, slot, kinds):
        for kind in kinds:
            for o in self.planes[1:]:
                self.wait(kind, slot, o)
                self.copy(kind, slot, o, o ^ 1, (self.me ^ 1, self.rep), slot)

    def ready(self, slot, kinds):
        for kind in kinds:
            for o in range(1, self.members, 2):
                self.wait(kind, slot, o)

    def finish(self):
        for (kind, slot), mine in self.sent.items():
            piece = self.place(kind, slot, 0)
            for at in mine.values():
                pltpu.make_async_copy(piece, piece, self.send_sem.at[self.base[kind] + slot, at]).wait()


U, V, C = (0, 1, 2), (3, 4, 5), (6, 7)
SLOTS = 8
WE, WR, AT, AB, KV = range(5)
BOTH, HALVES = (WE, WR), (AT, AB)
WQ, WMIX = 0, 1
SEND, NEAR, FAR, SWAP = range(4)
MLP_ORDER = (0, 1, 4, 3, 2, 6, 5, 7)
SERVE = {
    0: ((SEND, KV, 0),),
    1: ((SEND, WR, 0),),
    10: ((NEAR, KV, 0),),
    21: ((SEND, WE, 0),),
    24: ((NEAR, WR, 0),),
    25: ((FAR, KV, 0),),
    2: ((SEND, AT, 0),),
    4: ((NEAR, WE, 0),),
    5: ((FAR, WR, 0), (NEAR, AT, 0), (SEND, AB, 0), (FAR, WE, 0), (SEND, WE, 1), (SWAP, WR, 3), (FAR, AT, 0), (SEND, AB, 1), (SWAP, WE, 3), (NEAR, AB, 0), (NEAR, WE, 1), (SEND, AT, 1), (FAR, AB, 0),),
    15: ((NEAR, AB, 1),),
    41: ((FAR, WE, 1), (SEND, WR, 1),),
    43: ((FAR, AB, 1),),
    44: ((NEAR, AT, 1), (SEND, WE, 2), (SWAP, WE, 4),),
    46: ((NEAR, WR, 1),),
    7: ((FAR, AT, 1),),
    16: ((SEND, WR, 2),),
    17: ((FAR, WR, 1),),
    12: ((NEAR, WE, 2),),
    13: ((SEND, WR, 6),),
    60: ((NEAR, WR, 2),),
    61: ((SWAP, WR, 4),),
    62: ((FAR, WE, 2), (SEND, WE, 6),),
    63: ((FAR, WR, 2),),
    64: ((NEAR, WR, 6), (SEND, WE, 7),),
    66: ((NEAR, WE, 6),),
    67: ((FAR, WR, 6), (SEND, WR, 7),),
    69: ((NEAR, WE, 7), (FAR, WE, 6), (SWAP, WE, 5),),
    70: ((NEAR, WR, 7), (SWAP, WR, 5),),
    72: ((FAR, WE, 7), (FAR, WR, 7),),
}


def chunk_of(slot, parity):
    slot = jnp.int32(slot)
    low = jnp.where(slot < 3, slot, slot + 2)
    high = jnp.where(slot < 3, slot + 5, slot - 3)
    return jnp.where(slot >= 6, slot - 3, jnp.where(parity == 0, low, high))


def norm_parts(v):
    center = v - jnp.mean(v, axis=-1, keepdims=True)
    inv = lax.rsqrt(jnp.mean(center * center, axis=-1, keepdims=True) + eps)
    return center * inv, inv


def norm_back(n, inv, gain, dn):
    w = gain * dn
    return (w - jnp.mean(w, axis=-1, keepdims=True)
            - n * jnp.mean(w * n, axis=-1, keepdims=True)) * inv


class Sizes:
    def __init__(self, members, replicas, length, d, ff, hd, rk, rank, seqs, projs):
        self.members, self.replicas, self.length, self.d, self.ff = members, replicas, length, d, ff
        self.hd, self.rk, self.rank, self.seqs, self.projs = hd, rk, rank, seqs, projs
        self.heads = d // hd
        self.cap = 3 * length // (2 * members)
        self.slots = members * self.cap
        self.w = 2 * hd
        self.rows = d // members
        self.sub = ff // members // SLOTS
        self.fc = self.sub * members
        self.aligned = self.sub % 128 == 0
        self.be_at = 7 * self.rows
        self.vb_at = self.be_at + ff // members
        self.len_at = self.vb_at + 128
        self.ids_at = self.len_at + 128
        self.small_cols = self.ids_at + 128


class FwdIn(NamedTuple):
    x: object
    attn_g: object
    attn_b: object
    bq: object
    bmix: object
    mlp_g: object
    mlp_b: object
    bred: object
    bexp: object
    bv: object
    lens: object
    ids: object
    group: object
    q_dn: object
    q_up: object
    kv_dn: object
    kv_up: object
    dy: object
    mix_dn: object
    mix_up: object
    exp_dn: object
    exp_up: object
    red_dn: object
    red_up: object
    wq: object
    wkv: object
    wmix: object
    wexp: object
    wred: object


class FwdOut(NamedTuple):
    dres: object
    put: object
    slot: object
    info: object
    chosen: object
    low0: object
    low1: object
    low2: object
    low4: object
    e3: object
    gain: object
    a: object
    q: object
    o: object
    m: object
    resid: object
    kd: object
    gup: object
    gdn: object
    layer: object
    kvs: object
    ge: object
    gr: object
    ga: object
    gb: object
    gk: object


class FwdScratch(NamedTuple):
    y: object
    dy_v: object
    mix_dn_v: object
    mix_up_v: object
    exp_dn_v: object
    exp_up_v: object
    red_dn_v: object
    red_up_v: object
    late_sem: object
    we_v: object
    wr_v: object
    a_v: object
    q_v: object
    kvp: object
    kvb: object
    kd_st: object
    gup_st: object
    gdn_st: object
    sm: object
    lowr: object
    er: object
    low3: object
    e4: object
    send_sem: object
    recv_sem: object
    sm_send: object
    sm_recv: object
    kv_send: object
    kv_recv: object
    stage_sem: object
    store_sem: object
    load_sem: object
    kvb_sem: object
    kd_sem: object
    g_sem: object
    out_sem: object


class FwdRefs(NamedTuple):
    x: object
    attn_g: object
    attn_b: object
    bq: object
    bmix: object
    mlp_g: object
    mlp_b: object
    bred: object
    bexp: object
    bv: object
    lens: object
    ids: object
    group: object
    q_dn: object
    q_up: object
    kv_dn: object
    kv_up: object
    dy: object
    mix_dn: object
    mix_up: object
    exp_dn: object
    exp_up: object
    red_dn: object
    red_up: object
    wq: object
    wkv: object
    wmix: object
    wexp: object
    wred: object
    dres: object
    put: object
    slot: object
    info: object
    chosen: object
    low0: object
    low1: object
    low2: object
    low4: object
    e3: object
    gain: object
    a: object
    q: object
    o: object
    m: object
    resid: object
    kd: object
    gup: object
    gdn: object
    layer: object
    kvs: object
    ge: object
    gr: object
    ga: object
    gb: object
    gk: object
    y: object
    dy_v: object
    mix_dn_v: object
    mix_up_v: object
    exp_dn_v: object
    exp_up_v: object
    red_dn_v: object
    red_up_v: object
    late_sem: object
    we_v: object
    wr_v: object
    a_v: object
    q_v: object
    kvp: object
    kvb: object
    kd_st: object
    gup_st: object
    gdn_st: object
    sm: object
    lowr: object
    er: object
    low3: object
    e4: object
    send_sem: object
    recv_sem: object
    sm_send: object
    sm_recv: object
    kv_send: object
    kv_recv: object
    stage_sem: object
    store_sem: object
    load_sem: object
    kvb_sem: object
    kd_sem: object
    g_sem: object
    out_sem: object


def fwd_kernel(z, *refs):
    r = FwdRefs(*refs)
    members, rows, fc, sub, d, hd = z.members, z.rows, z.fc, z.sub, z.d, z.hd
    length, cap, w, heads, rk = z.length, z.cap, z.w, z.heads, z.rk
    me, rep = lax.axis_index("shard"), lax.axis_index("rep")
    parity = lax.rem(rep, 2)
    half = rows // 2
    att = (r.wq, r.wmix)
    g = Gather(
        members,
        [lambda s: r.ge.at[s, me],
         lambda s: r.wred.at[chunk_of(s, parity)],
         lambda s: att[s].at[0:half],
         lambda s: att[s].at[half:rows],
         lambda s: r.wkv],
        [r.ge, r.gr, r.ga, r.gb, r.gk],
        [SLOTS, SLOTS, 2, 2, 1], r.send_sem, r.recv_sem)
    we_v, wr_v, sm, y, dm = r.we_v, r.wr_v, r.sm, r.y, r.dres

    def serve(point):
        for op, kind, slot in SERVE.get(point, ()):
            swap_to = slot + 3 if slot in U and kind in BOTH else None
            if op == SEND:
                g.issue(slot, (kind,))
            elif op == SWAP:
                g.swapped(slot, (kind,))
            else:
                g.arrive(slot, (kind,), op == NEAR, swap_to)

    barrier = pltpu.get_barrier_semaphore()
    others = [(me ^ o, rep) for o in range(1, members)] + [(me, rep ^ 1)]
    for to in others:
        pl.semaphore_signal(barrier, inc=1, device_id=to, device_id_type=MESH)

    def stage_copies(slot):
        j = chunk_of(slot, parity)
        to = we_v.at[0, slot]
        if not z.aligned:
            return [pltpu.make_async_copy(r.wexp.at[j], to, r.stage_sem.at[slot])]
        return [pltpu.make_async_copy(
            r.wexp.at[:, pl.ds(pl.multiple_of(s * (z.ff // members) + j * sub, sub), sub)],
            to.at[:, s * sub : (s + 1) * sub], r.stage_sem.at[slot]) for s in range(members)]

    def stored(slot):
        return pltpu.make_async_copy(we_v.at[0, slot], r.ge.at[slot, me], r.store_sem.at[slot])

    def staged(slot):
        pltpu.make_async_copy(we_v.at[0, slot], we_v.at[0, slot], r.stage_sem.at[slot]).wait()
        stored(slot).start()

    for slot in range(SLOTS):
        for cp in stage_copies(slot):
            cp.start()
    pl.semaphore_wait(barrier, len(others))

    def small_copy(o):
        return pltpu.make_async_remote_copy(
            sm.at[me], sm.at[me], r.sm_send.at[o], r.sm_recv.at[o],
            device_id=(me ^ o, rep), device_id_type=MESH)

    serve(0)
    coming = [pltpu.make_async_copy(src, dst, r.late_sem.at[i]) for i, (src, dst) in enumerate((
        (r.mix_dn, r.mix_dn_v), (r.mix_up, r.mix_up_v), (r.dy, r.dy_v), (r.exp_dn, r.exp_dn_v),
        (r.exp_up, r.exp_up_v), (r.red_dn, r.red_dn_v), (r.red_up, r.red_up_v)))]
    for cp in coming:
        cp.start()
    r = r._replace(dy=r.dy_v, mix_dn=r.mix_dn_v, mix_up=r.mix_up_v, exp_dn=r.exp_dn_v, exp_up=r.exp_up_v,
                   red_dn=r.red_dn_v, red_up=r.red_up_v)
    sm[me] = jnp.zeros((1, z.small_cols), f32)
    for i, v in enumerate((r.attn_g, r.attn_b, r.bq, r.bmix, r.mlp_g, r.mlp_b, r.bred)):
        sm[me, :, i * rows : (i + 1) * rows] = v[...].astype(f32).reshape(1, rows)
    sm[me, :, z.be_at : z.vb_at] = r.bexp[...].astype(f32).reshape(1, z.vb_at - z.be_at)
    sm[me, :, z.vb_at : z.vb_at + hd // members] = r.bv[...].astype(f32).reshape(1, hd // members)
    sm[me, :, z.len_at : z.len_at + z.seqs] = r.lens[...].astype(f32)
    sm[me, :, z.ids_at : z.ids_at + z.seqs * z.projs] = r.ids[...].astype(f32)
    for o in range(1, members):
        small_copy(o).start()
    for slot in range(SLOTS):
        staged(slot)
    for slot in range(SLOTS):
        stored(slot).wait()
    serve(1)
    for o in range(1, members):
        pltpu.make_async_copy(sm.at[me ^ o], sm.at[me ^ o], r.sm_recv.at[o]).wait()

    def vec(row):
        return jnp.concatenate([sm[s, :, row * rows : (row + 1) * rows] for s in range(members)], axis=1)

    def norm_rows(src, gain, bias, dst, part):
        gv, bv = vec(gain), vec(bias)

        def body(i, _):
            at = pl.ds(pl.multiple_of(i * 128, 128), 128)
            n, _inv = norm_parts(src[at, :].astype(f32))
            dst[at, :] = (n * gv + bv).astype(bf16)
            return 0

        lax.fori_loop(part * length // 256, (part + 1) * length // 256, body, 0)

    for part in range(2):
        serve(10 + part)
        norm_rows(r.x, 0, 1, r.a_v, part)

    r.gain[...] = vec(0)

    t_row = lax.broadcasted_iota(jnp.int32, (1, length), 1)
    before_t = lax.broadcasted_iota(jnp.int32, (length, length), 0) < lax.broadcasted_iota(
        jnp.int32, (length, length), 1)
    c_ids = lax.broadcasted_iota(jnp.int32, (cap, length), 0)
    lane = lax.broadcasted_iota(jnp.int32, (cap, 128), 1)
    span = length * z.replicas
    first = (me * z.replicas + rep) * length
    tf = t_row.astype(f32)
    src_cols = lax.div(r.group[...], span).astype(f32).T
    chosen = jnp.zeros((length, 128), f32)
    for k in range(members):
        serve(20 + k)
        row = r.group[k : k + 1, :]
        src = lax.div(row, span)
        earlier = jnp.where((src_cols[:, k : k + 1] == src.astype(f32)) & before_t, 1.0, 0.0)
        slot_row = src * cap + jnp.sum(earlier, axis=0, keepdims=True).astype(jnp.int32)
        r.slot[k] = slot_row
        hit = slot_row == c_ids + me * cap

        def pick(values):
            return jnp.sum(jnp.where(hit, values, 0.0), axis=1, keepdims=True)

        full = pick(jnp.ones_like(tf))
        tok = pick((row - first + 1).astype(f32)) - 1.0
        put = jnp.where(tok == tf, 1.0, 0.0).astype(bf16)
        r.put[k] = put
        end = jnp.zeros((1, 1), f32)
        start = jnp.zeros_like(tf)
        ids = [jnp.zeros_like(tf) for _ in range(z.projs)]
        for j in range(z.seqs):
            n = sm[k, :, z.len_at + j : z.len_at + j + 1]
            inside = (tf >= end) & (tf < end + n)
            end = end + n
            start = start + jnp.where(tf >= end, n, 0.0)
            for p in range(z.projs):
                at = z.ids_at + j * z.projs + p
                ids[p] = ids[p] + jnp.where(inside, sm[k, :, at : at + 1], 0.0)
        info = jnp.where(lane == 0, pick(start) + (1.0 - full), 0.0)
        info = jnp.where(lane == 1, pick(tf), info)
        for p in range(z.projs):
            info = jnp.where(lane == 2 + p, pick(ids[p]), info)
        r.info[k] = info
        chosen = chosen + dot_tn(put, info.astype(bf16))
    r.chosen[...] = chosen
    rank_of = lax.broadcasted_iota(jnp.int32, (length, rk), 1) // z.rank

    def mask(p):
        return jnp.where(rank_of.astype(f32) == r.chosen[:, 2 + p : 3 + p], 1.0, 0.0)

    a_v, q_v = r.a_v, r.q_v
    o_v = q_v
    serve(2)
    r.low0[...] = (dot_nt(a_v[...], r.q_dn[...]) * mask(0)).astype(bf16)
    r.low1[...] = (dot_nt(a_v[...], r.kv_dn[...]) * mask(1)).astype(bf16)
    out_a = pltpu.make_async_copy(a_v, r.a, r.out_sem.at[0])
    out_a.start()

    serve(3)
    g.ready(0, (KV,))
    kv_loads = [pltpu.make_async_copy(
        r.wkv if o == 0 else g.place(KV, 0, o), we_v.at[1, me ^ o, :, 0:w], r.kv_send.at[o]) for o in range(members)]
    for cp in kv_loads:
        cp.start()
    for cp in kv_loads:
        cp.wait()
    back_kv = pltpu.make_async_copy(we_v.at[1, me, :, 0:w], g.place(KV, 0, 0), r.kv_send.at[0])
    back_kv.start()
    vb = jnp.concatenate([sm[s, :, z.vb_at : z.vb_at + hd // members] for s in range(members)], axis=1)
    kv_bias = jnp.concatenate([jnp.zeros((1, hd), f32), vb], axis=1)
    kv = (dot_nn(a_v[...], we_v[1, :, :, 0:w].reshape(d, w)) + kv_bias
          + scale_lora * dot_nn(r.low1[...], r.kv_up[...])).astype(bf16)
    for k in range(members):
        r.kvp[k] = dot_nn(r.put[k], kv).astype(bf16)

    def kv_copy(o):
        return pltpu.make_async_remote_copy(
            r.kvp, r.kvs.at[me], r.kv_send.at[o], r.kv_recv.at[o],
            device_id=(me ^ o, rep), device_id_type=MESH)

    back_kv.wait()
    own_kv = pltpu.make_async_copy(r.kvp, r.kvs.at[me], r.kv_send.at[0])
    for o in range(1, members):
        kv_copy(o).start()
    own_kv.start()

    for slot in V:
        g.issue(slot, BOTH, False)
    serve(4)

    def wide_load(which):
        g.ready(which, HALVES)
        out = []
        for kind in HALVES:
            for o in range(members):
                src = g.own[kind](which) if o == 0 else g.place(kind, which, o)
                for c in range(d // fc):
                    out.append(pltpu.make_async_copy(
                        src.at[:, c * fc : (c + 1) * fc],
                        we_v.at[c, me ^ o, (kind - AT) * half : (kind - AT + 1) * half],
                        r.load_sem.at[kind - AT, c, o]))
        for cp in out:
            cp.start()
        for cp in out:
            cp.wait()
        back = [pltpu.make_async_copy(
            we_v.at[c, me, (kind - AT) * half : (kind - AT + 1) * half],
            g.place(kind, which, 0).at[:, c * fc : (c + 1) * fc],
            r.load_sem.at[kind - AT, c, 0]) for kind in HALVES for c in range(d // fc)]
        for cp in back:
            cp.start()
        return back

    serve(5)
    back_q = wide_load(WQ)
    q_bias = vec(2)
    for c in range(d // fc):
        serve(14 + c)
        at = slice(c * fc, (c + 1) * fc)
        q_v[:, at] = (dot_nn(a_v[...], we_v[c].reshape(d, fc)) + q_bias[:, at]
                      + scale_lora * dot_nn(r.low0[...], r.q_up[:, at])).astype(bf16)
    out_q = pltpu.make_async_copy(q_v, r.q, r.out_sem.at[1])
    out_q.start()

    for cp in back_q:
        cp.wait()

    serve(6)

    for o in range(1, members):
        pltpu.make_async_copy(r.kvs.at[me ^ o], r.kvs.at[me ^ o], r.kv_recv.at[o]).wait()
    own_kv.wait()
    for cp in coming:
        cp.wait()
    dm[...] = jnp.zeros_like(dm)

    def kvb_load(k, buf):
        return pltpu.make_async_copy(r.kvs.at[:, k], r.kvb.at[buf], r.kvb_sem.at[buf])

    def kd_out(k, buf):
        return pltpu.make_async_copy(r.kd_st.at[buf], r.kd.at[k], r.kd_sem.at[buf])

    kvb_load(0, 0).start()
    groups = 2

    def attend(k, _):
        buf = lax.rem(k, 2)

        @pl.when(k + 1 < members)
        def _():
            kvb_load(k + 1, 1 - buf).start()

        for i in range(min(members, 16)):
            if 40 + i in SERVE:
                pl.when(k == i)(lambda i=i: serve(40 + i))
        kvb_load(k, buf).wait()
        oh = key_onehot(r.slot[k], z.slots)
        kvd = dot_tn(oh, r.kvb[buf].reshape(z.slots, w)).astype(bf16)

        @pl.when(k >= 2)
        def _():
            kd_out(k, buf).wait()

        r.kd_st[buf] = kvd
        kd_out(k, buf).start()
        put = r.put[k]
        qp = dot_nn(put, q_v[...]).astype(bf16)
        info = r.info[k]
        outs = []
        per = heads // groups
        for h in range(groups):
            qr = to_rows(qp[:, h * per * hd : (h + 1) * per * hd], per)
            p = softmax_rows(qr, kvd[:, :hd], info, per).astype(bf16)
            outs.append(to_cols(dot_nn(p, kvd[:, hd:]).astype(bf16), per))
        dm[...] += dot_tn(put, jnp.concatenate(outs, axis=1))
        return 0

    lax.fori_loop(0, members, attend, 0)
    out_q.wait()
    o_v[...] = dm[...].astype(bf16)
    out_o = pltpu.make_async_copy(o_v, r.o, r.out_sem.at[2])
    out_o.start()
    r.low2[...] = (dot_nt(o_v[...], r.mix_dn[...]) * mask(2)).astype(bf16)
    serve(7)
    back_m = wide_load(WMIX)
    mix_bias = vec(3)
    for c in range(d // fc):
        serve(16 + c)
        at = slice(c * fc, (c + 1) * fc)
        y[:, at] = (r.x[:, at].astype(f32) + dot_nn(o_v[...], we_v[c].reshape(d, fc)) + mix_bias[:, at]
                    + scale_lora * dot_nn(r.low2[...], r.mix_up[:, at]))

    def load(slot, buf):
        out = [pltpu.make_async_copy(r.ge.at[slot], we_v.at[buf], r.load_sem.at[0, buf, 0])]
        for o in range(members):
            src = g.own[WR](slot) if o == 0 else g.place(WR, slot, o)
            out.append(pltpu.make_async_copy(src, wr_v.at[buf, me ^ o], r.load_sem.at[1, buf, o]))
        return out

    def fetch(slot, buf):
        g.ready(slot, BOTH)
        for cp in load(slot, buf):
            cp.start()

    for cp in back_m:
        cp.wait()
    out_r = pltpu.make_async_copy(y, r.resid, r.out_sem.at[3])
    out_r.start()
    out_a.wait()
    m_v = a_v
    for part in range(2):
        serve(12 + part)
        norm_rows(y, 4, 5, m_v, part)
    serve(8)
    out_m = pltpu.make_async_copy(m_v, r.m, r.out_sem.at[0])
    out_m.start()
    r.low3[...] = (dot_nt(m_v[...], r.exp_dn[...]) * mask(3)).astype(bf16)
    r.e4[...] = (scale_lora * dot_nt(r.dy[...], r.red_up[...]) * mask(4)).astype(bf16)
    dm[...] = jnp.zeros_like(dm)
    r.lowr[...] = jnp.zeros_like(r.lowr)
    r.er[...] = jnp.zeros_like(r.er)
    out_r.wait()
    y[...] += vec(6)

    def g_out(j, buf):
        return (pltpu.make_async_copy(r.gup_st.at[buf], r.gup.at[:, j], r.g_sem.at[0, buf]),
                pltpu.make_async_copy(r.gdn_st.at[buf], r.gdn.at[:, j], r.g_sem.at[1, buf]))

    serve(9)
    fetch(MLP_ORDER[0], 0)

    def step(n, _):
        for i in range(SLOTS):
            if 60 + 2 * i in SERVE:
                pl.when(n == i)(lambda i=i: serve(60 + 2 * i))
        buf = lax.rem(n, 2)
        slot = jnp.int32(0)
        for i, q in enumerate(MLP_ORDER):
            slot = jnp.where(n == i, q, slot)
        for cp in load(slot, buf):
            cp.wait()
        j = chunk_of(slot, parity)
        we = we_v[buf].reshape(d, fc)
        wr = wr_v[buf].reshape(fc, d)
        if z.aligned:
            def cut(ref):
                return jnp.concatenate([ref[:, pl.ds(pl.multiple_of(s * (z.ff // members) + j * sub, sub), sub)]
                                        for s in range(members)], axis=1)
            bup, adn = cut(r.exp_up), cut(r.red_dn)
        else:
            bup, adn = r.exp_up[j], r.red_dn[j]
        be = jnp.zeros((1, fc), f32)
        for i in range(SLOTS):
            lo = z.be_at + i * sub
            row = jnp.concatenate([sm[s, :, lo : lo + sub] for s in range(members)], axis=1)
            be = jnp.where(j == i, row, be)
        hid = dot_nn(m_v[...], we) + be
        hid = hid + scale_lora * dot_nn(r.low3[...], bup)
        cube = hid * hid * hid
        t = jnp.tanh(gelu_c * (hid + 0.044715 * cube))
        act = (0.5 * hid * (1.0 + t)).astype(bf16)
        slope = 0.5 * (1.0 + t) + 0.5 * hid * (1.0 - t * t) * (
            gelu_c * (1.0 + 3.0 * 0.044715 * hid * hid)
        )
        dact = dot_nt(r.dy[...], wr) + dot_nn(r.e4[...], adn)
        dh = (dact * slope).astype(bf16)
        for i in range(SLOTS):
            def middle(i=i):
                serve(61 + 2 * i)
                if i + 1 < SLOTS:
                    fetch(MLP_ORDER[i + 1], (i + 1) % 2)
            pl.when(n == i)(middle)
        y[...] += dot_nn(act, wr)
        dm[...] += dot_nt(dh, we)
        r.lowr[...] += dot_nt(act, adn)
        r.er[...] += dot_nt(dh, bup)
        gup = (scale_lora * dot_tn(r.low3[...], dh)).astype(bf16)
        gdn = dot_tn(r.e4[...], act).astype(bf16)

        @pl.when(n >= 2)
        def _():
            for cp in g_out(j, buf):
                cp.wait()

        for to in range(members):
            r.gup_st[buf, to] = gup[:, to * sub : (to + 1) * sub]
            r.gdn_st[buf, to] = gdn[:, to * sub : (to + 1) * sub]
        for cp in g_out(j, buf):
            cp.start()
        return 0

    lax.fori_loop(0, SLOTS, step, 0)

    low4 = (r.lowr[...] * mask(4)).astype(bf16)
    r.low4[...] = low4
    out_o.wait()
    layer_v = q_v
    for c in range(d // fc):
        at = slice(c * fc, (c + 1) * fc)
        layer_v[:, at] = (y[:, at] + scale_lora * dot_nn(low4, r.red_up[:, at])).astype(bf16)
    out_l = pltpu.make_async_copy(layer_v, r.layer, r.out_sem.at[1])
    out_l.start()
    back_r = pltpu.make_async_copy(r.resid, y, r.out_sem.at[3])
    back_r.start()
    e3 = (scale_lora * r.er[...] * mask(3)).astype(bf16)
    r.e3[...] = e3
    gain = vec(4)
    back_r.wait()

    def last(i, _):
        at = pl.ds(pl.multiple_of(i * 128, 128), 128)
        n, inv = norm_parts(y[at, :])
        dn = dm[at, :] + dot_nn(r.e3[at, :], r.exp_dn[...])
        dm[at, :] = r.dy[at, :].astype(f32) + norm_back(n, inv, gain, dn)
        return 0

    lax.fori_loop(0, length // 128, last, 0)
    out_l.wait()
    out_m.wait()
    for buf in range(2):
        kd_out(buf, buf).wait()
        for cp in g_out(buf, buf):
            cp.wait()
    for o in range(1, members):
        small_copy(o).wait_send()
        kv_copy(o).wait_send()
    g.finish()


def forward(z, args):
    vm = pl.BlockSpec(memory_space=pltpu.VMEM)
    hbm = pl.BlockSpec(memory_space=pl.ANY)
    m, n, d, rk, w = z.members, z.length, z.d, z.rk, z.w
    s = jax.ShapeDtypeStruct
    half = z.rows // 2
    outs = dict(
        dres=s((n, d), f32), put=s((m, z.cap, n), bf16), slot=s((m, 1, n), jnp.int32),
        info=s((m, z.cap, 128), f32), chosen=s((n, 128), f32),
        low0=s((n, rk), bf16), low1=s((n, rk), bf16), low2=s((n, rk), bf16), low4=s((n, rk), bf16), e3=s((n, rk), bf16), gain=s((1, d), f32),
        a=s((n, d), bf16), q=s((n, d), bf16), o=s((n, d), bf16), m=s((n, d), bf16), resid=s((n, d), f32),
        kd=s((m, n, w), bf16), gup=s((m, SLOTS, rk, z.sub), bf16), gdn=s((m, SLOTS, rk, z.sub), bf16),
        layer=s((n, d), bf16), kvs=s((m, m, z.cap, w), bf16),
        ge=s((SLOTS, m, z.rows, z.fc), bf16), gr=s((SLOTS, m, z.sub, d), bf16),
        ga=s((2, m, half, d), bf16), gb=s((2, m, half, d), bf16), gk=s((1, m, z.rows, w), bf16))
    in_vmem = 11
    sends = m - 1 + m // 2
    dma = pltpu.SemaphoreType.DMA
    items = 2 * SLOTS + 5
    scratch = dict(
        y=pltpu.VMEM((n, d), f32), dy_v=pltpu.VMEM((n, d), bf16), mix_dn_v=pltpu.VMEM((rk, d), bf16),
        mix_up_v=pltpu.VMEM((rk, d), bf16), exp_dn_v=pltpu.VMEM((rk, d), bf16),
        exp_up_v=pltpu.VMEM(args.exp_up.shape, bf16), red_dn_v=pltpu.VMEM(args.exp_up.shape, bf16),
        red_up_v=pltpu.VMEM((rk, d), bf16), late_sem=dma((7,)), we_v=pltpu.VMEM((2, m, z.rows, z.fc), bf16), wr_v=pltpu.VMEM((2, m, z.sub, d), bf16),
        a_v=pltpu.VMEM((n, d), bf16), q_v=pltpu.VMEM((n, d), bf16),
        kvp=pltpu.VMEM((m, z.cap, w), bf16), kvb=pltpu.VMEM((2, m, z.cap, w), bf16),
        kd_st=pltpu.VMEM((2, n, w), bf16), gup_st=pltpu.VMEM((2, m, rk, z.sub), bf16),
        gdn_st=pltpu.VMEM((2, m, rk, z.sub), bf16), sm=pltpu.VMEM((m, 1, z.small_cols), f32),
        lowr=pltpu.VMEM((n, rk), f32), er=pltpu.VMEM((n, rk), f32), low3=pltpu.VMEM((n, rk), bf16), e4=pltpu.VMEM((n, rk), bf16),
        send_sem=dma((items, sends)), recv_sem=dma((items, m)), sm_send=dma((m,)), sm_recv=dma((m,)),
        kv_send=dma((m,)), kv_recv=dma((m,)), stage_sem=dma((SLOTS,)), store_sem=dma((SLOTS,)),
        load_sem=dma((2, 2, m)), kvb_sem=dma((2,)), kd_sem=dma((2,)), g_sem=dma((2, 2)), out_sem=dma((4,)))
    got = pl.pallas_call(
        lambda *refs: fwd_kernel(z, *refs),
        in_specs=[vm] * 17 + [hbm] * 12,
        out_specs=[vm] * in_vmem + [hbm] * (len(FwdOut._fields) - in_vmem),
        out_shape=list(FwdOut(**outs)),
        scratch_shapes=list(FwdScratch(**scratch)),
        compiler_params=pltpu.CompilerParams(
            vmem_limit_bytes=FWD_VMEM, collective_id=1, has_side_effects=True),
    )(*args)
    return FwdOut(*got)


FWD_VMEM = 62 * 1024 * 1024


HALVE, PLANE, SCATTER, COLLECT = range(4)


class Job:
    def __init__(self, members, replicas, work, got, out, send_sem, recv_sem, turn, direct):
        self.me, self.rep = lax.axis_index("shard"), lax.axis_index("rep")
        self.work, self.got, self.out = work, got, out
        self.send_sem, self.recv_sem = send_sem, recv_sem
        self.size = work.shape[2] // replicas
        bits = [1 << i for i in range(members.bit_length() - 1)]
        bits = bits if turn == 0 else bits[:1] + bits[1:][::-1]
        self.stages = []
        at, decided = 0, 0
        for b in bits[:1] if direct else bits:
            free = [f for f in range(members) if not f & (decided | b)]
            self.stages.append((HALVE, at, free, b, decided))
            at += len(free)
            decided |= b
        if direct:
            self.stages.append((PLANE, at, list(range(2, members, 2)), 0, 0))
            at += members // 2 - 1
        turns = list(range(1, replicas))
        self.stages.append((SCATTER, at, turns, at, 0))
        self.stages.append((COLLECT, at + len(turns), turns, at + 1, 0))
        self.count = len(self.stages)

    def rows(self, rep):
        return pl.ds(pl.multiple_of(rep * self.size, self.size), self.size)

    def copy(self, i, n):
        kind, at, items, b, decided = self.stages[i]
        item = items[n]
        if kind == HALVE:
            src = self.work.at[item | (self.me & decided) | ((self.me ^ b) & b)]
            dst, to = self.got.at[at + n], (self.me ^ b, self.rep)
        elif kind == PLANE:
            src, dst, to = self.work.at[self.me ^ item], self.got.at[at + n], (self.me ^ item, self.rep)
        else:
            src = self.work.at[self.me, :, self.rows(self.rep ^ item if kind == SCATTER else self.rep)]
            dst = self.got.at[b, :, n * self.size : (n + 1) * self.size]
            to = (self.me, self.rep ^ item)
        return pltpu.make_async_remote_copy(
            src, dst, self.send_sem.at[at + n], self.recv_sem.at[at + n], device_id=to, device_id_type=MESH)

    def start(self, i):
        for n in range(len(self.stages[i][2])):
            self.copy(i, n).start()

    def add(self, i):
        kind, at, items, b, decided = self.stages[i]
        for n in range(len(items)):
            cp = self.copy(i, n)
            cp.wait_recv()
            cp.wait_send()
        if kind == HALVE:
            for n, item in enumerate(items):
                keep = item | (self.me & decided) | (self.me & b)
                self.work[keep] = (self.work[keep].astype(f32) + self.got[at + n].astype(f32)).astype(bf16)
        elif kind == PLANE:
            total = self.work[self.me].astype(f32)
            for n in range(len(items)):
                total = total + self.got[at + n].astype(f32)
            self.work[self.me] = total.astype(bf16)
        elif kind == SCATTER:
            near = self.rows(self.rep)
            total = self.work[self.me, :, near].astype(f32)
            for n in range(len(items)):
                total = total + self.got[b, :, n * self.size : (n + 1) * self.size].astype(f32)
            self.work[self.me, :, near] = total.astype(bf16)
        else:
            for n, item in enumerate(items):
                self.work[self.me, :, self.rows(self.rep ^ item)] = self.got[b, :, n * self.size : (n + 1) * self.size]
            blocks, lanes = self.work.shape[1], self.work.shape[3]
            for j in range(blocks):
                self.out[:, j * lanes : (j + 1) * lanes] = self.work[self.me, j].astype(f32)

    def move(self, i):
        self.add(i)
        if i + 1 < self.count:
            self.start(i + 1)


class BwdIn(NamedTuple):
    dres: object
    put: object
    slot: object
    info: object
    chosen: object
    low0: object
    low1: object
    low2: object
    low4: object
    e3: object
    gain: object
    mix_dn: object
    mix_up: object
    q_dn: object
    q_up: object
    kv_dn: object
    kv_up: object
    ga: object
    gb: object
    gk: object
    q: object
    a: object
    o: object
    m: object
    dy: object
    x: object
    kd: object
    gup: object
    gdn: object


class BwdOut(NamedTuple):
    dx: object
    ja_out: object
    jb_out: object
    jc_out: object
    jd_out: object
    je_out: object
    jf_out: object
    jg_out: object


class BwdScratch(NamedTuple):
    w_v: object
    wk_v: object
    t1: object
    t2: object
    q_v: object
    do_v: object
    dq: object
    kd_st: object
    ds_st: object
    dk_r: object
    w_sem: object
    t_sem: object
    g_sem: object
    kd_sem: object
    dk_send: object
    dk_recv: object
    out_sem: object
    ja_w: object
    ja_g: object
    ja_s: object
    ja_r: object
    jb_w: object
    jb_g: object
    jb_s: object
    jb_r: object
    jc_w: object
    jc_g: object
    jc_s: object
    jc_r: object
    jd_w: object
    jd_g: object
    jd_s: object
    jd_r: object
    je_w: object
    je_g: object
    je_s: object
    je_r: object
    jf_w: object
    jf_g: object
    jf_s: object
    jf_r: object
    jg_w: object
    jg_g: object
    jg_s: object
    jg_r: object


class BwdRefs(NamedTuple):
    dres: object
    put: object
    slot: object
    info: object
    chosen: object
    low0: object
    low1: object
    low2: object
    low4: object
    e3: object
    gain: object
    mix_dn: object
    mix_up: object
    q_dn: object
    q_up: object
    kv_dn: object
    kv_up: object
    ga: object
    gb: object
    gk: object
    q: object
    a: object
    o: object
    m: object
    dy: object
    x: object
    kd: object
    gup: object
    gdn: object
    dx: object
    ja_out: object
    jb_out: object
    jc_out: object
    jd_out: object
    je_out: object
    jf_out: object
    jg_out: object
    w_v: object
    wk_v: object
    t1: object
    t2: object
    q_v: object
    do_v: object
    dq: object
    kd_st: object
    ds_st: object
    dk_r: object
    w_sem: object
    t_sem: object
    g_sem: object
    kd_sem: object
    dk_send: object
    dk_recv: object
    out_sem: object
    ja_w: object
    ja_g: object
    ja_s: object
    ja_r: object
    jb_w: object
    jb_g: object
    jb_s: object
    jb_r: object
    jc_w: object
    jc_g: object
    jc_s: object
    jc_r: object
    jd_w: object
    jd_g: object
    jd_s: object
    jd_r: object
    je_w: object
    je_g: object
    je_s: object
    je_r: object
    jf_w: object
    jf_g: object
    jf_s: object
    jf_r: object
    jg_w: object
    jg_g: object
    jg_s: object
    jg_r: object


def job_shapes(z):
    wide = z.rows // min(128, z.rows)
    lanes = min(128, z.rows)
    chunks = (SLOTS, z.sub) if z.aligned else (SLOTS * z.sub // 128, 128)
    return (chunks, chunks, (2 * wide, lanes), (2 * wide, lanes), (wide, lanes), (wide, lanes), (wide + 1, lanes))


def bwd_kernel(z, *refs):
    r = BwdRefs(*refs)
    members, replicas, rows, fc, d, hd = z.members, z.replicas, z.rows, z.fc, z.d, z.hd
    length, cap, w, heads, rk = z.length, z.cap, z.w, z.heads, z.rk
    me, rep = lax.axis_index("shard"), lax.axis_index("rep")
    half = rows // 2
    halves = d // fc
    w_v, t1, t2, q_v, do_v, dq, dres = r.w_v, r.t1, r.t2, r.q_v, r.do_v, r.dq, r.dres
    outs = refs[len(BwdIn._fields) + 1 : len(BwdIn._fields) + len(BwdOut._fields)]
    held = refs[-4 * len(outs) :]
    ja, jb, jc, jd, je, jf, jg = (
        Job(members, replicas, held[4 * i], held[4 * i + 1], out, held[4 * i + 2], held[4 * i + 3], i % 2, i >= 4)
        for i, out in enumerate(outs))

    barrier = pltpu.get_barrier_semaphore()
    others = [(me ^ o, rep) for o in range(1, members)] + [(me, rep ^ o) for o in range(1, replicas)]
    for to in others:
        pl.semaphore_signal(barrier, inc=1, device_id=to, device_id_type=MESH)

    def local(src, dst, sem):
        return pltpu.make_async_copy(src, dst, sem)

    def wide(which):
        return [local(part.at[which, :, :, c * fc : (c + 1) * fc],
                      w_v.at[c, :, h * half : (h + 1) * half], r.w_sem.at[h, c])
                for h, part in enumerate((r.ga, r.gb)) for c in range(halves)]

    load_up = local(r.gup, r.ja_w, r.g_sem.at[0])
    load_dn = local(r.gdn, r.jb_w, r.g_sem.at[1])
    load_up.start()
    load_dn.start()
    mix = wide(WMIX)
    for cp in mix:
        cp.start()
    load_m = local(r.m, t1, r.t_sem.at[0])
    load_dy = local(r.dy, t2, r.t_sem.at[1])
    load_q = local(r.q, q_v, r.t_sem.at[2])
    load_k = local(r.gk.at[0], r.wk_v, r.t_sem.at[3])
    for cp in (load_m, load_dy, load_q, load_k):
        cp.start()
    pl.semaphore_wait(barrier, len(others))
    load_up.wait()
    ja.start(0)
    load_dn.wait()
    jb.start(0)

    rank_of = (lax.broadcasted_iota(jnp.int32, (length, rk), 1) // z.rank).astype(f32)

    def mask(p):
        return jnp.where(rank_of == r.chosen[:, 2 + p : 3 + p], 1.0, 0.0)

    def terms(job, block, left, right, sc):
        lanes = job.work.shape[3]
        g = dot_tn(left, right) * sc
        width = right.shape[1] // members
        for to in range(members):
            for i in range(-(-width // lanes)):
                part = g[:, to * width + i * lanes : to * width + min((i + 1) * lanes, width)]
                if part.shape[1] < lanes:
                    part = jnp.concatenate([part, jnp.zeros((rk, lanes - part.shape[1]), f32)], axis=1)
                job.work[to, block + i] = part.astype(bf16)

    per = r.jc_w.shape[1] // 2

    dresl = do_v
    dresl[...] = dres[...].astype(bf16)
    e2 = (scale_lora * dot_nt(dresl[...], r.mix_up[...]) * mask(2)).astype(bf16)
    terms(jd, per, r.low2[...], dresl[...], scale_lora)
    load_m.wait()
    terms(jc, 0, r.e3[...], t1[...], 1.0)
    load_o = local(r.o, t1, r.t_sem.at[0])
    load_o.start()
    load_dy.wait()
    terms(jd, 0, r.low4[...], t2[...], scale_lora)
    load_x = local(r.x, t2, r.t_sem.at[1])
    load_x.start()
    jd.start(0)
    for cp in mix:
        cp.wait()
    ja.move(0)
    dq[...] = dot_nt(dresl[:, 0:fc], w_v[0].reshape(d, fc)) + dot_nn(e2, r.mix_dn[...])
    jb.move(0)
    for c in range(1, halves):
        dq[...] += dot_nt(dresl[:, c * fc : (c + 1) * fc], w_v[c].reshape(d, fc))
    do_v[...] = dq[...].astype(bf16)
    query = wide(WQ)
    for cp in query:
        cp.start()
    load_o.wait()
    terms(jc, per, e2, t1[...], 1.0)
    jc.start(0)
    load_a = local(r.a, t1, r.t_sem.at[0])
    load_a.start()
    jd.move(0)
    dq[...] = jnp.zeros_like(dq)
    load_q.wait()

    def kd_load(k, buf):
        return local(r.kd.at[k], r.kd_st.at[buf], r.kd_sem.at[buf])

    def ds_copy(k, buf, o):
        return pltpu.make_async_remote_copy(
            r.ds_st.at[buf, me ^ o], r.dk_r.at[me, k], r.dk_send.at[buf, o], r.dk_recv.at[o],
            device_id=(me ^ o, rep), device_id_type=MESH)

    kd_load(0, 0).start()
    groups = 4
    sc = hd ** (-0.5)
    plan = (((jc, 0),), (), ((ja, 1), (jb, 1), (jd, 1)), (), ((jc, 1), (ja, 2), (jb, 2)), ((jd, 2),), ((jc, 2), (ja, 3), (jb, 3)),
            ((jd, 3),))

    def act(some):
        for job, i in some:
            job.move(i)

    def attend(k, _):
        buf = lax.rem(k, 2)

        @pl.when(k + 1 < members)
        def _():
            kd_load(k + 1, 1 - buf).start()

        for i, some in enumerate(plan):
            pl.when(k == i)(lambda some=some: act(some))
        kd_load(k, buf).wait()
        kvd = r.kd_st[buf]
        kd, vd = kvd[:, :hd], kvd[:, hd:]
        put = r.put[k]
        qp = dot_nn(put, q_v[...]).astype(bf16)
        dop = dot_nn(put, do_v[...]).astype(bf16)
        info = r.info[k]
        n = heads // groups
        dqs = []
        dk = jnp.zeros((length, hd), f32)
        dv = jnp.zeros((length, hd), f32)
        for h in range(groups):
            at = slice(h * n * hd, (h + 1) * n * hd)
            qr, dor = to_rows(qp[:, at], n), to_rows(dop[:, at], n)
            p = softmax_rows(qr, kd, info, n)
            dp = dot_nt(dor, vd)
            ds = (p * (dp - jnp.sum(dp * p, axis=1, keepdims=True))).astype(bf16)
            dqs.append(to_cols((dot_nn(ds, kd) * sc).astype(bf16), n))
            dk = dk + dot_tn(ds, qr)
            dv = dv + dot_tn(p.astype(bf16), dor)
        dq[...] += dot_tn(put, jnp.concatenate(dqs, axis=1))
        dkv = jnp.concatenate([dk * sc, dv], axis=1).astype(bf16)
        slots = dot_nn(key_onehot(r.slot[k], z.slots), dkv).astype(bf16).reshape(members, cap, w)

        @pl.when(k >= 2)
        def _():
            for o in range(1, members):
                ds_copy(k, buf, o).wait_send()

        r.ds_st[buf] = slots
        r.dk_r[me, k] = r.ds_st[buf, me]
        for o in range(1, members):
            ds_copy(k, buf, o).start()
        return 0

    lax.fori_loop(0, members, attend, 0)

    following = {ja: 4, jb: 4, jc: 3, jd: 4, je: 0, jf: 0, jg: 0}

    def go(*jobs):
        for job in jobs:
            if following[job] < job.count:
                job.move(following[job])
                following[job] += 1

    go(ja, jb)
    q_v[...] = dq[...].astype(bf16)
    e0 = (scale_lora * dot_nt(q_v[...], r.q_up[...]) * mask(0)).astype(bf16)
    load_a.wait()
    terms(je, 0, e0, t1[...], 1.0)
    je.start(0)
    terms(jf, 0, r.low0[...], q_v[...], scale_lora)
    jf.start(0)
    for o in range(1, members):
        local(r.dk_r.at[me ^ o], r.dk_r.at[me ^ o], r.dk_recv.at[o]).wait()
    go(jd, jc)
    dkv = jnp.zeros((length, w), f32)
    for k in range(members):
        total = r.dk_r[0, k].astype(f32)
        for s in range(1, members):
            total = total + r.dk_r[s, k].astype(f32)
        dkv = dkv + dot_tn(r.put[k], total.astype(bf16))
    dkv = dkv.astype(bf16)
    go(je, jf)
    e1 = (scale_lora * dot_nt(dkv, r.kv_up[...]) * mask(1)).astype(bf16)
    terms(jg, 0, e1, t1[...], 1.0)
    terms(jg, per, r.low1[...], dkv, scale_lora)
    jg.start(0)
    load_k.wait()
    dq[...] = (dot_nn(e0, r.q_dn[...]) + dot_nn(e1, r.kv_dn[...])
               + dot_nt(dkv, r.wk_v[...].reshape(d, w)))
    go(jd, jc, je, jf, jg)
    for cp in query:
        cp.wait()
    for c in range(halves):
        dq[...] += dot_nt(q_v[:, c * fc : (c + 1) * fc], w_v[c].reshape(d, fc))
        go(je, jf, jg)
    load_x.wait()
    gain = r.gain[...]

    def back(i, _):
        at = pl.ds(pl.multiple_of(i * 128, 128), 128)
        n, inv = norm_parts(t2[at, :].astype(f32))
        do_v[at, :] = (dres[at, :] + norm_back(n, inv, gain, dq[at, :])).astype(bf16)
        return 0

    for part in range(2):
        lax.fori_loop(part * length // 256, (part + 1) * length // 256, back, 0)
        go(je, jf, jg)
    out = local(do_v, r.dx, r.out_sem)
    out.start()
    while any(following[job] < job.count for job in following):
        go(ja, jb, jc, jd, je, jf, jg)
    out.wait()
    for buf in range(2):
        for o in range(1, members):
            ds_copy(buf, buf, o).wait_send()


def backward(z, args):
    vm = pl.BlockSpec(memory_space=pltpu.VMEM)
    hbm = pl.BlockSpec(memory_space=pl.ANY)
    m, n, d, rk, w = z.members, z.length, z.d, z.rk, z.w
    s = jax.ShapeDtypeStruct
    dma = pltpu.SemaphoreType.DMA
    shapes = job_shapes(z)
    legs = m - 1 + 2
    sems = m - 1 + 2 * (z.replicas - 1)
    scratch = dict(
        w_v=pltpu.VMEM((d // z.fc, m, z.rows, z.fc), bf16), wk_v=pltpu.VMEM((m, z.rows, w), bf16),
        t1=pltpu.VMEM((n, d), bf16), t2=pltpu.VMEM((n, d), bf16), q_v=pltpu.VMEM((n, d), bf16), do_v=pltpu.VMEM((n, d), bf16),
        dq=pltpu.VMEM((n, d), f32), kd_st=pltpu.VMEM((2, n, w), bf16), ds_st=pltpu.VMEM((2, m, z.cap, w), bf16),
        dk_r=pltpu.VMEM((m, m, z.cap, w), bf16),
        w_sem=dma((2, d // z.fc)), t_sem=dma((4,)), g_sem=dma((2,)), kd_sem=dma((2,)), dk_send=dma((2, m)),
        dk_recv=dma((m,)), out_sem=dma(()))
    scratch = [scratch[k] for k in BwdScratch._fields[: len(scratch)]]
    job_outs = [s((rk, blocks * lanes), f32) for blocks, lanes in shapes]
    job_scratch = [x for blocks, lanes in shapes for x in (
        pltpu.VMEM((m, blocks, rk, lanes), bf16), pltpu.VMEM((legs, blocks, rk, lanes), bf16), dma((sems,)), dma((sems,)))]
    first_hbm = 17
    got = pl.pallas_call(
        lambda *refs: bwd_kernel(z, *refs),
        in_specs=[vm] * first_hbm + [hbm] * (len(BwdIn._fields) - first_hbm),
        out_specs=[hbm] + [vm] * len(shapes),
        out_shape=[s((n, d), bf16)] + job_outs,
        scratch_shapes=scratch + job_scratch,
        compiler_params=pltpu.CompilerParams(
            vmem_limit_bytes=FWD_VMEM, collective_id=2, has_side_effects=True),
    )(*BwdIn(**args))
    return BwdOut(*got)


def final(sums, z, experts, rank):
    c, n = z.rows, z.w // z.members
    ff = z.ff // z.members
    cuts = ((4, 0, c), (5, 0, c), (6, 0, c), (6, c, n), (2, c, c), (3, c, c), (2, 0, c), (0, 0, ff), (1, 0, ff), (3, 0, c))

    def kernel(*refs):
        for (job, at, width), out in zip(cuts, refs[len(sums):]):
            out[...] = refs[job][:, at : at + width].reshape(experts, rank, width)

    vm = pl.BlockSpec(memory_space=pltpu.VMEM)
    return pl.pallas_call(
        kernel, in_specs=[vm] * len(sums), out_specs=[vm] * len(cuts),
        out_shape=[jax.ShapeDtypeStruct((experts, rank, w), f32) for _, _, w in cuts])(*sums)


def local(tokens, out_grad, token_perm, seq_lens, adapter_ids,
          attn_g, attn_b, wq, bq, wkv, bv, wmix, bmix, mlp_g, mlp_b, wexp, bexp, wred, bred,
          q_dn, q_up, kv_dn, kv_up, mix_dn, mix_up, exp_dn, exp_up, red_dn, red_up):
    members = lax.axis_size("shard")
    replicas = lax.axis_size("rep")
    rep = lax.axis_index("rep")
    length, d = tokens.shape
    experts, rank = q_dn.shape[:2]
    rk = experts * rank
    z = Sizes(members, replicas, length, d, wexp.shape[1], bv.shape[0] * members, rk, rank,
              seq_lens.shape[1], adapter_ids.shape[2])
    flat = lambda s: s.reshape(rk, s.shape[2])
    q_dn, q_up, kv_dn, kv_up, mix_dn, mix_up, exp_dn, exp_up, red_dn, red_up = map(
        flat, (q_dn, q_up, kv_dn, kv_up, mix_dn, mix_up, exp_dn, exp_up, red_dn, red_up))
    group = lax.dynamic_index_in_dim(
        token_perm.reshape(members, replicas, length), rep, 1, keepdims=False)

    by_chunk = lambda s: s.reshape(s.shape[0], members, SLOTS, z.sub).transpose(2, 0, 1, 3).reshape(
        SLOTS, s.shape[0], z.fc)
    chunked = (lambda s: s) if z.aligned else by_chunk
    got = forward(z, FwdIn(
        x=tokens, dy=out_grad, attn_g=attn_g, attn_b=attn_b, bq=bq, bmix=bmix, mlp_g=mlp_g, mlp_b=mlp_b, bred=bred, bexp=bexp, bv=bv,
        lens=seq_lens, ids=adapter_ids.reshape(1, -1), group=group,
        q_dn=q_dn, q_up=q_up, kv_dn=kv_dn, kv_up=kv_up, mix_dn=mix_dn, mix_up=mix_up, exp_dn=exp_dn,
        exp_up=chunked(exp_up), red_dn=chunked(red_dn), red_up=red_up,
        wq=wq, wkv=wkv, wmix=wmix, wexp=chunked(wexp), wred=wred.reshape(SLOTS, z.sub, d)))
    gup, gdn = got.gup, got.gdn
    if not z.aligned:
        pack = 128 // z.sub
        gup, gdn = (g.reshape(members, SLOTS // pack, pack, rk, z.sub).transpose(0, 1, 3, 2, 4).reshape(
            members, SLOTS // pack, rk, 128) for g in (gup, gdn))
    back = backward(z, dict(
        dres=got.dres, put=got.put, slot=got.slot, info=got.info, chosen=got.chosen, low0=got.low0, low1=got.low1,
        low2=got.low2, low4=got.low4, e3=got.e3, gain=got.gain, ga=got.ga, gb=got.gb, gk=got.gk, q=got.q, a=got.a,
        o=got.o, m=got.m, kd=got.kd, gup=gup, gdn=gdn,
        mix_dn=mix_dn, mix_up=mix_up, q_dn=q_dn, q_up=q_up, kv_dn=kv_dn, kv_up=kv_up, dy=out_grad, x=tokens))
    g = final(back[1:], z, experts, rank)
    return (got.layer, back.dx, *g)


def solution(mesh):
    both = ("shard", "rep")
    row, vec = P("shard", None), P("shard")
    in_specs = (
        P(both, None), P(both, None), P(), P(both, None), P(both, None, None),
        vec, vec, row, vec, row, vec, row, vec, vec, vec, row, vec, row, vec,
    ) + (P(),) * 10
    out_specs = (P(both, None), P(both, None)) + (P(None, None, "shard"),) * 10
    return jax.shard_map(local, mesh=mesh, in_specs=in_specs, out_specs=out_specs, check_vma=False)
```

```python
import jax
import jax.numpy as jnp
from jax import lax
from jax.experimental import pallas as pl
from jax.experimental.pallas import tpu as pltpu
from jax.sharding import PartitionSpec as P
from typing import NamedTuple

scale_lora = 0.5
eps = 1e-05
f32 = jnp.float32
bf16 = jnp.bfloat16
neg_big = -1e30
log2_e = 1.4426950408889634
gelu_c = 0.7978845608028654
VMEM_LIMIT = 60 * 1024 * 1024


def dot_nn(a, b):
    return lax.dot_general(a, b, (((1,), (0,)), ((), ())), preferred_element_type=f32)


def dot_nt(a, b):
    return lax.dot_general(a, b, (((1,), (1,)), ((), ())), preferred_element_type=f32)


def dot_tn(a, b):
    return lax.dot_general(a, b, (((0,), (0,)), ((), ())), preferred_element_type=f32)


def key_onehot(slot_row, slots):
    ids = lax.broadcasted_iota(jnp.int32, (slots, slot_row.shape[1]), 0)
    return jnp.where(ids == slot_row, 1.0, 0.0).astype(bf16)


def to_rows(x, heads):
    hd = x.shape[1] // heads
    return jnp.concatenate([x[:, h * hd : (h + 1) * hd] for h in range(heads)], axis=0)


def to_cols(x, heads):
    c = x.shape[0] // heads
    return jnp.concatenate([x[h * c : (h + 1) * c] for h in range(heads)], axis=1)


def softmax_rows(qr, kd, span, heads):
    rows, keys = qr.shape[0], kd.shape[0]
    c = rows // heads
    u = lax.broadcasted_iota(jnp.int32, (c, keys), 1).astype(f32)
    allowed = (u >= span[:, 0:1]) & (u <= span[:, 1:2])
    s = jnp.where(allowed[None], dot_nt(qr, kd).reshape(heads, c, keys), neg_big)
    top = jnp.max(s, axis=2, keepdims=True)
    e = jnp.exp2((s - top) * (kd.shape[1] ** (-0.5) * log2_e))
    p = e * (1.0 / jnp.sum(e, axis=2, keepdims=True))
    return p.reshape(rows, keys)


MESH = pl.DeviceIdType.MESH


class Gather:
    def __init__(self, members, own, full, slots, send_sem, recv_sem):
        self.members = members
        self.me, self.rep = lax.axis_index("shard"), lax.axis_index("rep")
        self.own, self.full = own, full
        self.base = [sum(slots[:i]) for i in range(len(slots))]
        self.send_sem, self.recv_sem = send_sem, recv_sem
        self.bits = [1 << i for i in range(1, members.bit_length() - 1)]
        self.planes = list(range(0, members, 2))
        self.sent = {}

    def place(self, kind, slot, offset):
        return self.full[kind].at[slot, self.me ^ offset]

    def copy(self, kind, slot, offset, there, to, to_slot):
        mine = self.sent.setdefault((kind, slot), {})
        at = mine.setdefault((offset, there, to_slot), len(mine))
        src = self.own[kind](slot) if offset == 0 else self.place(kind, slot, offset)
        pltpu.make_async_remote_copy(
            src, self.full[kind].at[to_slot, self.me ^ offset],
            self.send_sem.at[self.base[kind] + slot, at],
            self.recv_sem.at[self.base[kind] + to_slot, there],
            device_id=to, device_id_type=MESH).start()

    def wait(self, kind, slot, offset):
        piece = self.place(kind, slot, offset)
        pltpu.make_async_copy(piece, piece, self.recv_sem.at[self.base[kind] + slot, offset]).wait()

    def order(self, kind):
        return self.bits if kind % 2 == 0 else self.bits[::-1]

    def stage(self, kind, offset):
        return max(i for i, b in enumerate(self.order(kind)) if offset & b)

    def issue(self, slot, kinds, plane=True):
        for kind in kinds:
            if plane:
                for b in self.order(kind):
                    self.copy(kind, slot, 0, b, (self.me ^ b, self.rep), slot)
            self.copy(kind, slot, 0, 1, (self.me ^ 1, self.rep), slot)

    def arrive(self, slot, kinds, direct, swap_to=None):
        for kind in kinds:
            order = self.order(kind)
            some = [o for o in self.planes if o and (bin(o).count("1") == 1) == direct]
            some.sort(key=lambda o: self.stage(kind, o))
            for o in some:
                self.wait(kind, slot, o)
                for i in range(self.stage(kind, o) + 1, len(order)):
                    self.copy(kind, slot, o, o ^ order[i], (self.me ^ order[i], self.rep), slot)
                if swap_to is not None:
                    self.copy(kind, slot, o, o, (self.me, self.rep ^ 1), swap_to)
                self.copy(kind, slot, o, o ^ 1, (self.me ^ 1, self.rep), slot)

    def swapped(self, slot, kinds):
        for kind in kinds:
            for o in self.planes[1:]:
                self.wait(kind, slot, o)
                self.copy(kind, slot, o, o ^ 1, (self.me ^ 1, self.rep), slot)

    def ready(self, slot, kinds):
        for kind in kinds:
            for o in range(1, self.members, 2):
                self.wait(kind, slot, o)

    def finish(self):
        for (kind, slot), mine in self.sent.items():
            piece = self.place(kind, slot, 0)
            for at in mine.values():
                pltpu.make_async_copy(piece, piece, self.send_sem.at[self.base[kind] + slot, at]).wait()


U, V, C = (0, 1, 2), (3, 4, 5), (6, 7)
SLOTS = 8
WE, WR, AT, AB, KV = range(5)
BOTH, HALVES = (WE, WR), (AT, AB)
WQ, WMIX = 0, 1
SEND, NEAR, FAR, SWAP = range(4)
MLP_ORDER = (0, 1, 4, 3, 2, 6, 5, 7)
SERVE = {
    0: ((SEND, KV, 0),),
    1: ((SEND, WR, 0),),
    10: ((NEAR, KV, 0),),
    21: ((SEND, WE, 0),),
    24: ((NEAR, WR, 0),),
    25: ((FAR, KV, 0),),
    2: ((SEND, AT, 0),),
    4: ((NEAR, WE, 0),),
    5: ((FAR, WR, 0), (NEAR, AT, 0), (SEND, AB, 0), (FAR, WE, 0), (SEND, WE, 1), (SWAP, WR, 3), (FAR, AT, 0), (SEND, AB, 1), (SWAP, WE, 3), (NEAR, AB, 0), (NEAR, WE, 1), (SEND, AT, 1), (FAR, AB, 0),),
    15: ((NEAR, AB, 1),),
    41: ((FAR, WE, 1), (SEND, WR, 1),),
    43: ((FAR, AB, 1),),
    44: ((NEAR, AT, 1), (SEND, WE, 2), (SWAP, WE, 4),),
    46: ((NEAR, WR, 1),),
    7: ((FAR, AT, 1),),
    16: ((SEND, WR, 2),),
    17: ((FAR, WR, 1),),
    12: ((NEAR, WE, 2),),
    13: ((SEND, WR, 6),),
    60: ((NEAR, WR, 2),),
    61: ((SWAP, WR, 4),),
    62: ((FAR, WE, 2), (SEND, WE, 6),),
    63: ((FAR, WR, 2),),
    64: ((NEAR, WR, 6), (SEND, WE, 7),),
    66: ((NEAR, WE, 6),),
    67: ((FAR, WR, 6), (SEND, WR, 7),),
    69: ((NEAR, WE, 7), (FAR, WE, 6), (SWAP, WE, 5),),
    70: ((NEAR, WR, 7), (SWAP, WR, 5),),
    72: ((FAR, WE, 7), (FAR, WR, 7),),
}


def chunk_of(slot, parity):
    slot = jnp.int32(slot)
    low = jnp.where(slot < 3, slot, slot + 2)
    high = jnp.where(slot < 3, slot + 5, slot - 3)
    return jnp.where(slot >= 6, slot - 3, jnp.where(parity == 0, low, high))


def norm_parts(v):
    center = v - jnp.mean(v, axis=-1, keepdims=True)
    inv = lax.rsqrt(jnp.mean(center * center, axis=-1, keepdims=True) + eps)
    return center * inv, inv


def norm_back(n, inv, gain, dn):
    w = gain * dn
    return (w - jnp.mean(w, axis=-1, keepdims=True)
            - n * jnp.mean(w * n, axis=-1, keepdims=True)) * inv


class Sizes:
    def __init__(self, members, replicas, length, d, ff, hd, rk, rank, seqs, projs):
        self.members, self.replicas, self.length, self.d, self.ff = members, replicas, length, d, ff
        self.hd, self.rk, self.rank, self.seqs, self.projs = hd, rk, rank, seqs, projs
        self.heads = d // hd
        self.cap = 3 * length // (2 * members)
        self.slots = members * self.cap
        self.w = 2 * hd
        self.rows = d // members
        self.sub = ff // members // SLOTS
        self.fc = self.sub * members
        self.aligned = self.sub % 128 == 0
        self.be_at = 7 * self.rows
        self.vb_at = self.be_at + ff // members
        self.len_at = self.vb_at + 128
        self.ids_at = self.len_at + 128
        self.small_cols = self.ids_at + 128


class FwdIn(NamedTuple):
    x: object
    attn_g: object
    attn_b: object
    bq: object
    bmix: object
    mlp_g: object
    mlp_b: object
    bred: object
    bexp: object
    bv: object
    lens: object
    ids: object
    group: object
    q_dn: object
    q_up: object
    kv_dn: object
    kv_up: object
    dy: object
    mix_dn: object
    mix_up: object
    exp_dn: object
    exp_up: object
    red_dn: object
    red_up: object
    wq: object
    wkv: object
    wmix: object
    wexp: object
    wred: object


class FwdOut(NamedTuple):
    dres: object
    put: object
    slot: object
    info: object
    chosen: object
    low0: object
    low1: object
    low2: object
    low4: object
    e3: object
    gain: object
    a: object
    q: object
    o: object
    m: object
    resid: object
    kd: object
    gup: object
    gdn: object
    layer: object
    kvs: object
    ge: object
    gr: object
    ga: object
    gb: object
    gk: object


class FwdScratch(NamedTuple):
    y: object
    dy_v: object
    mix_dn_v: object
    mix_up_v: object
    exp_dn_v: object
    exp_up_v: object
    red_dn_v: object
    red_up_v: object
    late_sem: object
    we_v: object
    wr_v: object
    a_v: object
    q_v: object
    kvp: object
    kvb: object
    kd_st: object
    gup_st: object
    gdn_st: object
    sm: object
    lowr: object
    er: object
    low3: object
    e4: object
    send_sem: object
    recv_sem: object
    sm_send: object
    sm_recv: object
    kv_send: object
    kv_recv: object
    stage_sem: object
    store_sem: object
    load_sem: object
    kvb_sem: object
    kd_sem: object
    g_sem: object
    out_sem: object


class FwdRefs(NamedTuple):
    x: object
    attn_g: object
    attn_b: object
    bq: object
    bmix: object
    mlp_g: object
    mlp_b: object
    bred: object
    bexp: object
    bv: object
    lens: object
    ids: object
    group: object
    q_dn: object
    q_up: object
    kv_dn: object
    kv_up: object
    dy: object
    mix_dn: object
    mix_up: object
    exp_dn: object
    exp_up: object
    red_dn: object
    red_up: object
    wq: object
    wkv: object
    wmix: object
    wexp: object
    wred: object
    dres: object
    put: object
    slot: object
    info: object
    chosen: object
    low0: object
    low1: object
    low2: object
    low4: object
    e3: object
    gain: object
    a: object
    q: object
    o: object
    m: object
    resid: object
    kd: object
    gup: object
    gdn: object
    layer: object
    kvs: object
    ge: object
    gr: object
    ga: object
    gb: object
    gk: object
    y: object
    dy_v: object
    mix_dn_v: object
    mix_up_v: object
    exp_dn_v: object
    exp_up_v: object
    red_dn_v: object
    red_up_v: object
    late_sem: object
    we_v: object
    wr_v: object
    a_v: object
    q_v: object
    kvp: object
    kvb: object
    kd_st: object
    gup_st: object
    gdn_st: object
    sm: object
    lowr: object
    er: object
    low3: object
    e4: object
    send_sem: object
    recv_sem: object
    sm_send: object
    sm_recv: object
    kv_send: object
    kv_recv: object
    stage_sem: object
    store_sem: object
    load_sem: object
    kvb_sem: object
    kd_sem: object
    g_sem: object
    out_sem: object


def fwd_kernel(z, *refs):
    r = FwdRefs(*refs)
    members, rows, fc, sub, d, hd = z.members, z.rows, z.fc, z.sub, z.d, z.hd
    length, cap, w, heads, rk = z.length, z.cap, z.w, z.heads, z.rk
    me, rep = lax.axis_index("shard"), lax.axis_index("rep")
    parity = lax.rem(rep, 2)
    half = rows // 2
    att = (r.wq, r.wmix)
    g = Gather(
        members,
        [lambda s: r.ge.at[s, me],
         lambda s: r.wred.at[chunk_of(s, parity)],
         lambda s: att[s].at[0:half],
         lambda s: att[s].at[half:rows],
         lambda s: r.wkv],
        [r.ge, r.gr, r.ga, r.gb, r.gk],
        [SLOTS, SLOTS, 2, 2, 1], r.send_sem, r.recv_sem)
    we_v, wr_v, sm, y, dm = r.we_v, r.wr_v, r.sm, r.y, r.dres

    def serve(point):
        for op, kind, slot in SERVE.get(point, ()):
            swap_to = slot + 3 if slot in U and kind in BOTH else None
            if op == SEND:
                g.issue(slot, (kind,))
            elif op == SWAP:
                g.swapped(slot, (kind,))
            else:
                g.arrive(slot, (kind,), op == NEAR, swap_to)

    barrier = pltpu.get_barrier_semaphore()
    others = [(me ^ o, rep) for o in range(1, members)] + [(me, rep ^ 1)]
    for to in others:
        pl.semaphore_signal(barrier, inc=1, device_id=to, device_id_type=MESH)

    def stage_copies(slot):
        j = chunk_of(slot, parity)
        to = we_v.at[0, slot]
        if not z.aligned:
            return [pltpu.make_async_copy(r.wexp.at[j], to, r.stage_sem.at[slot])]
        return [pltpu.make_async_copy(
            r.wexp.at[:, pl.ds(pl.multiple_of(s * (z.ff // members) + j * sub, sub), sub)],
            to.at[:, s * sub : (s + 1) * sub], r.stage_sem.at[slot]) for s in range(members)]

    def stored(slot):
        return pltpu.make_async_copy(we_v.at[0, slot], r.ge.at[slot, me], r.store_sem.at[slot])

    def staged(slot):
        pltpu.make_async_copy(we_v.at[0, slot], we_v.at[0, slot], r.stage_sem.at[slot]).wait()
        stored(slot).start()

    for slot in range(SLOTS):
        for cp in stage_copies(slot):
            cp.start()
    pl.semaphore_wait(barrier, len(others))

    def small_copy(o):
        return pltpu.make_async_remote_copy(
            sm.at[me], sm.at[me], r.sm_send.at[o], r.sm_recv.at[o],
            device_id=(me ^ o, rep), device_id_type=MESH)

    serve(0)
    coming = [pltpu.make_async_copy(src, dst, r.late_sem.at[i]) for i, (src, dst) in enumerate((
        (r.mix_dn, r.mix_dn_v), (r.mix_up, r.mix_up_v), (r.dy, r.dy_v), (r.exp_dn, r.exp_dn_v),
        (r.exp_up, r.exp_up_v), (r.red_dn, r.red_dn_v), (r.red_up, r.red_up_v)))]
    for cp in coming:
        cp.start()
    r = r._replace(dy=r.dy_v, mix_dn=r.mix_dn_v, mix_up=r.mix_up_v, exp_dn=r.exp_dn_v, exp_up=r.exp_up_v,
                   red_dn=r.red_dn_v, red_up=r.red_up_v)
    sm[me] = jnp.zeros((1, z.small_cols), f32)
    for i, v in enumerate((r.attn_g, r.attn_b, r.bq, r.bmix, r.mlp_g, r.mlp_b, r.bred)):
        sm[me, :, i * rows : (i + 1) * rows] = v[...].astype(f32).reshape(1, rows)
    sm[me, :, z.be_at : z.vb_at] = r.bexp[...].astype(f32).reshape(1, z.vb_at - z.be_at)
    sm[me, :, z.vb_at : z.vb_at + hd // members] = r.bv[...].astype(f32).reshape(1, hd // members)
    sm[me, :, z.len_at : z.len_at + z.seqs] = r.lens[...].astype(f32)
    for j in range(z.seqs):
        at = z.ids_at + j * z.projs
        sm[me, :, at : at + z.projs] = r.ids[0, j : j + 1, :].astype(f32)
    for o in range(1, members):
        small_copy(o).start()
    for slot in range(SLOTS):
        staged(slot)
    for slot in range(SLOTS):
        stored(slot).wait()
    serve(1)
    for o in range(1, members):
        pltpu.make_async_copy(sm.at[me ^ o], sm.at[me ^ o], r.sm_recv.at[o]).wait()

    def vec(row):
        return jnp.concatenate([sm[s, :, row * rows : (row + 1) * rows] for s in range(members)], axis=1)

    def norm_rows(src, gain, bias, dst, part):
        gv, bv = vec(gain), vec(bias)

        def body(i, _):
            at = pl.ds(pl.multiple_of(i * 128, 128), 128)
            n, _inv = norm_parts(src[at, :].astype(f32))
            dst[at, :] = (n * gv + bv).astype(bf16)
            return 0

        lax.fori_loop(part * length // 256, (part + 1) * length // 256, body, 0)

    for part in range(2):
        serve(10 + part)
        norm_rows(r.x, 0, 1, r.a_v, part)

    r.gain[...] = vec(0)

    t_row = lax.broadcasted_iota(jnp.int32, (1, length), 1)
    before_t = lax.broadcasted_iota(jnp.int32, (length, length), 0) < lax.broadcasted_iota(
        jnp.int32, (length, length), 1)
    c_ids = lax.broadcasted_iota(jnp.int32, (cap, length), 0)
    lane = lax.broadcasted_iota(jnp.int32, (cap, 128), 1)
    span = length * z.replicas
    first = (me * z.replicas + rep) * length
    tf = t_row.astype(f32)
    src_cols = lax.div(r.group[...], span).astype(f32).T
    chosen = jnp.zeros((length, 128), f32)
    for k in range(members):
        serve(20 + k)
        row = r.group[k : k + 1, :]
        src = lax.div(row, span)
        earlier = jnp.where((src_cols[:, k : k + 1] == src.astype(f32)) & before_t, 1.0, 0.0)
        slot_row = src * cap + jnp.sum(earlier, axis=0, keepdims=True).astype(jnp.int32)
        r.slot[k] = slot_row
        hit = slot_row == c_ids + me * cap

        def pick(values):
            return jnp.sum(jnp.where(hit, values, 0.0), axis=1, keepdims=True)

        full = pick(jnp.ones_like(tf))
        tok = pick((row - first + 1).astype(f32)) - 1.0
        put = jnp.where(tok == tf, 1.0, 0.0).astype(bf16)
        r.put[k] = put
        end = jnp.zeros((1, 1), f32)
        start = jnp.zeros_like(tf)
        ids = [jnp.zeros_like(tf) for _ in range(z.projs)]
        for j in range(z.seqs):
            n = sm[k, :, z.len_at + j : z.len_at + j + 1]
            inside = (tf >= end) & (tf < end + n)
            end = end + n
            start = start + jnp.where(tf >= end, n, 0.0)
            for p in range(z.projs):
                at = z.ids_at + j * z.projs + p
                ids[p] = ids[p] + jnp.where(inside, sm[k, :, at : at + 1], 0.0)
        info = jnp.where(lane == 0, pick(start) + (1.0 - full), 0.0)
        info = jnp.where(lane == 1, pick(tf), info)
        for p in range(z.projs):
            info = jnp.where(lane == 2 + p, pick(ids[p]), info)
        r.info[k] = info
        chosen = chosen + dot_tn(put, info.astype(bf16))
    r.chosen[...] = chosen
    rank_of = lax.broadcasted_iota(jnp.int32, (length, rk), 1) // z.rank

    def mask(p):
        return jnp.where(rank_of.astype(f32) == r.chosen[:, 2 + p : 3 + p], 1.0, 0.0)

    a_v, q_v = r.a_v, r.q_v
    o_v = q_v
    serve(2)
    r.low0[...] = (dot_nt(a_v[...], r.q_dn[...]) * mask(0)).astype(bf16)
    r.low1[...] = (dot_nt(a_v[...], r.kv_dn[...]) * mask(1)).astype(bf16)
    out_a = pltpu.make_async_copy(a_v, r.a, r.out_sem.at[0])
    out_a.start()

    serve(3)
    g.ready(0, (KV,))
    kv_loads = [pltpu.make_async_copy(
        r.wkv if o == 0 else g.place(KV, 0, o), we_v.at[1, me ^ o, :, 0:w], r.kv_send.at[o]) for o in range(members)]
    for cp in kv_loads:
        cp.start()
    for cp in kv_loads:
        cp.wait()
    back_kv = pltpu.make_async_copy(we_v.at[1, me, :, 0:w], g.place(KV, 0, 0), r.kv_send.at[0])
    back_kv.start()
    vb = jnp.concatenate([sm[s, :, z.vb_at : z.vb_at + hd // members] for s in range(members)], axis=1)
    kv_bias = jnp.concatenate([jnp.zeros((1, hd), f32), vb], axis=1)
    kv = (dot_nn(a_v[...], we_v[1, :, :, 0:w].reshape(d, w)) + kv_bias
          + scale_lora * dot_nn(r.low1[...], r.kv_up[...])).astype(bf16)
    for k in range(members):
        r.kvp[k] = dot_nn(r.put[k], kv).astype(bf16)

    def kv_copy(o):
        return pltpu.make_async_remote_copy(
            r.kvp, r.kvs.at[me], r.kv_send.at[o], r.kv_recv.at[o],
            device_id=(me ^ o, rep), device_id_type=MESH)

    back_kv.wait()
    own_kv = pltpu.make_async_copy(r.kvp, r.kvs.at[me], r.kv_send.at[0])
    for o in range(1, members):
        kv_copy(o).start()
    own_kv.start()

    for slot in V:
        g.issue(slot, BOTH, False)
    serve(4)

    def wide_load(which):
        g.ready(which, HALVES)
        out = []
        for kind in HALVES:
            for o in range(members):
                src = g.own[kind](which) if o == 0 else g.place(kind, which, o)
                for c in range(d // fc):
                    out.append(pltpu.make_async_copy(
                        src.at[:, c * fc : (c + 1) * fc],
                        we_v.at[c, me ^ o, (kind - AT) * half : (kind - AT + 1) * half],
                        r.load_sem.at[kind - AT, c, o]))
        for cp in out:
            cp.start()
        for cp in out:
            cp.wait()
        back = [pltpu.make_async_copy(
            we_v.at[c, me, (kind - AT) * half : (kind - AT + 1) * half],
            g.place(kind, which, 0).at[:, c * fc : (c + 1) * fc],
            r.load_sem.at[kind - AT, c, 0]) for kind in HALVES for c in range(d // fc)]
        for cp in back:
            cp.start()
        return back

    serve(5)
    back_q = wide_load(WQ)
    q_bias = vec(2)
    for c in range(d // fc):
        serve(14 + c)
        at = slice(c * fc, (c + 1) * fc)
        q_v[:, at] = (dot_nn(a_v[...], we_v[c].reshape(d, fc)) + q_bias[:, at]
                      + scale_lora * dot_nn(r.low0[...], r.q_up[:, at])).astype(bf16)
    out_q = pltpu.make_async_copy(q_v, r.q, r.out_sem.at[1])
    out_q.start()

    for cp in back_q:
        cp.wait()

    serve(6)

    for o in range(1, members):
        pltpu.make_async_copy(r.kvs.at[me ^ o], r.kvs.at[me ^ o], r.kv_recv.at[o]).wait()
    own_kv.wait()
    for cp in coming:
        cp.wait()
    dm[...] = jnp.zeros_like(dm)

    def kvb_load(k, buf):
        return pltpu.make_async_copy(r.kvs.at[:, k], r.kvb.at[buf], r.kvb_sem.at[buf])

    def kd_out(k, buf):
        return pltpu.make_async_copy(r.kd_st.at[buf], r.kd.at[k], r.kd_sem.at[buf])

    kvb_load(0, 0).start()
    groups = 2

    def attend(k, _):
        buf = lax.rem(k, 2)

        @pl.when(k + 1 < members)
        def _():
            kvb_load(k + 1, 1 - buf).start()

        for i in range(min(members, 16)):
            if 40 + i in SERVE:
                pl.when(k == i)(lambda i=i: serve(40 + i))
        kvb_load(k, buf).wait()
        oh = key_onehot(r.slot[k], z.slots)
        kvd = dot_tn(oh, r.kvb[buf].reshape(z.slots, w)).astype(bf16)

        @pl.when(k >= 2)
        def _():
            kd_out(k, buf).wait()

        r.kd_st[buf] = kvd
        kd_out(k, buf).start()
        put = r.put[k]
        qp = dot_nn(put, q_v[...]).astype(bf16)
        info = r.info[k]
        outs = []
        per = heads // groups
        for h in range(groups):
            qr = to_rows(qp[:, h * per * hd : (h + 1) * per * hd], per)
            p = softmax_rows(qr, kvd[:, :hd], info, per).astype(bf16)
            outs.append(to_cols(dot_nn(p, kvd[:, hd:]).astype(bf16), per))
        dm[...] += dot_tn(put, jnp.concatenate(outs, axis=1))
        return 0

    lax.fori_loop(0, members, attend, 0)
    out_q.wait()
    o_v[...] = dm[...].astype(bf16)
    out_o = pltpu.make_async_copy(o_v, r.o, r.out_sem.at[2])
    out_o.start()
    r.low2[...] = (dot_nt(o_v[...], r.mix_dn[...]) * mask(2)).astype(bf16)
    serve(7)
    back_m = wide_load(WMIX)
    mix_bias = vec(3)
    for c in range(d // fc):
        serve(16 + c)
        at = slice(c * fc, (c + 1) * fc)
        y[:, at] = (r.x[:, at].astype(f32) + dot_nn(o_v[...], we_v[c].reshape(d, fc)) + mix_bias[:, at]
                    + scale_lora * dot_nn(r.low2[...], r.mix_up[:, at]))

    def load(slot, buf):
        out = [pltpu.make_async_copy(r.ge.at[slot], we_v.at[buf], r.load_sem.at[0, buf, 0])]
        for o in range(members):
            src = g.own[WR](slot) if o == 0 else g.place(WR, slot, o)
            out.append(pltpu.make_async_copy(src, wr_v.at[buf, me ^ o], r.load_sem.at[1, buf, o]))
        return out

    def fetch(slot, buf):
        g.ready(slot, BOTH)
        for cp in load(slot, buf):
            cp.start()

    for cp in back_m:
        cp.wait()
    out_r = pltpu.make_async_copy(y, r.resid, r.out_sem.at[3])
    out_r.start()
    out_a.wait()
    m_v = a_v
    for part in range(2):
        serve(12 + part)
        norm_rows(y, 4, 5, m_v, part)
    serve(8)
    out_m = pltpu.make_async_copy(m_v, r.m, r.out_sem.at[0])
    out_m.start()
    r.low3[...] = (dot_nt(m_v[...], r.exp_dn[...]) * mask(3)).astype(bf16)
    r.e4[...] = (scale_lora * dot_nt(r.dy[...], r.red_up[...]) * mask(4)).astype(bf16)
    dm[...] = jnp.zeros_like(dm)
    r.lowr[...] = jnp.zeros_like(r.lowr)
    r.er[...] = jnp.zeros_like(r.er)
    out_r.wait()
    y[...] += vec(6)

    def g_out(j, buf):
        return (pltpu.make_async_copy(r.gup_st.at[buf], r.gup.at[:, j], r.g_sem.at[0, buf]),
                pltpu.make_async_copy(r.gdn_st.at[buf], r.gdn.at[:, j], r.g_sem.at[1, buf]))

    serve(9)
    fetch(MLP_ORDER[0], 0)

    def step(n, _):
        for i in range(SLOTS):
            if 60 + 2 * i in SERVE:
                pl.when(n == i)(lambda i=i: serve(60 + 2 * i))
        buf = lax.rem(n, 2)
        slot = jnp.int32(0)
        for i, q in enumerate(MLP_ORDER):
            slot = jnp.where(n == i, q, slot)
        for cp in load(slot, buf):
            cp.wait()
        j = chunk_of(slot, parity)
        we = we_v[buf].reshape(d, fc)
        wr = wr_v[buf].reshape(fc, d)
        if z.aligned:
            def cut(ref):
                return jnp.concatenate([ref[:, pl.ds(pl.multiple_of(s * (z.ff // members) + j * sub, sub), sub)]
                                        for s in range(members)], axis=1)
            bup, adn = cut(r.exp_up), cut(r.red_dn)
        else:
            bup, adn = r.exp_up[j], r.red_dn[j]
        be = jnp.zeros((1, fc), f32)
        for i in range(SLOTS):
            lo = z.be_at + i * sub
            row = jnp.concatenate([sm[s, :, lo : lo + sub] for s in range(members)], axis=1)
            be = jnp.where(j == i, row, be)
        hid = dot_nn(m_v[...], we) + be
        hid = hid + scale_lora * dot_nn(r.low3[...], bup)
        cube = hid * hid * hid
        t = jnp.tanh(gelu_c * (hid + 0.044715 * cube))
        act = (0.5 * hid * (1.0 + t)).astype(bf16)
        slope = 0.5 * (1.0 + t) + 0.5 * hid * (1.0 - t * t) * (
            gelu_c * (1.0 + 3.0 * 0.044715 * hid * hid)
        )
        dact = dot_nt(r.dy[...], wr) + dot_nn(r.e4[...], adn)
        dh = (dact * slope).astype(bf16)
        for i in range(SLOTS):
            def middle(i=i):
                serve(61 + 2 * i)
                if i + 1 < SLOTS:
                    fetch(MLP_ORDER[i + 1], (i + 1) % 2)
            pl.when(n == i)(middle)
        y[...] += dot_nn(act, wr)
        dm[...] += dot_nt(dh, we)
        r.lowr[...] += dot_nt(act, adn)
        r.er[...] += dot_nt(dh, bup)
        gup = (scale_lora * dot_tn(r.low3[...], dh)).astype(bf16)
        gdn = dot_tn(r.e4[...], act).astype(bf16)

        @pl.when(n >= 2)
        def _():
            for cp in g_out(j, buf):
                cp.wait()

        for to in range(members):
            r.gup_st[buf, to] = gup[:, to * sub : (to + 1) * sub]
            r.gdn_st[buf, to] = gdn[:, to * sub : (to + 1) * sub]
        for cp in g_out(j, buf):
            cp.start()
        return 0

    lax.fori_loop(0, SLOTS, step, 0)

    low4 = (r.lowr[...] * mask(4)).astype(bf16)
    r.low4[...] = low4
    out_o.wait()
    layer_v = q_v
    for c in range(d // fc):
        at = slice(c * fc, (c + 1) * fc)
        layer_v[:, at] = (y[:, at] + scale_lora * dot_nn(low4, r.red_up[:, at])).astype(bf16)
    out_l = pltpu.make_async_copy(layer_v, r.layer, r.out_sem.at[1])
    out_l.start()
    back_r = pltpu.make_async_copy(r.resid, y, r.out_sem.at[3])
    back_r.start()
    e3 = (scale_lora * r.er[...] * mask(3)).astype(bf16)
    r.e3[...] = e3
    gain = vec(4)
    back_r.wait()

    def last(i, _):
        at = pl.ds(pl.multiple_of(i * 128, 128), 128)
        n, inv = norm_parts(y[at, :])
        dn = dm[at, :] + dot_nn(r.e3[at, :], r.exp_dn[...])
        dm[at, :] = r.dy[at, :].astype(f32) + norm_back(n, inv, gain, dn)
        return 0

    lax.fori_loop(0, length // 128, last, 0)
    out_l.wait()
    out_m.wait()
    for buf in range(2):
        kd_out(buf, buf).wait()
        for cp in g_out(buf, buf):
            cp.wait()
    for o in range(1, members):
        small_copy(o).wait_send()
        kv_copy(o).wait_send()
    g.finish()


def forward(z, args):
    vm = pl.BlockSpec(memory_space=pltpu.VMEM)
    hbm = pl.BlockSpec(memory_space=pl.ANY)
    m, n, d, rk, w = z.members, z.length, z.d, z.rk, z.w
    s = jax.ShapeDtypeStruct
    half = z.rows // 2
    outs = dict(
        dres=s((n, d), f32), put=s((m, z.cap, n), bf16), slot=s((m, 1, n), jnp.int32),
        info=s((m, z.cap, 128), f32), chosen=s((n, 128), f32),
        low0=s((n, rk), bf16), low1=s((n, rk), bf16), low2=s((n, rk), bf16), low4=s((n, rk), bf16), e3=s((n, rk), bf16), gain=s((1, d), f32),
        a=s((n, d), bf16), q=s((n, d), bf16), o=s((n, d), bf16), m=s((n, d), bf16), resid=s((n, d), f32),
        kd=s((m, n, w), bf16), gup=s((m, SLOTS, rk, z.sub), bf16), gdn=s((m, SLOTS, rk, z.sub), bf16),
        layer=s((n, d), bf16), kvs=s((m, m, z.cap, w), bf16),
        ge=s((SLOTS, m, z.rows, z.fc), bf16), gr=s((SLOTS, m, z.sub, d), bf16),
        ga=s((2, m, half, d), bf16), gb=s((2, m, half, d), bf16), gk=s((1, m, z.rows, w), bf16))
    in_vmem = 11
    sends = m - 1 + m // 2
    dma = pltpu.SemaphoreType.DMA
    items = 2 * SLOTS + 5
    scratch = dict(
        y=pltpu.VMEM((n, d), f32), dy_v=pltpu.VMEM((n, d), bf16), mix_dn_v=pltpu.VMEM((rk, d), bf16),
        mix_up_v=pltpu.VMEM((rk, d), bf16), exp_dn_v=pltpu.VMEM((rk, d), bf16),
        exp_up_v=pltpu.VMEM(args.exp_up.shape, bf16), red_dn_v=pltpu.VMEM(args.exp_up.shape, bf16),
        red_up_v=pltpu.VMEM((rk, d), bf16), late_sem=dma((7,)), we_v=pltpu.VMEM((2, m, z.rows, z.fc), bf16), wr_v=pltpu.VMEM((2, m, z.sub, d), bf16),
        a_v=pltpu.VMEM((n, d), bf16), q_v=pltpu.VMEM((n, d), bf16),
        kvp=pltpu.VMEM((m, z.cap, w), bf16), kvb=pltpu.VMEM((2, m, z.cap, w), bf16),
        kd_st=pltpu.VMEM((2, n, w), bf16), gup_st=pltpu.VMEM((2, m, rk, z.sub), bf16),
        gdn_st=pltpu.VMEM((2, m, rk, z.sub), bf16), sm=pltpu.VMEM((m, 1, z.small_cols), f32),
        lowr=pltpu.VMEM((n, rk), f32), er=pltpu.VMEM((n, rk), f32), low3=pltpu.VMEM((n, rk), bf16), e4=pltpu.VMEM((n, rk), bf16),
        send_sem=dma((items, sends)), recv_sem=dma((items, m)), sm_send=dma((m,)), sm_recv=dma((m,)),
        kv_send=dma((m,)), kv_recv=dma((m,)), stage_sem=dma((SLOTS,)), store_sem=dma((SLOTS,)),
        load_sem=dma((2, 2, m)), kvb_sem=dma((2,)), kd_sem=dma((2,)), g_sem=dma((2, 2)), out_sem=dma((4,)))
    got = pl.pallas_call(
        lambda *refs: fwd_kernel(z, *refs),
        in_specs=[vm] * 17 + [hbm] * 12,
        out_specs=[vm] * in_vmem + [hbm] * (len(FwdOut._fields) - in_vmem),
        out_shape=list(FwdOut(**outs)),
        scratch_shapes=list(FwdScratch(**scratch)),
        compiler_params=pltpu.CompilerParams(
            vmem_limit_bytes=FWD_VMEM, collective_id=1, has_side_effects=True),
    )(*args)
    return FwdOut(*got)


FWD_VMEM = 62 * 1024 * 1024


HALVE, PLANE, SCATTER, COLLECT = range(4)


class Job:
    def __init__(self, members, replicas, work, got, out, send_sem, recv_sem, turn, direct):
        self.me, self.rep = lax.axis_index("shard"), lax.axis_index("rep")
        self.work, self.got, self.out = work, got, out
        self.send_sem, self.recv_sem = send_sem, recv_sem
        self.size = work.shape[2] // replicas
        bits = [1 << i for i in range(members.bit_length() - 1)]
        bits = bits if turn == 0 else bits[:1] + bits[1:][::-1]
        self.stages = []
        at, decided = 0, 0
        for b in bits[:1] if direct else bits:
            free = [f for f in range(members) if not f & (decided | b)]
            self.stages.append((HALVE, at, free, b, decided))
            at += len(free)
            decided |= b
        if direct:
            self.stages.append((PLANE, at, list(range(2, members, 2)), 0, 0))
            at += members // 2 - 1
        turns = list(range(1, replicas))
        self.stages.append((SCATTER, at, turns, at, 0))
        self.stages.append((COLLECT, at + len(turns), turns, at + 1, 0))
        self.count = len(self.stages)

    def rows(self, rep):
        return pl.ds(pl.multiple_of(rep * self.size, self.size), self.size)

    def copy(self, i, n):
        kind, at, items, b, decided = self.stages[i]
        item = items[n]
        if kind == HALVE:
            src = self.work.at[item | (self.me & decided) | ((self.me ^ b) & b)]
            dst, to = self.got.at[at + n], (self.me ^ b, self.rep)
        elif kind == PLANE:
            src, dst, to = self.work.at[self.me ^ item], self.got.at[at + n], (self.me ^ item, self.rep)
        else:
            src = self.work.at[self.me, :, self.rows(self.rep ^ item if kind == SCATTER else self.rep)]
            dst = self.got.at[b, :, n * self.size : (n + 1) * self.size]
            to = (self.me, self.rep ^ item)
        return pltpu.make_async_remote_copy(
            src, dst, self.send_sem.at[at + n], self.recv_sem.at[at + n], device_id=to, device_id_type=MESH)

    def start(self, i):
        for n in range(len(self.stages[i][2])):
            self.copy(i, n).start()

    def add(self, i):
        kind, at, items, b, decided = self.stages[i]
        for n in range(len(items)):
            cp = self.copy(i, n)
            cp.wait_recv()
            cp.wait_send()
        if kind == HALVE:
            for n, item in enumerate(items):
                keep = item | (self.me & decided) | (self.me & b)
                self.work[keep] = (self.work[keep].astype(f32) + self.got[at + n].astype(f32)).astype(bf16)
        elif kind == PLANE:
            total = self.work[self.me].astype(f32)
            for n in range(len(items)):
                total = total + self.got[at + n].astype(f32)
            self.work[self.me] = total.astype(bf16)
        elif kind == SCATTER:
            near = self.rows(self.rep)
            total = self.work[self.me, :, near].astype(f32)
            for n in range(len(items)):
                total = total + self.got[b, :, n * self.size : (n + 1) * self.size].astype(f32)
            self.work[self.me, :, near] = total.astype(bf16)
        else:
            for n, item in enumerate(items):
                self.work[self.me, :, self.rows(self.rep ^ item)] = self.got[b, :, n * self.size : (n + 1) * self.size]
            blocks, lanes = self.work.shape[1], self.work.shape[3]
            for j in range(blocks):
                self.out[:, j * lanes : (j + 1) * lanes] = self.work[self.me, j].astype(f32)

    def move(self, i):
        self.add(i)
        if i + 1 < self.count:
            self.start(i + 1)


class BwdIn(NamedTuple):
    dres: object
    put: object
    slot: object
    info: object
    chosen: object
    low0: object
    low1: object
    low2: object
    low4: object
    e3: object
    gain: object
    mix_dn: object
    mix_up: object
    q_dn: object
    q_up: object
    kv_dn: object
    kv_up: object
    ga: object
    gb: object
    gk: object
    q: object
    a: object
    o: object
    m: object
    dy: object
    x: object
    kd: object
    gup: object
    gdn: object


class BwdOut(NamedTuple):
    dx: object
    ja_out: object
    jb_out: object
    jc_out: object
    jd_out: object
    je_out: object
    jf_out: object
    jg_out: object


class BwdScratch(NamedTuple):
    w_v: object
    wk_v: object
    t1: object
    t2: object
    q_v: object
    do_v: object
    dq: object
    kd_st: object
    ds_st: object
    dk_r: object
    w_sem: object
    t_sem: object
    g_sem: object
    kd_sem: object
    dk_send: object
    dk_recv: object
    out_sem: object
    ja_w: object
    ja_g: object
    ja_s: object
    ja_r: object
    jb_w: object
    jb_g: object
    jb_s: object
    jb_r: object
    jc_w: object
    jc_g: object
    jc_s: object
    jc_r: object
    jd_w: object
    jd_g: object
    jd_s: object
    jd_r: object
    je_w: object
    je_g: object
    je_s: object
    je_r: object
    jf_w: object
    jf_g: object
    jf_s: object
    jf_r: object
    jg_w: object
    jg_g: object
    jg_s: object
    jg_r: object


class BwdRefs(NamedTuple):
    dres: object
    put: object
    slot: object
    info: object
    chosen: object
    low0: object
    low1: object
    low2: object
    low4: object
    e3: object
    gain: object
    mix_dn: object
    mix_up: object
    q_dn: object
    q_up: object
    kv_dn: object
    kv_up: object
    ga: object
    gb: object
    gk: object
    q: object
    a: object
    o: object
    m: object
    dy: object
    x: object
    kd: object
    gup: object
    gdn: object
    dx: object
    ja_out: object
    jb_out: object
    jc_out: object
    jd_out: object
    je_out: object
    jf_out: object
    jg_out: object
    w_v: object
    wk_v: object
    t1: object
    t2: object
    q_v: object
    do_v: object
    dq: object
    kd_st: object
    ds_st: object
    dk_r: object
    w_sem: object
    t_sem: object
    g_sem: object
    kd_sem: object
    dk_send: object
    dk_recv: object
    out_sem: object
    ja_w: object
    ja_g: object
    ja_s: object
    ja_r: object
    jb_w: object
    jb_g: object
    jb_s: object
    jb_r: object
    jc_w: object
    jc_g: object
    jc_s: object
    jc_r: object
    jd_w: object
    jd_g: object
    jd_s: object
    jd_r: object
    je_w: object
    je_g: object
    je_s: object
    je_r: object
    jf_w: object
    jf_g: object
    jf_s: object
    jf_r: object
    jg_w: object
    jg_g: object
    jg_s: object
    jg_r: object


def job_shapes(z):
    wide = z.rows // min(128, z.rows)
    lanes = min(128, z.rows)
    chunks = (SLOTS, z.sub) if z.aligned else (SLOTS * z.sub // 128, 128)
    return (chunks, chunks, (2 * wide, lanes), (2 * wide, lanes), (wide, lanes), (wide, lanes), (wide + 1, lanes))


def bwd_kernel(z, *refs):
    r = BwdRefs(*refs)
    members, replicas, rows, fc, d, hd = z.members, z.replicas, z.rows, z.fc, z.d, z.hd
    length, cap, w, heads, rk = z.length, z.cap, z.w, z.heads, z.rk
    me, rep = lax.axis_index("shard"), lax.axis_index("rep")
    half = rows // 2
    halves = d // fc
    w_v, t1, t2, q_v, do_v, dq, dres = r.w_v, r.t1, r.t2, r.q_v, r.do_v, r.dq, r.dres
    outs = refs[len(BwdIn._fields) + 1 : len(BwdIn._fields) + len(BwdOut._fields)]
    held = refs[-4 * len(outs) :]
    ja, jb, jc, jd, je, jf, jg = (
        Job(members, replicas, held[4 * i], held[4 * i + 1], out, held[4 * i + 2], held[4 * i + 3], i % 2, i >= 4)
        for i, out in enumerate(outs))

    barrier = pltpu.get_barrier_semaphore()
    others = [(me ^ o, rep) for o in range(1, members)] + [(me, rep ^ o) for o in range(1, replicas)]
    for to in others:
        pl.semaphore_signal(barrier, inc=1, device_id=to, device_id_type=MESH)

    def local(src, dst, sem):
        return pltpu.make_async_copy(src, dst, sem)

    def wide(which):
        return [local(part.at[which, :, :, c * fc : (c + 1) * fc],
                      w_v.at[c, :, h * half : (h + 1) * half], r.w_sem.at[h, c])
                for h, part in enumerate((r.ga, r.gb)) for c in range(halves)]

    load_up = local(r.gup, r.ja_w, r.g_sem.at[0])
    load_dn = local(r.gdn, r.jb_w, r.g_sem.at[1])
    load_up.start()
    load_dn.start()
    mix = wide(WMIX)
    for cp in mix:
        cp.start()
    load_m = local(r.m, t1, r.t_sem.at[0])
    load_dy = local(r.dy, t2, r.t_sem.at[1])
    load_q = local(r.q, q_v, r.t_sem.at[2])
    load_k = local(r.gk.at[0], r.wk_v, r.t_sem.at[3])
    for cp in (load_m, load_dy, load_q, load_k):
        cp.start()
    pl.semaphore_wait(barrier, len(others))
    load_up.wait()
    ja.start(0)
    load_dn.wait()
    jb.start(0)

    rank_of = (lax.broadcasted_iota(jnp.int32, (length, rk), 1) // z.rank).astype(f32)

    def mask(p):
        return jnp.where(rank_of == r.chosen[:, 2 + p : 3 + p], 1.0, 0.0)

    def terms(job, block, left, right, sc):
        lanes = job.work.shape[3]
        g = dot_tn(left, right) * sc
        width = right.shape[1] // members
        for to in range(members):
            for i in range(-(-width // lanes)):
                part = g[:, to * width + i * lanes : to * width + min((i + 1) * lanes, width)]
                if part.shape[1] < lanes:
                    part = jnp.concatenate([part, jnp.zeros((rk, lanes - part.shape[1]), f32)], axis=1)
                job.work[to, block + i] = part.astype(bf16)

    per = r.jc_w.shape[1] // 2

    dresl = do_v
    dresl[...] = dres[...].astype(bf16)
    e2 = (scale_lora * dot_nt(dresl[...], r.mix_up[...]) * mask(2)).astype(bf16)
    terms(jd, per, r.low2[...], dresl[...], scale_lora)
    load_m.wait()
    terms(jc, 0, r.e3[...], t1[...], 1.0)
    load_o = local(r.o, t1, r.t_sem.at[0])
    load_o.start()
    load_dy.wait()
    terms(jd, 0, r.low4[...], t2[...], scale_lora)
    load_x = local(r.x, t2, r.t_sem.at[1])
    load_x.start()
    jd.start(0)
    for cp in mix:
        cp.wait()
    ja.move(0)
    dq[...] = dot_nt(dresl[:, 0:fc], w_v[0].reshape(d, fc)) + dot_nn(e2, r.mix_dn[...])
    jb.move(0)
    for c in range(1, halves):
        dq[...] += dot_nt(dresl[:, c * fc : (c + 1) * fc], w_v[c].reshape(d, fc))
    do_v[...] = dq[...].astype(bf16)
    query = wide(WQ)
    for cp in query:
        cp.start()
    load_o.wait()
    terms(jc, per, e2, t1[...], 1.0)
    jc.start(0)
    load_a = local(r.a, t1, r.t_sem.at[0])
    load_a.start()
    jd.move(0)
    dq[...] = jnp.zeros_like(dq)
    load_q.wait()

    def kd_load(k, buf):
        return local(r.kd.at[k], r.kd_st.at[buf], r.kd_sem.at[buf])

    def ds_copy(k, buf, o):
        return pltpu.make_async_remote_copy(
            r.ds_st.at[buf, me ^ o], r.dk_r.at[me, k], r.dk_send.at[buf, o], r.dk_recv.at[o],
            device_id=(me ^ o, rep), device_id_type=MESH)

    kd_load(0, 0).start()
    groups = 4
    sc = hd ** (-0.5)
    plan = ((), (), ((jc, 0),), (), ((ja, 1), (jb, 1), (jd, 1)), (), ((jc, 1), (ja, 2), (jb, 2)), ((jd, 2),))


    def act(some):
        for job, i in some:
            job.move(i)

    def attend(k, _):
        buf = lax.rem(k, 2)

        @pl.when(k + 1 < members)
        def _():
            kd_load(k + 1, 1 - buf).start()

        for i, some in enumerate(plan):
            pl.when(k == i)(lambda some=some: act(some))
        kd_load(k, buf).wait()
        kvd = r.kd_st[buf]
        kd, vd = kvd[:, :hd], kvd[:, hd:]
        put = r.put[k]
        qp = dot_nn(put, q_v[...]).astype(bf16)
        dop = dot_nn(put, do_v[...]).astype(bf16)
        info = r.info[k]
        n = heads // groups
        dqs = []
        dk = jnp.zeros((length, hd), f32)
        dv = jnp.zeros((length, hd), f32)
        for h in range(groups):
            at = slice(h * n * hd, (h + 1) * n * hd)
            qr, dor = to_rows(qp[:, at], n), to_rows(dop[:, at], n)
            p = softmax_rows(qr, kd, info, n)
            dp = dot_nt(dor, vd)
            ds = (p * (dp - jnp.sum(dp * p, axis=1, keepdims=True))).astype(bf16)
            dqs.append(to_cols((dot_nn(ds, kd) * sc).astype(bf16), n))
            dk = dk + dot_tn(ds, qr)
            dv = dv + dot_tn(p.astype(bf16), dor)
        dq[...] += dot_tn(put, jnp.concatenate(dqs, axis=1))
        dkv = jnp.concatenate([dk * sc, dv], axis=1).astype(bf16)
        slots = dot_nn(key_onehot(r.slot[k], z.slots), dkv).astype(bf16).reshape(members, cap, w)

        @pl.when(k >= 2)
        def _():
            for o in range(1, members):
                ds_copy(k, buf, o).wait_send()

        r.ds_st[buf] = slots
        r.dk_r[me, k] = r.ds_st[buf, me]
        for o in range(1, members):
            ds_copy(k, buf, o).start()
        return 0

    lax.fori_loop(0, members, attend, 0)

    following = {ja: 3, jb: 3, jc: 2, jd: 3, je: 0, jf: 0, jg: 0}

    def go(*jobs):
        for job in jobs:
            if following[job] < job.count:
                job.move(following[job])
                following[job] += 1

    go(ja, jb)
    q_v[...] = dq[...].astype(bf16)
    e0 = (scale_lora * dot_nt(q_v[...], r.q_up[...]) * mask(0)).astype(bf16)
    load_a.wait()
    terms(je, 0, e0, t1[...], 1.0)
    je.start(0)
    terms(jf, 0, r.low0[...], q_v[...], scale_lora)
    jf.start(0)
    for o in range(1, members):
        local(r.dk_r.at[me ^ o], r.dk_r.at[me ^ o], r.dk_recv.at[o]).wait()
    go(jd, jc)
    dkv = jnp.zeros((length, w), f32)
    for k in range(members):
        total = r.dk_r[0, k].astype(f32)
        for s in range(1, members):
            total = total + r.dk_r[s, k].astype(f32)
        dkv = dkv + dot_tn(r.put[k], total.astype(bf16))
    dkv = dkv.astype(bf16)
    go(je, jf)
    e1 = (scale_lora * dot_nt(dkv, r.kv_up[...]) * mask(1)).astype(bf16)
    terms(jg, 0, e1, t1[...], 1.0)
    terms(jg, per, r.low1[...], dkv, scale_lora)
    jg.start(0)
    load_k.wait()
    dq[...] = (dot_nn(e0, r.q_dn[...]) + dot_nn(e1, r.kv_dn[...])
               + dot_nt(dkv, r.wk_v[...].reshape(d, w)))
    go(jd, jc, je, jf, jg)
    for cp in query:
        cp.wait()
    for c in range(halves):
        dq[...] += dot_nt(q_v[:, c * fc : (c + 1) * fc], w_v[c].reshape(d, fc))
        go(je, jf, jg)
    load_x.wait()
    gain = r.gain[...]

    def back(i, _):
        at = pl.ds(pl.multiple_of(i * 128, 128), 128)
        n, inv = norm_parts(t2[at, :].astype(f32))
        do_v[at, :] = (dres[at, :] + norm_back(n, inv, gain, dq[at, :])).astype(bf16)
        return 0

    for part in range(2):
        lax.fori_loop(part * length // 256, (part + 1) * length // 256, back, 0)
        go(je, jf, jg)
    out = local(do_v, r.dx, r.out_sem)
    out.start()
    while any(following[job] < job.count for job in following):
        go(ja, jb, jc, jd, je, jf, jg)
    out.wait()
    for buf in range(2):
        for o in range(1, members):
            ds_copy(buf, buf, o).wait_send()


def backward(z, args):
    vm = pl.BlockSpec(memory_space=pltpu.VMEM)
    hbm = pl.BlockSpec(memory_space=pl.ANY)
    m, n, d, rk, w = z.members, z.length, z.d, z.rk, z.w
    s = jax.ShapeDtypeStruct
    dma = pltpu.SemaphoreType.DMA
    shapes = job_shapes(z)
    legs = m - 1 + 2
    sems = m - 1 + 2 * (z.replicas - 1)
    scratch = dict(
        w_v=pltpu.VMEM((d // z.fc, m, z.rows, z.fc), bf16), wk_v=pltpu.VMEM((m, z.rows, w), bf16),
        t1=pltpu.VMEM((n, d), bf16), t2=pltpu.VMEM((n, d), bf16), q_v=pltpu.VMEM((n, d), bf16), do_v=pltpu.VMEM((n, d), bf16),
        dq=pltpu.VMEM((n, d), f32), kd_st=pltpu.VMEM((2, n, w), bf16), ds_st=pltpu.VMEM((2, m, z.cap, w), bf16),
        dk_r=pltpu.VMEM((m, m, z.cap, w), bf16),
        w_sem=dma((2, d // z.fc)), t_sem=dma((4,)), g_sem=dma((2,)), kd_sem=dma((2,)), dk_send=dma((2, m)),
        dk_recv=dma((m,)), out_sem=dma(()))
    scratch = [scratch[k] for k in BwdScratch._fields[: len(scratch)]]
    job_outs = [s((rk, blocks * lanes), f32) for blocks, lanes in shapes]
    job_scratch = [x for blocks, lanes in shapes for x in (
        pltpu.VMEM((m, blocks, rk, lanes), bf16), pltpu.VMEM((legs, blocks, rk, lanes), bf16), dma((sems,)), dma((sems,)))]
    first_hbm = 17
    got = pl.pallas_call(
        lambda *refs: bwd_kernel(z, *refs),
        in_specs=[vm] * first_hbm + [hbm] * (len(BwdIn._fields) - first_hbm),
        out_specs=[hbm] + [vm] * len(shapes),
        out_shape=[s((n, d), bf16)] + job_outs,
        scratch_shapes=scratch + job_scratch,
        compiler_params=pltpu.CompilerParams(
            vmem_limit_bytes=FWD_VMEM, collective_id=2, has_side_effects=True),
    )(*BwdIn(**args))
    return BwdOut(*got)


def final(sums, z, experts, rank):
    c, n = z.rows, z.w // z.members
    ff = z.ff // z.members
    cuts = ((4, 0, c), (5, 0, c), (6, 0, c), (6, c, n), (2, c, c), (3, c, c), (2, 0, c), (0, 0, ff), (1, 0, ff), (3, 0, c))

    def kernel(*refs):
        for (job, at, width), out in zip(cuts, refs[len(sums):]):
            out[...] = refs[job][:, at : at + width].reshape(experts, rank, width)

    vm = pl.BlockSpec(memory_space=pltpu.VMEM)
    return pl.pallas_call(
        kernel, in_specs=[vm] * len(sums), out_specs=[vm] * len(cuts),
        out_shape=[jax.ShapeDtypeStruct((experts, rank, w), f32) for _, _, w in cuts])(*sums)


def local(tokens, out_grad, token_perm, seq_lens, adapter_ids,
          attn_g, attn_b, wq, bq, wkv, bv, wmix, bmix, mlp_g, mlp_b, wexp, bexp, wred, bred,
          q_dn, q_up, kv_dn, kv_up, mix_dn, mix_up, exp_dn, exp_up, red_dn, red_up):
    members = lax.axis_size("shard")
    replicas = lax.axis_size("rep")
    rep = lax.axis_index("rep")
    length, d = tokens.shape
    experts, rank = q_dn.shape[:2]
    rk = experts * rank
    z = Sizes(members, replicas, length, d, wexp.shape[1], bv.shape[0] * members, rk, rank,
              seq_lens.shape[1], adapter_ids.shape[2])
    flat = lambda s: s.reshape(rk, s.shape[2])
    q_dn, q_up, kv_dn, kv_up, mix_dn, mix_up, exp_dn, exp_up, red_dn, red_up = map(
        flat, (q_dn, q_up, kv_dn, kv_up, mix_dn, mix_up, exp_dn, exp_up, red_dn, red_up))
    group = lax.dynamic_index_in_dim(
        token_perm.reshape(members, replicas, length), rep, 1, keepdims=False)

    by_chunk = lambda s: s.reshape(s.shape[0], members, SLOTS, z.sub).transpose(2, 0, 1, 3).reshape(
        SLOTS, s.shape[0], z.fc)
    chunked = (lambda s: s) if z.aligned else by_chunk
    got = forward(z, FwdIn(
        x=tokens, dy=out_grad, attn_g=attn_g, attn_b=attn_b, bq=bq, bmix=bmix, mlp_g=mlp_g, mlp_b=mlp_b, bred=bred, bexp=bexp, bv=bv,
        lens=seq_lens, ids=adapter_ids, group=group,
        q_dn=q_dn, q_up=q_up, kv_dn=kv_dn, kv_up=kv_up, mix_dn=mix_dn, mix_up=mix_up, exp_dn=exp_dn,
        exp_up=chunked(exp_up), red_dn=chunked(red_dn), red_up=red_up,
        wq=wq, wkv=wkv, wmix=wmix, wexp=chunked(wexp), wred=wred.reshape(SLOTS, z.sub, d)))
    gup, gdn = got.gup, got.gdn
    if not z.aligned:
        pack = 128 // z.sub
        gup, gdn = (g.reshape(members, SLOTS // pack, pack, rk, z.sub).transpose(0, 1, 3, 2, 4).reshape(
            members, SLOTS // pack, rk, 128) for g in (gup, gdn))
    back = backward(z, dict(
        dres=got.dres, put=got.put, slot=got.slot, info=got.info, chosen=got.chosen, low0=got.low0, low1=got.low1,
        low2=got.low2, low4=got.low4, e3=got.e3, gain=got.gain, ga=got.ga, gb=got.gb, gk=got.gk, q=got.q, a=got.a,
        o=got.o, m=got.m, kd=got.kd, gup=gup, gdn=gdn,
        mix_dn=mix_dn, mix_up=mix_up, q_dn=q_dn, q_up=q_up, kv_dn=kv_dn, kv_up=kv_up, dy=out_grad, x=tokens))
    g = final(back[1:], z, experts, rank)
    return (got.layer, back.dx, *g)


def solution(mesh):
    both = ("shard", "rep")
    row, vec = P("shard", None), P("shard")
    in_specs = (
        P(both, None), P(both, None), P(), P(both, None), P(both, None, None),
        vec, vec, row, vec, row, vec, row, vec, vec, vec, row, vec, row, vec,
    ) + (P(),) * 10
    out_specs = (P(both, None), P(both, None)) + (P(None, None, "shard"),) * 10
    return jax.shard_map(local, mesh=mesh, in_specs=in_specs, out_specs=out_specs, check_vma=False)
```

```python
import jax
import jax.numpy as jnp
from jax import lax
from jax.experimental import pallas as pl
from jax.experimental.pallas import tpu as pltpu
from jax.sharding import PartitionSpec as P
from typing import NamedTuple

scale_lora = 0.5
eps = 1e-05
f32 = jnp.float32
bf16 = jnp.bfloat16
neg_big = -1e30
log2_e = 1.4426950408889634
gelu_c = 0.7978845608028654
VMEM_LIMIT = 60 * 1024 * 1024


def dot_nn(a, b):
    return lax.dot_general(a, b, (((1,), (0,)), ((), ())), preferred_element_type=f32)


def dot_nt(a, b):
    return lax.dot_general(a, b, (((1,), (1,)), ((), ())), preferred_element_type=f32)


def dot_tn(a, b):
    return lax.dot_general(a, b, (((0,), (0,)), ((), ())), preferred_element_type=f32)


def key_onehot(slot_row, slots):
    ids = lax.broadcasted_iota(jnp.int32, (slots, slot_row.shape[1]), 0)
    return jnp.where(ids == slot_row, 1.0, 0.0).astype(bf16)


def to_rows(x, heads):
    hd = x.shape[1] // heads
    return jnp.concatenate([x[:, h * hd : (h + 1) * hd] for h in range(heads)], axis=0)


def to_cols(x, heads):
    c = x.shape[0] // heads
    return jnp.concatenate([x[h * c : (h + 1) * c] for h in range(heads)], axis=1)


def softmax_rows(qr, kd, span, heads):
    rows, keys = qr.shape[0], kd.shape[0]
    c = rows // heads
    u = lax.broadcasted_iota(jnp.int32, (c, keys), 1).astype(f32)
    allowed = (u >= span[:, 0:1]) & (u <= span[:, 1:2])
    s = jnp.where(allowed[None], dot_nt(qr, kd).reshape(heads, c, keys), neg_big)
    top = jnp.max(s, axis=2, keepdims=True)
    e = jnp.exp2((s - top) * (kd.shape[1] ** (-0.5) * log2_e))
    p = e * (1.0 / jnp.sum(e, axis=2, keepdims=True))
    return p.reshape(rows, keys)


MESH = pl.DeviceIdType.MESH


class Gather:
    def __init__(self, members, own, full, slots, send_sem, recv_sem):
        self.members = members
        self.me, self.rep = lax.axis_index("shard"), lax.axis_index("rep")
        self.own, self.full = own, full
        self.base = [sum(slots[:i]) for i in range(len(slots))]
        self.send_sem, self.recv_sem = send_sem, recv_sem
        self.bits = [1 << i for i in range(1, members.bit_length() - 1)]
        self.planes = list(range(0, members, 2))
        self.sent = {}

    def place(self, kind, slot, offset):
        return self.full[kind].at[slot, self.me ^ offset]

    def copy(self, kind, slot, offset, there, to, to_slot):
        mine = self.sent.setdefault((kind, slot), {})
        at = mine.setdefault((offset, there, to_slot), len(mine))
        src = self.own[kind](slot) if offset == 0 else self.place(kind, slot, offset)
        pltpu.make_async_remote_copy(
            src, self.full[kind].at[to_slot, self.me ^ offset],
            self.send_sem.at[self.base[kind] + slot, at],
            self.recv_sem.at[self.base[kind] + to_slot, there],
            device_id=to, device_id_type=MESH).start()

    def wait(self, kind, slot, offset):
        piece = self.place(kind, slot, offset)
        pltpu.make_async_copy(piece, piece, self.recv_sem.at[self.base[kind] + slot, offset]).wait()

    def order(self, kind):
        return self.bits if kind % 2 == 0 else self.bits[::-1]

    def stage(self, kind, offset):
        return max(i for i, b in enumerate(self.order(kind)) if offset & b)

    def issue(self, slot, kinds, plane=True):
        for kind in kinds:
            if plane:
                for b in self.order(kind):
                    self.copy(kind, slot, 0, b, (self.me ^ b, self.rep), slot)
            self.copy(kind, slot, 0, 1, (self.me ^ 1, self.rep), slot)

    def arrive(self, slot, kinds, direct, swap_to=None):
        for kind in kinds:
            order = self.order(kind)
            some = [o for o in self.planes if o and (bin(o).count("1") == 1) == direct]
            some.sort(key=lambda o: self.stage(kind, o))
            for o in some:
                self.wait(kind, slot, o)
                for i in range(self.stage(kind, o) + 1, len(order)):
                    self.copy(kind, slot, o, o ^ order[i], (self.me ^ order[i], self.rep), slot)
                if swap_to is not None:
                    self.copy(kind, slot, o, o, (self.me, self.rep ^ 1), swap_to)
                self.copy(kind, slot, o, o ^ 1, (self.me ^ 1, self.rep), slot)

    def swapped(self, slot, kinds):
        for kind in kinds:
            for o in self.planes[1:]:
                self.wait(kind, slot, o)
                self.copy(kind, slot, o, o ^ 1, (self.me ^ 1, self.rep), slot)

    def ready(self, slot, kinds):
        for kind in kinds:
            for o in range(1, self.members, 2):
                self.wait(kind, slot, o)

    def finish(self):
        for (kind, slot), mine in self.sent.items():
            piece = self.place(kind, slot, 0)
            for at in mine.values():
                pltpu.make_async_copy(piece, piece, self.send_sem.at[self.base[kind] + slot, at]).wait()


U, V, C = (0, 1, 2), (3, 4, 5), (6, 7)
SLOTS = 8
WE, WR, AT, AB, KV = range(5)
BOTH, HALVES = (WE, WR), (AT, AB)
WQ, WMIX = 0, 1
SEND, NEAR, FAR, SWAP = range(4)
MLP_ORDER = (0, 1, 4, 3, 2, 6, 5, 7)
SERVE = {
    0: ((SEND, KV, 0),),
    1: ((SEND, WR, 0),),
    10: ((NEAR, KV, 0),),
    21: ((SEND, WE, 0),),
    24: ((NEAR, WR, 0),),
    25: ((FAR, KV, 0),),
    2: ((SEND, AT, 0),),
    4: ((NEAR, WE, 0),),
    5: ((FAR, WR, 0), (NEAR, AT, 0), (SEND, AB, 0), (FAR, WE, 0), (SEND, WE, 1), (SWAP, WR, 3), (FAR, AT, 0), (SEND, AB, 1), (SWAP, WE, 3), (NEAR, AB, 0), (NEAR, WE, 1), (SEND, AT, 1), (FAR, AB, 0),),
    15: ((NEAR, AB, 1),),
    41: ((FAR, WE, 1), (SEND, WR, 1),),
    43: ((FAR, AB, 1),),
    44: ((NEAR, AT, 1), (SEND, WE, 2), (SWAP, WE, 4),),
    46: ((NEAR, WR, 1),),
    7: ((FAR, AT, 1),),
    16: ((SEND, WR, 2),),
    17: ((FAR, WR, 1),),
    12: ((NEAR, WE, 2),),
    13: ((SEND, WR, 6),),
    60: ((NEAR, WR, 2),),
    61: ((SWAP, WR, 4),),
    62: ((FAR, WE, 2), (SEND, WE, 6),),
    63: ((FAR, WR, 2),),
    64: ((NEAR, WR, 6), (SEND, WE, 7),),
    66: ((NEAR, WE, 6),),
    67: ((FAR, WR, 6), (SEND, WR, 7),),
    69: ((NEAR, WE, 7), (FAR, WE, 6), (SWAP, WE, 5),),
    70: ((NEAR, WR, 7), (SWAP, WR, 5),),
    72: ((FAR, WE, 7), (FAR, WR, 7),),
}


def chunk_of(slot, parity):
    slot = jnp.int32(slot)
    low = jnp.where(slot < 3, slot, slot + 2)
    high = jnp.where(slot < 3, slot + 5, slot - 3)
    return jnp.where(slot >= 6, slot - 3, jnp.where(parity == 0, low, high))


def norm_parts(v):
    center = v - jnp.mean(v, axis=-1, keepdims=True)
    inv = lax.rsqrt(jnp.mean(center * center, axis=-1, keepdims=True) + eps)
    return center * inv, inv


def norm_back(n, inv, gain, dn):
    w = gain * dn
    return (w - jnp.mean(w, axis=-1, keepdims=True)
            - n * jnp.mean(w * n, axis=-1, keepdims=True)) * inv


class Sizes:
    def __init__(self, members, replicas, length, d, ff, hd, rk, rank, seqs, projs):
        self.members, self.replicas, self.length, self.d, self.ff = members, replicas, length, d, ff
        self.hd, self.rk, self.rank, self.seqs, self.projs = hd, rk, rank, seqs, projs
        self.heads = d // hd
        self.cap = 3 * length // (2 * members)
        self.slots = members * self.cap
        self.w = 2 * hd
        self.rows = d // members
        self.sub = ff // members // SLOTS
        self.fc = self.sub * members
        self.aligned = self.sub % 128 == 0
        self.be_at = 7 * self.rows
        self.vb_at = self.be_at + ff // members
        self.len_at = self.vb_at + 128
        self.ids_at = self.len_at + 128
        self.small_cols = self.ids_at + 128


class FwdIn(NamedTuple):
    x: object
    attn_g: object
    attn_b: object
    bq: object
    bmix: object
    mlp_g: object
    mlp_b: object
    bred: object
    bexp: object
    bv: object
    lens: object
    ids: object
    group: object
    q_dn: object
    q_up: object
    kv_dn: object
    kv_up: object
    dy: object
    mix_dn: object
    mix_up: object
    exp_dn: object
    exp_up: object
    red_dn: object
    red_up: object
    wq: object
    wkv: object
    wmix: object
    wexp: object
    wred: object


class FwdOut(NamedTuple):
    dres: object
    put: object
    slot: object
    info: object
    chosen: object
    low0: object
    low1: object
    low2: object
    low4: object
    e3: object
    gain: object
    a: object
    q: object
    o: object
    m: object
    resid: object
    kd: object
    gup: object
    gdn: object
    layer: object
    kvs: object
    ge: object
    gr: object
    ga: object
    gb: object
    gk: object


class FwdScratch(NamedTuple):
    y: object
    dy_v: object
    mix_dn_v: object
    mix_up_v: object
    exp_dn_v: object
    exp_up_v: object
    red_dn_v: object
    red_up_v: object
    late_sem: object
    we_v: object
    wr_v: object
    a_v: object
    q_v: object
    kvp: object
    kvb: object
    kd_st: object
    gup_st: object
    gdn_st: object
    sm: object
    lowr: object
    er: object
    low3: object
    e4: object
    send_sem: object
    recv_sem: object
    sm_send: object
    sm_recv: object
    kv_send: object
    kv_recv: object
    stage_sem: object
    store_sem: object
    load_sem: object
    kvb_sem: object
    kd_sem: object
    g_sem: object
    out_sem: object


class FwdRefs(NamedTuple):
    x: object
    attn_g: object
    attn_b: object
    bq: object
    bmix: object
    mlp_g: object
    mlp_b: object
    bred: object
    bexp: object
    bv: object
    lens: object
    ids: object
    group: object
    q_dn: object
    q_up: object
    kv_dn: object
    kv_up: object
    dy: object
    mix_dn: object
    mix_up: object
    exp_dn: object
    exp_up: object
    red_dn: object
    red_up: object
    wq: object
    wkv: object
    wmix: object
    wexp: object
    wred: object
    dres: object
    put: object
    slot: object
    info: object
    chosen: object
    low0: object
    low1: object
    low2: object
    low4: object
    e3: object
    gain: object
    a: object
    q: object
    o: object
    m: object
    resid: object
    kd: object
    gup: object
    gdn: object
    layer: object
    kvs: object
    ge: object
    gr: object
    ga: object
    gb: object
    gk: object
    y: object
    dy_v: object
    mix_dn_v: object
    mix_up_v: object
    exp_dn_v: object
    exp_up_v: object
    red_dn_v: object
    red_up_v: object
    late_sem: object
    we_v: object
    wr_v: object
    a_v: object
    q_v: object
    kvp: object
    kvb: object
    kd_st: object
    gup_st: object
    gdn_st: object
    sm: object
    lowr: object
    er: object
    low3: object
    e4: object
    send_sem: object
    recv_sem: object
    sm_send: object
    sm_recv: object
    kv_send: object
    kv_recv: object
    stage_sem: object
    store_sem: object
    load_sem: object
    kvb_sem: object
    kd_sem: object
    g_sem: object
    out_sem: object


def fwd_kernel(z, *refs):
    r = FwdRefs(*refs)
    members, rows, fc, sub, d, hd = z.members, z.rows, z.fc, z.sub, z.d, z.hd
    length, cap, w, heads, rk = z.length, z.cap, z.w, z.heads, z.rk
    me, rep = lax.axis_index("shard"), lax.axis_index("rep")
    parity = lax.rem(rep, 2)
    half = rows // 2
    att = (r.wq, r.wmix)
    g = Gather(
        members,
        [lambda s: r.ge.at[s, me],
         lambda s: r.wred.at[chunk_of(s, parity)],
         lambda s: att[s].at[0:half],
         lambda s: att[s].at[half:rows],
         lambda s: r.wkv],
        [r.ge, r.gr, r.ga, r.gb, r.gk],
        [SLOTS, SLOTS, 2, 2, 1], r.send_sem, r.recv_sem)
    we_v, wr_v, sm, y, dm = r.we_v, r.wr_v, r.sm, r.y, r.dres

    def serve(point):
        for op, kind, slot in SERVE.get(point, ()):
            swap_to = slot + 3 if slot in U and kind in BOTH else None
            if op == SEND:
                g.issue(slot, (kind,))
            elif op == SWAP:
                g.swapped(slot, (kind,))
            else:
                g.arrive(slot, (kind,), op == NEAR, swap_to)

    barrier = pltpu.get_barrier_semaphore()
    others = [(me ^ o, rep) for o in range(1, members)] + [(me, rep ^ 1)]
    for to in others:
        pl.semaphore_signal(barrier, inc=1, device_id=to, device_id_type=MESH)

    def stage_copies(slot):
        j = chunk_of(slot, parity)
        to = we_v.at[0, slot]
        if not z.aligned:
            return [pltpu.make_async_copy(r.wexp.at[j], to, r.stage_sem.at[slot])]
        return [pltpu.make_async_copy(
            r.wexp.at[:, pl.ds(pl.multiple_of(s * (z.ff // members) + j * sub, sub), sub)],
            to.at[:, s * sub : (s + 1) * sub], r.stage_sem.at[slot]) for s in range(members)]

    def stored(slot):
        return pltpu.make_async_copy(we_v.at[0, slot], r.ge.at[slot, me], r.store_sem.at[slot])

    def staged(slot):
        pltpu.make_async_copy(we_v.at[0, slot], we_v.at[0, slot], r.stage_sem.at[slot]).wait()
        stored(slot).start()

    for slot in range(SLOTS):
        for cp in stage_copies(slot):
            cp.start()
    pl.semaphore_wait(barrier, len(others))

    def small_copy(o):
        return pltpu.make_async_remote_copy(
            sm.at[me], sm.at[me], r.sm_send.at[o], r.sm_recv.at[o],
            device_id=(me ^ o, rep), device_id_type=MESH)

    serve(0)
    coming = [pltpu.make_async_copy(src, dst, r.late_sem.at[i]) for i, (src, dst) in enumerate((
        (r.mix_dn, r.mix_dn_v), (r.mix_up, r.mix_up_v), (r.dy, r.dy_v), (r.exp_dn, r.exp_dn_v),
        (r.exp_up, r.exp_up_v), (r.red_dn, r.red_dn_v), (r.red_up, r.red_up_v)))]
    for cp in coming:
        cp.start()
    r = r._replace(dy=r.dy_v, mix_dn=r.mix_dn_v, mix_up=r.mix_up_v, exp_dn=r.exp_dn_v, exp_up=r.exp_up_v,
                   red_dn=r.red_dn_v, red_up=r.red_up_v)
    sm[me] = jnp.zeros((1, z.small_cols), f32)
    for i, v in enumerate((r.attn_g, r.attn_b, r.bq, r.bmix, r.mlp_g, r.mlp_b, r.bred)):
        sm[me, :, i * rows : (i + 1) * rows] = v[...].astype(f32).reshape(1, rows)
    sm[me, :, z.be_at : z.vb_at] = r.bexp[...].astype(f32).reshape(1, z.vb_at - z.be_at)
    sm[me, :, z.vb_at : z.vb_at + hd // members] = r.bv[...].astype(f32).reshape(1, hd // members)
    sm[me, :, z.len_at : z.len_at + z.seqs] = r.lens[...].astype(f32)
    for j in range(z.seqs):
        at = z.ids_at + j * z.projs
        sm[me, :, at : at + z.projs] = r.ids[0, j : j + 1, :].astype(f32)
    for o in range(1, members):
        small_copy(o).start()
    serve(1)
    for slot in range(SLOTS):
        staged(slot)
    for slot in range(SLOTS):
        stored(slot).wait()
    for o in range(1, members):
        pltpu.make_async_copy(sm.at[me ^ o], sm.at[me ^ o], r.sm_recv.at[o]).wait()

    def vec(row):
        return jnp.concatenate([sm[s, :, row * rows : (row + 1) * rows] for s in range(members)], axis=1)

    def norm_rows(src, gain, bias, dst, part):
        gv, bv = vec(gain), vec(bias)

        def body(i, _):
            at = pl.ds(pl.multiple_of(i * 128, 128), 128)
            n, _inv = norm_parts(src[at, :].astype(f32))
            dst[at, :] = (n * gv + bv).astype(bf16)
            return 0

        lax.fori_loop(part * length // 256, (part + 1) * length // 256, body, 0)

    for part in range(2):
        serve(10 + part)
        norm_rows(r.x, 0, 1, r.a_v, part)

    r.gain[...] = vec(0)

    t_row = lax.broadcasted_iota(jnp.int32, (1, length), 1)
    before_t = lax.broadcasted_iota(jnp.int32, (length, length), 0) < lax.broadcasted_iota(
        jnp.int32, (length, length), 1)
    c_ids = lax.broadcasted_iota(jnp.int32, (cap, length), 0)
    lane = lax.broadcasted_iota(jnp.int32, (cap, 128), 1)
    span = length * z.replicas
    first = (me * z.replicas + rep) * length
    tf = t_row.astype(f32)
    src_cols = lax.div(r.group[...], span).astype(f32).T
    chosen = jnp.zeros((length, 128), f32)
    for k in range(members):
        serve(20 + k)
        row = r.group[k : k + 1, :]
        src = lax.div(row, span)
        earlier = jnp.where((src_cols[:, k : k + 1] == src.astype(f32)) & before_t, 1.0, 0.0)
        slot_row = src * cap + jnp.sum(earlier, axis=0, keepdims=True).astype(jnp.int32)
        r.slot[k] = slot_row
        hit = slot_row == c_ids + me * cap

        def pick(values):
            return jnp.sum(jnp.where(hit, values, 0.0), axis=1, keepdims=True)

        full = pick(jnp.ones_like(tf))
        tok = pick((row - first + 1).astype(f32)) - 1.0
        put = jnp.where(tok == tf, 1.0, 0.0).astype(bf16)
        r.put[k] = put
        end = jnp.zeros((1, 1), f32)
        start = jnp.zeros_like(tf)
        ids = [jnp.zeros_like(tf) for _ in range(z.projs)]
        for j in range(z.seqs):
            n = sm[k, :, z.len_at + j : z.len_at + j + 1]
            inside = (tf >= end) & (tf < end + n)
            end = end + n
            start = start + jnp.where(tf >= end, n, 0.0)
            for p in range(z.projs):
                at = z.ids_at + j * z.projs + p
                ids[p] = ids[p] + jnp.where(inside, sm[k, :, at : at + 1], 0.0)
        info = jnp.where(lane == 0, pick(start) + (1.0 - full), 0.0)
        info = jnp.where(lane == 1, pick(tf), info)
        for p in range(z.projs):
            info = jnp.where(lane == 2 + p, pick(ids[p]), info)
        r.info[k] = info
        chosen = chosen + dot_tn(put, info.astype(bf16))
    r.chosen[...] = chosen
    rank_of = lax.broadcasted_iota(jnp.int32, (length, rk), 1) // z.rank

    def mask(p):
        return jnp.where(rank_of.astype(f32) == r.chosen[:, 2 + p : 3 + p], 1.0, 0.0)

    a_v, q_v = r.a_v, r.q_v
    o_v = q_v
    serve(2)
    r.low0[...] = (dot_nt(a_v[...], r.q_dn[...]) * mask(0)).astype(bf16)
    r.low1[...] = (dot_nt(a_v[...], r.kv_dn[...]) * mask(1)).astype(bf16)
    out_a = pltpu.make_async_copy(a_v, r.a, r.out_sem.at[0])
    out_a.start()

    serve(3)
    g.ready(0, (KV,))
    kv_loads = [pltpu.make_async_copy(
        r.wkv if o == 0 else g.place(KV, 0, o), we_v.at[1, me ^ o, :, 0:w], r.kv_send.at[o]) for o in range(members)]
    for cp in kv_loads:
        cp.start()
    for cp in kv_loads:
        cp.wait()
    back_kv = pltpu.make_async_copy(we_v.at[1, me, :, 0:w], g.place(KV, 0, 0), r.kv_send.at[0])
    back_kv.start()
    vb = jnp.concatenate([sm[s, :, z.vb_at : z.vb_at + hd // members] for s in range(members)], axis=1)
    kv_bias = jnp.concatenate([jnp.zeros((1, hd), f32), vb], axis=1)
    kv = (dot_nn(a_v[...], we_v[1, :, :, 0:w].reshape(d, w)) + kv_bias
          + scale_lora * dot_nn(r.low1[...], r.kv_up[...])).astype(bf16)
    for k in range(members):
        r.kvp[k] = dot_nn(r.put[k], kv).astype(bf16)

    def kv_copy(o):
        return pltpu.make_async_remote_copy(
            r.kvp, r.kvs.at[me], r.kv_send.at[o], r.kv_recv.at[o],
            device_id=(me ^ o, rep), device_id_type=MESH)

    back_kv.wait()
    own_kv = pltpu.make_async_copy(r.kvp, r.kvs.at[me], r.kv_send.at[0])
    for o in range(1, members):
        kv_copy(o).start()
    own_kv.start()

    for slot in V:
        g.issue(slot, BOTH, False)
    serve(4)

    def wide_load(which):
        g.ready(which, HALVES)
        out = []
        for kind in HALVES:
            for o in range(members):
                src = g.own[kind](which) if o == 0 else g.place(kind, which, o)
                for c in range(d // fc):
                    out.append(pltpu.make_async_copy(
                        src.at[:, c * fc : (c + 1) * fc],
                        we_v.at[c, me ^ o, (kind - AT) * half : (kind - AT + 1) * half],
                        r.load_sem.at[kind - AT, c, o]))
        for cp in out:
            cp.start()
        for cp in out:
            cp.wait()
        back = [pltpu.make_async_copy(
            we_v.at[c, me, (kind - AT) * half : (kind - AT + 1) * half],
            g.place(kind, which, 0).at[:, c * fc : (c + 1) * fc],
            r.load_sem.at[kind - AT, c, 0]) for kind in HALVES for c in range(d // fc)]
        for cp in back:
            cp.start()
        return back

    serve(5)
    back_q = wide_load(WQ)
    q_bias = vec(2)
    for c in range(d // fc):
        serve(14 + c)
        at = slice(c * fc, (c + 1) * fc)
        q_v[:, at] = (dot_nn(a_v[...], we_v[c].reshape(d, fc)) + q_bias[:, at]
                      + scale_lora * dot_nn(r.low0[...], r.q_up[:, at])).astype(bf16)
    out_q = pltpu.make_async_copy(q_v, r.q, r.out_sem.at[1])
    out_q.start()

    for cp in back_q:
        cp.wait()

    serve(6)

    for o in range(1, members):
        pltpu.make_async_copy(r.kvs.at[me ^ o], r.kvs.at[me ^ o], r.kv_recv.at[o]).wait()
    own_kv.wait()
    for cp in coming:
        cp.wait()
    dm[...] = jnp.zeros_like(dm)

    def kvb_load(k, buf):
        return pltpu.make_async_copy(r.kvs.at[:, k], r.kvb.at[buf], r.kvb_sem.at[buf])

    def kd_out(k, buf):
        return pltpu.make_async_copy(r.kd_st.at[buf], r.kd.at[k], r.kd_sem.at[buf])

    kvb_load(0, 0).start()
    groups = 2

    def attend(k, _):
        buf = lax.rem(k, 2)

        @pl.when(k + 1 < members)
        def _():
            kvb_load(k + 1, 1 - buf).start()

        for i in range(min(members, 16)):
            if 40 + i in SERVE:
                pl.when(k == i)(lambda i=i: serve(40 + i))
        kvb_load(k, buf).wait()
        oh = key_onehot(r.slot[k], z.slots)
        kvd = dot_tn(oh, r.kvb[buf].reshape(z.slots, w)).astype(bf16)

        @pl.when(k >= 2)
        def _():
            kd_out(k, buf).wait()

        r.kd_st[buf] = kvd
        kd_out(k, buf).start()
        put = r.put[k]
        qp = dot_nn(put, q_v[...]).astype(bf16)
        info = r.info[k]
        outs = []
        per = heads // groups
        for h in range(groups):
            qr = to_rows(qp[:, h * per * hd : (h + 1) * per * hd], per)
            p = softmax_rows(qr, kvd[:, :hd], info, per).astype(bf16)
            outs.append(to_cols(dot_nn(p, kvd[:, hd:]).astype(bf16), per))
        dm[...] += dot_tn(put, jnp.concatenate(outs, axis=1))
        return 0

    lax.fori_loop(0, members, attend, 0)
    out_q.wait()
    o_v[...] = dm[...].astype(bf16)
    out_o = pltpu.make_async_copy(o_v, r.o, r.out_sem.at[2])
    out_o.start()
    r.low2[...] = (dot_nt(o_v[...], r.mix_dn[...]) * mask(2)).astype(bf16)
    serve(7)
    back_m = wide_load(WMIX)
    mix_bias = vec(3)
    for c in range(d // fc):
        serve(16 + c)
        at = slice(c * fc, (c + 1) * fc)
        y[:, at] = (r.x[:, at].astype(f32) + dot_nn(o_v[...], we_v[c].reshape(d, fc)) + mix_bias[:, at]
                    + scale_lora * dot_nn(r.low2[...], r.mix_up[:, at]))

    def load(slot, buf):
        out = [pltpu.make_async_copy(r.ge.at[slot], we_v.at[buf], r.load_sem.at[0, buf, 0])]
        for o in range(members):
            src = g.own[WR](slot) if o == 0 else g.place(WR, slot, o)
            out.append(pltpu.make_async_copy(src, wr_v.at[buf, me ^ o], r.load_sem.at[1, buf, o]))
        return out

    def fetch(slot, buf):
        g.ready(slot, BOTH)
        for cp in load(slot, buf):
            cp.start()

    for cp in back_m:
        cp.wait()
    out_r = pltpu.make_async_copy(y, r.resid, r.out_sem.at[3])
    out_r.start()
    out_a.wait()
    m_v = a_v
    for part in range(2):
        serve(12 + part)
        norm_rows(y, 4, 5, m_v, part)
    serve(8)
    out_m = pltpu.make_async_copy(m_v, r.m, r.out_sem.at[0])
    out_m.start()
    r.low3[...] = (dot_nt(m_v[...], r.exp_dn[...]) * mask(3)).astype(bf16)
    r.e4[...] = (scale_lora * dot_nt(r.dy[...], r.red_up[...]) * mask(4)).astype(bf16)
    dm[...] = jnp.zeros_like(dm)
    r.lowr[...] = jnp.zeros_like(r.lowr)
    r.er[...] = jnp.zeros_like(r.er)
    out_r.wait()
    y[...] += vec(6)

    def g_out(j, buf):
        return (pltpu.make_async_copy(r.gup_st.at[buf], r.gup.at[:, j], r.g_sem.at[0, buf]),
                pltpu.make_async_copy(r.gdn_st.at[buf], r.gdn.at[:, j], r.g_sem.at[1, buf]))

    serve(9)
    fetch(MLP_ORDER[0], 0)

    def step(n, _):
        for i in range(SLOTS):
            if 60 + 2 * i in SERVE:
                pl.when(n == i)(lambda i=i: serve(60 + 2 * i))
        buf = lax.rem(n, 2)
        slot = jnp.int32(0)
        for i, q in enumerate(MLP_ORDER):
            slot = jnp.where(n == i, q, slot)
        for cp in load(slot, buf):
            cp.wait()
        j = chunk_of(slot, parity)
        we = we_v[buf].reshape(d, fc)
        wr = wr_v[buf].reshape(fc, d)
        if z.aligned:
            def cut(ref):
                return jnp.concatenate([ref[:, pl.ds(pl.multiple_of(s * (z.ff // members) + j * sub, sub), sub)]
                                        for s in range(members)], axis=1)
            bup, adn = cut(r.exp_up), cut(r.red_dn)
        else:
            bup, adn = r.exp_up[j], r.red_dn[j]
        be = jnp.zeros((1, fc), f32)
        for i in range(SLOTS):
            lo = z.be_at + i * sub
            row = jnp.concatenate([sm[s, :, lo : lo + sub] for s in range(members)], axis=1)
            be = jnp.where(j == i, row, be)
        hid = dot_nn(m_v[...], we) + be
        hid = hid + scale_lora * dot_nn(r.low3[...], bup)
        cube = hid * hid * hid
        t = jnp.tanh(gelu_c * (hid + 0.044715 * cube))
        act = (0.5 * hid * (1.0 + t)).astype(bf16)
        slope = 0.5 * (1.0 + t) + 0.5 * hid * (1.0 - t * t) * (
            gelu_c * (1.0 + 3.0 * 0.044715 * hid * hid)
        )
        dact = dot_nt(r.dy[...], wr) + dot_nn(r.e4[...], adn)
        dh = (dact * slope).astype(bf16)
        for i in range(SLOTS):
            def middle(i=i):
                serve(61 + 2 * i)
                if i + 1 < SLOTS:
                    fetch(MLP_ORDER[i + 1], (i + 1) % 2)
            pl.when(n == i)(middle)
        y[...] += dot_nn(act, wr)
        dm[...] += dot_nt(dh, we)
        r.lowr[...] += dot_nt(act, adn)
        r.er[...] += dot_nt(dh, bup)
        gup = (scale_lora * dot_tn(r.low3[...], dh)).astype(bf16)
        gdn = dot_tn(r.e4[...], act).astype(bf16)

        @pl.when(n >= 2)
        def _():
            for cp in g_out(j, buf):
                cp.wait()

        for to in range(members):
            r.gup_st[buf, to] = gup[:, to * sub : (to + 1) * sub]
            r.gdn_st[buf, to] = gdn[:, to * sub : (to + 1) * sub]
        for cp in g_out(j, buf):
            cp.start()
        return 0

    lax.fori_loop(0, SLOTS, step, 0)

    low4 = (r.lowr[...] * mask(4)).astype(bf16)
    r.low4[...] = low4
    out_o.wait()
    layer_v = q_v
    for c in range(d // fc):
        at = slice(c * fc, (c + 1) * fc)
        layer_v[:, at] = (y[:, at] + scale_lora * dot_nn(low4, r.red_up[:, at])).astype(bf16)
    out_l = pltpu.make_async_copy(layer_v, r.layer, r.out_sem.at[1])
    out_l.start()
    back_r = pltpu.make_async_copy(r.resid, y, r.out_sem.at[3])
    back_r.start()
    e3 = (scale_lora * r.er[...] * mask(3)).astype(bf16)
    r.e3[...] = e3
    gain = vec(4)
    back_r.wait()

    def last(i, _):
        at = pl.ds(pl.multiple_of(i * 128, 128), 128)
        n, inv = norm_parts(y[at, :])
        dn = dm[at, :] + dot_nn(r.e3[at, :], r.exp_dn[...])
        dm[at, :] = r.dy[at, :].astype(f32) + norm_back(n, inv, gain, dn)
        return 0

    lax.fori_loop(0, length // 128, last, 0)
    out_l.wait()
    out_m.wait()
    for buf in range(2):
        kd_out(buf, buf).wait()
        for cp in g_out(buf, buf):
            cp.wait()
    for o in range(1, members):
        small_copy(o).wait_send()
        kv_copy(o).wait_send()
    g.finish()


def forward(z, args):
    vm = pl.BlockSpec(memory_space=pltpu.VMEM)
    hbm = pl.BlockSpec(memory_space=pl.ANY)
    m, n, d, rk, w = z.members, z.length, z.d, z.rk, z.w
    s = jax.ShapeDtypeStruct
    half = z.rows // 2
    outs = dict(
        dres=s((n, d), f32), put=s((m, z.cap, n), bf16), slot=s((m, 1, n), jnp.int32),
        info=s((m, z.cap, 128), f32), chosen=s((n, 128), f32),
        low0=s((n, rk), bf16), low1=s((n, rk), bf16), low2=s((n, rk), bf16), low4=s((n, rk), bf16), e3=s((n, rk), bf16), gain=s((1, d), f32),
        a=s((n, d), bf16), q=s((n, d), bf16), o=s((n, d), bf16), m=s((n, d), bf16), resid=s((n, d), f32),
        kd=s((m, n, w), bf16), gup=s((m, SLOTS, rk, z.sub), bf16), gdn=s((m, SLOTS, rk, z.sub), bf16),
        layer=s((n, d), bf16), kvs=s((m, m, z.cap, w), bf16),
        ge=s((SLOTS, m, z.rows, z.fc), bf16), gr=s((SLOTS, m, z.sub, d), bf16),
        ga=s((2, m, half, d), bf16), gb=s((2, m, half, d), bf16), gk=s((1, m, z.rows, w), bf16))
    in_vmem = 11
    sends = m - 1 + m // 2
    dma = pltpu.SemaphoreType.DMA
    items = 2 * SLOTS + 5
    scratch = dict(
        y=pltpu.VMEM((n, d), f32), dy_v=pltpu.VMEM((n, d), bf16), mix_dn_v=pltpu.VMEM((rk, d), bf16),
        mix_up_v=pltpu.VMEM((rk, d), bf16), exp_dn_v=pltpu.VMEM((rk, d), bf16),
        exp_up_v=pltpu.VMEM(args.exp_up.shape, bf16), red_dn_v=pltpu.VMEM(args.exp_up.shape, bf16),
        red_up_v=pltpu.VMEM((rk, d), bf16), late_sem=dma((7,)), we_v=pltpu.VMEM((2, m, z.rows, z.fc), bf16), wr_v=pltpu.VMEM((2, m, z.sub, d), bf16),
        a_v=pltpu.VMEM((n, d), bf16), q_v=pltpu.VMEM((n, d), bf16),
        kvp=pltpu.VMEM((m, z.cap, w), bf16), kvb=pltpu.VMEM((2, m, z.cap, w), bf16),
        kd_st=pltpu.VMEM((2, n, w), bf16), gup_st=pltpu.VMEM((2, m, rk, z.sub), bf16),
        gdn_st=pltpu.VMEM((2, m, rk, z.sub), bf16), sm=pltpu.VMEM((m, 1, z.small_cols), f32),
        lowr=pltpu.VMEM((n, rk), f32), er=pltpu.VMEM((n, rk), f32), low3=pltpu.VMEM((n, rk), bf16), e4=pltpu.VMEM((n, rk), bf16),
        send_sem=dma((items, sends)), recv_sem=dma((items, m)), sm_send=dma((m,)), sm_recv=dma((m,)),
        kv_send=dma((m,)), kv_recv=dma((m,)), stage_sem=dma((SLOTS,)), store_sem=dma((SLOTS,)),
        load_sem=dma((2, 2, m)), kvb_sem=dma((2,)), kd_sem=dma((2,)), g_sem=dma((2, 2)), out_sem=dma((4,)))
    got = pl.pallas_call(
        lambda *refs: fwd_kernel(z, *refs),
        in_specs=[vm] * 17 + [hbm] * 12,
        out_specs=[vm] * in_vmem + [hbm] * (len(FwdOut._fields) - in_vmem),
        out_shape=list(FwdOut(**outs)),
        scratch_shapes=list(FwdScratch(**scratch)),
        compiler_params=pltpu.CompilerParams(
            vmem_limit_bytes=FWD_VMEM, collective_id=1, has_side_effects=True),
    )(*args)
    return FwdOut(*got)


FWD_VMEM = 62 * 1024 * 1024


HALVE, PLANE, SCATTER, COLLECT = range(4)


class Job:
    def __init__(self, members, replicas, work, got, out, send_sem, recv_sem, turn, direct):
        self.me, self.rep = lax.axis_index("shard"), lax.axis_index("rep")
        self.work, self.got, self.out = work, got, out
        self.send_sem, self.recv_sem = send_sem, recv_sem
        self.size = work.shape[2] // replicas
        bits = [1 << i for i in range(members.bit_length() - 1)]
        bits = bits if turn == 0 else bits[:1] + bits[1:][::-1]
        self.stages = []
        at, decided = 0, 0
        for b in bits[:1] if direct else bits:
            free = [f for f in range(members) if not f & (decided | b)]
            self.stages.append((HALVE, at, free, b, decided))
            at += len(free)
            decided |= b
        if direct:
            self.stages.append((PLANE, at, list(range(2, members, 2)), 0, 0))
            at += members // 2 - 1
        turns = list(range(1, replicas))
        self.stages.append((SCATTER, at, turns, at, 0))
        self.stages.append((COLLECT, at + len(turns), turns, at + 1, 0))
        self.count = len(self.stages)

    def rows(self, rep):
        return pl.ds(pl.multiple_of(rep * self.size, self.size), self.size)

    def copy(self, i, n):
        kind, at, items, b, decided = self.stages[i]
        item = items[n]
        if kind == HALVE:
            src = self.work.at[item | (self.me & decided) | ((self.me ^ b) & b)]
            dst, to = self.got.at[at + n], (self.me ^ b, self.rep)
        elif kind == PLANE:
            src, dst, to = self.work.at[self.me ^ item], self.got.at[at + n], (self.me ^ item, self.rep)
        else:
            src = self.work.at[self.me, :, self.rows(self.rep ^ item if kind == SCATTER else self.rep)]
            dst = self.got.at[b, :, n * self.size : (n + 1) * self.size]
            to = (self.me, self.rep ^ item)
        return pltpu.make_async_remote_copy(
            src, dst, self.send_sem.at[at + n], self.recv_sem.at[at + n], device_id=to, device_id_type=MESH)

    def start(self, i):
        for n in range(len(self.stages[i][2])):
            self.copy(i, n).start()

    def add(self, i):
        kind, at, items, b, decided = self.stages[i]
        for n in range(len(items)):
            cp = self.copy(i, n)
            cp.wait_recv()
            cp.wait_send()
        if kind == HALVE:
            for n, item in enumerate(items):
                keep = item | (self.me & decided) | (self.me & b)
                self.work[keep] = (self.work[keep].astype(f32) + self.got[at + n].astype(f32)).astype(bf16)
        elif kind == PLANE:
            total = self.work[self.me].astype(f32)
            for n in range(len(items)):
                total = total + self.got[at + n].astype(f32)
            self.work[self.me] = total.astype(bf16)
        elif kind == SCATTER:
            near = self.rows(self.rep)
            total = self.work[self.me, :, near].astype(f32)
            for n in range(len(items)):
                total = total + self.got[b, :, n * self.size : (n + 1) * self.size].astype(f32)
            self.work[self.me, :, near] = total.astype(bf16)
        else:
            for n, item in enumerate(items):
                self.work[self.me, :, self.rows(self.rep ^ item)] = self.got[b, :, n * self.size : (n + 1) * self.size]
            blocks, lanes = self.work.shape[1], self.work.shape[3]
            for j in range(blocks):
                self.out[:, j * lanes : (j + 1) * lanes] = self.work[self.me, j].astype(f32)

    def move(self, i):
        self.add(i)
        if i + 1 < self.count:
            self.start(i + 1)


class BwdIn(NamedTuple):
    dres: object
    put: object
    slot: object
    info: object
    chosen: object
    low0: object
    low1: object
    low2: object
    low4: object
    e3: object
    gain: object
    mix_dn: object
    mix_up: object
    q_dn: object
    q_up: object
    kv_dn: object
    kv_up: object
    ga: object
    gb: object
    gk: object
    q: object
    a: object
    o: object
    m: object
    dy: object
    x: object
    kd: object
    gup: object
    gdn: object


class BwdOut(NamedTuple):
    dx: object
    ja_out: object
    jb_out: object
    jc_out: object
    jd_out: object
    je_out: object
    jf_out: object
    jg_out: object


class BwdScratch(NamedTuple):
    w_v: object
    wk_v: object
    t1: object
    t2: object
    q_v: object
    do_v: object
    dq: object
    kd_st: object
    ds_st: object
    dk_r: object
    w_sem: object
    t_sem: object
    g_sem: object
    kd_sem: object
    dk_send: object
    dk_recv: object
    out_sem: object
    ja_w: object
    ja_g: object
    ja_s: object
    ja_r: object
    jb_w: object
    jb_g: object
    jb_s: object
    jb_r: object
    jc_w: object
    jc_g: object
    jc_s: object
    jc_r: object
    jd_w: object
    jd_g: object
    jd_s: object
    jd_r: object
    je_w: object
    je_g: object
    je_s: object
    je_r: object
    jf_w: object
    jf_g: object
    jf_s: object
    jf_r: object
    jg_w: object
    jg_g: object
    jg_s: object
    jg_r: object


class BwdRefs(NamedTuple):
    dres: object
    put: object
    slot: object
    info: object
    chosen: object
    low0: object
    low1: object
    low2: object
    low4: object
    e3: object
    gain: object
    mix_dn: object
    mix_up: object
    q_dn: object
    q_up: object
    kv_dn: object
    kv_up: object
    ga: object
    gb: object
    gk: object
    q: object
    a: object
    o: object
    m: object
    dy: object
    x: object
    kd: object
    gup: object
    gdn: object
    dx: object
    ja_out: object
    jb_out: object
    jc_out: object
    jd_out: object
    je_out: object
    jf_out: object
    jg_out: object
    w_v: object
    wk_v: object
    t1: object
    t2: object
    q_v: object
    do_v: object
    dq: object
    kd_st: object
    ds_st: object
    dk_r: object
    w_sem: object
    t_sem: object
    g_sem: object
    kd_sem: object
    dk_send: object
    dk_recv: object
    out_sem: object
    ja_w: object
    ja_g: object
    ja_s: object
    ja_r: object
    jb_w: object
    jb_g: object
    jb_s: object
    jb_r: object
    jc_w: object
    jc_g: object
    jc_s: object
    jc_r: object
    jd_w: object
    jd_g: object
    jd_s: object
    jd_r: object
    je_w: object
    je_g: object
    je_s: object
    je_r: object
    jf_w: object
    jf_g: object
    jf_s: object
    jf_r: object
    jg_w: object
    jg_g: object
    jg_s: object
    jg_r: object


def job_shapes(z):
    wide = z.rows // min(128, z.rows)
    lanes = min(128, z.rows)
    chunks = (SLOTS, z.sub) if z.aligned else (SLOTS * z.sub // 128, 128)
    return (chunks, chunks, (2 * wide, lanes), (2 * wide, lanes), (wide, lanes), (wide, lanes), (wide + 1, lanes))


def bwd_kernel(z, *refs):
    r = BwdRefs(*refs)
    members, replicas, rows, fc, d, hd = z.members, z.replicas, z.rows, z.fc, z.d, z.hd
    length, cap, w, heads, rk = z.length, z.cap, z.w, z.heads, z.rk
    me, rep = lax.axis_index("shard"), lax.axis_index("rep")
    half = rows // 2
    halves = d // fc
    w_v, t1, t2, q_v, do_v, dq, dres = r.w_v, r.t1, r.t2, r.q_v, r.do_v, r.dq, r.dres
    outs = refs[len(BwdIn._fields) + 1 : len(BwdIn._fields) + len(BwdOut._fields)]
    held = refs[-4 * len(outs) :]
    ja, jb, jc, jd, je, jf, jg = (
        Job(members, replicas, held[4 * i], held[4 * i + 1], out, held[4 * i + 2], held[4 * i + 3], i % 2, i >= 4)
        for i, out in enumerate(outs))

    barrier = pltpu.get_barrier_semaphore()
    others = [(me ^ o, rep) for o in range(1, members)] + [(me, rep ^ o) for o in range(1, replicas)]
    for to in others:
        pl.semaphore_signal(barrier, inc=1, device_id=to, device_id_type=MESH)

    def local(src, dst, sem):
        return pltpu.make_async_copy(src, dst, sem)

    def wide(which):
        return [local(part.at[which, :, :, c * fc : (c + 1) * fc],
                      w_v.at[c, :, h * half : (h + 1) * half], r.w_sem.at[h, c])
                for h, part in enumerate((r.ga, r.gb)) for c in range(halves)]

    load_up = local(r.gup, r.ja_w, r.g_sem.at[0])
    load_dn = local(r.gdn, r.jb_w, r.g_sem.at[1])
    load_up.start()
    load_dn.start()
    mix = wide(WMIX)
    for cp in mix:
        cp.start()
    load_m = local(r.m, t1, r.t_sem.at[0])
    load_dy = local(r.dy, t2, r.t_sem.at[1])
    load_q = local(r.q, q_v, r.t_sem.at[2])
    load_k = local(r.gk.at[0], r.wk_v, r.t_sem.at[3])
    for cp in (load_m, load_dy, load_q, load_k):
        cp.start()
    pl.semaphore_wait(barrier, len(others))
    load_up.wait()
    ja.start(0)
    load_dn.wait()
    jb.start(0)

    rank_of = (lax.broadcasted_iota(jnp.int32, (length, rk), 1) // z.rank).astype(f32)

    def mask(p):
        return jnp.where(rank_of == r.chosen[:, 2 + p : 3 + p], 1.0, 0.0)

    def terms(job, block, left, right, sc):
        lanes = job.work.shape[3]
        g = dot_tn(left, right) * sc
        width = right.shape[1] // members
        for to in range(members):
            for i in range(-(-width // lanes)):
                part = g[:, to * width + i * lanes : to * width + min((i + 1) * lanes, width)]
                if part.shape[1] < lanes:
                    part = jnp.concatenate([part, jnp.zeros((rk, lanes - part.shape[1]), f32)], axis=1)
                job.work[to, block + i] = part.astype(bf16)

    per = r.jc_w.shape[1] // 2

    dresl = do_v
    dresl[...] = dres[...].astype(bf16)
    e2 = (scale_lora * dot_nt(dresl[...], r.mix_up[...]) * mask(2)).astype(bf16)
    terms(jd, per, r.low2[...], dresl[...], scale_lora)
    load_m.wait()
    terms(jc, 0, r.e3[...], t1[...], 1.0)
    load_o = local(r.o, t1, r.t_sem.at[0])
    load_o.start()
    load_dy.wait()
    terms(jd, 0, r.low4[...], t2[...], scale_lora)
    load_x = local(r.x, t2, r.t_sem.at[1])
    load_x.start()
    jd.start(0)
    for cp in mix:
        cp.wait()
    ja.move(0)
    dq[...] = dot_nt(dresl[:, 0:fc], w_v[0].reshape(d, fc)) + dot_nn(e2, r.mix_dn[...])
    jb.move(0)
    for c in range(1, halves):
        dq[...] += dot_nt(dresl[:, c * fc : (c + 1) * fc], w_v[c].reshape(d, fc))
    do_v[...] = dq[...].astype(bf16)
    query = wide(WQ)
    for cp in query:
        cp.start()
    load_o.wait()
    terms(jc, per, e2, t1[...], 1.0)
    jc.start(0)
    load_a = local(r.a, t1, r.t_sem.at[0])
    load_a.start()
    jd.move(0)
    dq[...] = jnp.zeros_like(dq)
    load_q.wait()

    def kd_load(k, buf):
        return local(r.kd.at[k], r.kd_st.at[buf], r.kd_sem.at[buf])

    def ds_copy(k, buf, o):
        return pltpu.make_async_remote_copy(
            r.ds_st.at[buf, me ^ o], r.dk_r.at[me, k], r.dk_send.at[buf, o], r.dk_recv.at[o],
            device_id=(me ^ o, rep), device_id_type=MESH)

    kd_load(0, 0).start()
    groups = 4
    sc = hd ** (-0.5)
    plan = ((), (), ((jc, 0),), (), ((ja, 1), (jb, 1), (jd, 1)), (), ((jc, 1), (ja, 2), (jb, 2)), ((jd, 2),))


    def act(some):
        for job, i in some:
            job.move(i)

    def attend(k, _):
        buf = lax.rem(k, 2)

        @pl.when(k + 1 < members)
        def _():
            kd_load(k + 1, 1 - buf).start()

        for i, some in enumerate(plan):
            pl.when(k == i)(lambda some=some: act(some))
        kd_load(k, buf).wait()
        kvd = r.kd_st[buf]
        kd, vd = kvd[:, :hd], kvd[:, hd:]
        put = r.put[k]
        qp = dot_nn(put, q_v[...]).astype(bf16)
        dop = dot_nn(put, do_v[...]).astype(bf16)
        info = r.info[k]
        n = heads // groups
        dqs = []
        dk = jnp.zeros((length, hd), f32)
        dv = jnp.zeros((length, hd), f32)
        for h in range(groups):
            at = slice(h * n * hd, (h + 1) * n * hd)
            qr, dor = to_rows(qp[:, at], n), to_rows(dop[:, at], n)
            p = softmax_rows(qr, kd, info, n)
            dp = dot_nt(dor, vd)
            ds = (p * (dp - jnp.sum(dp * p, axis=1, keepdims=True))).astype(bf16)
            dqs.append(to_cols((dot_nn(ds, kd) * sc).astype(bf16), n))
            dk = dk + dot_tn(ds, qr)
            dv = dv + dot_tn(p.astype(bf16), dor)
        dq[...] += dot_tn(put, jnp.concatenate(dqs, axis=1))
        dkv = jnp.concatenate([dk * sc, dv], axis=1).astype(bf16)
        slots = dot_nn(key_onehot(r.slot[k], z.slots), dkv).astype(bf16).reshape(members, cap, w)

        @pl.when(k >= 2)
        def _():
            for o in range(1, members):
                ds_copy(k, buf, o).wait_send()

        r.ds_st[buf] = slots
        r.dk_r[me, k] = r.ds_st[buf, me]
        for o in range(1, members):
            ds_copy(k, buf, o).start()
        return 0

    lax.fori_loop(0, members, attend, 0)

    following = {ja: 3, jb: 3, jc: 2, jd: 3, je: 0, jf: 0, jg: 0}

    def go(*jobs):
        for job in jobs:
            if following[job] < job.count:
                job.move(following[job])
                following[job] += 1

    go(ja, jb)
    q_v[...] = dq[...].astype(bf16)
    e0 = (scale_lora * dot_nt(q_v[...], r.q_up[...]) * mask(0)).astype(bf16)
    load_a.wait()
    terms(je, 0, e0, t1[...], 1.0)
    je.start(0)
    terms(jf, 0, r.low0[...], q_v[...], scale_lora)
    jf.start(0)
    for o in range(1, members):
        local(r.dk_r.at[me ^ o], r.dk_r.at[me ^ o], r.dk_recv.at[o]).wait()
    go(jd, jc)
    dkv = jnp.zeros((length, w), f32)
    for k in range(members):
        total = r.dk_r[0, k].astype(f32)
        for s in range(1, members):
            total = total + r.dk_r[s, k].astype(f32)
        dkv = dkv + dot_tn(r.put[k], total.astype(bf16))
    dkv = dkv.astype(bf16)
    go(je, jf)
    e1 = (scale_lora * dot_nt(dkv, r.kv_up[...]) * mask(1)).astype(bf16)
    terms(jg, 0, e1, t1[...], 1.0)
    terms(jg, per, r.low1[...], dkv, scale_lora)
    jg.start(0)
    load_k.wait()
    dq[...] = (dot_nn(e0, r.q_dn[...]) + dot_nn(e1, r.kv_dn[...])
               + dot_nt(dkv, r.wk_v[...].reshape(d, w)))
    go(jd, jc, je, jf, jg)
    for cp in query:
        cp.wait()
    for c in range(halves):
        dq[...] += dot_nt(q_v[:, c * fc : (c + 1) * fc], w_v[c].reshape(d, fc))
        go(je, jf, jg)
    load_x.wait()
    gain = r.gain[...]

    def back(i, _):
        at = pl.ds(pl.multiple_of(i * 128, 128), 128)
        n, inv = norm_parts(t2[at, :].astype(f32))
        do_v[at, :] = (dres[at, :] + norm_back(n, inv, gain, dq[at, :])).astype(bf16)
        return 0

    for part in range(2):
        lax.fori_loop(part * length // 256, (part + 1) * length // 256, back, 0)
        go(je, jf, jg)
    out = local(do_v, r.dx, r.out_sem)
    out.start()
    while any(following[job] < job.count for job in following):
        go(ja, jb, jc, jd, je, jf, jg)
    out.wait()
    for buf in range(2):
        for o in range(1, members):
            ds_copy(buf, buf, o).wait_send()


def backward(z, args):
    vm = pl.BlockSpec(memory_space=pltpu.VMEM)
    hbm = pl.BlockSpec(memory_space=pl.ANY)
    m, n, d, rk, w = z.members, z.length, z.d, z.rk, z.w
    s = jax.ShapeDtypeStruct
    dma = pltpu.SemaphoreType.DMA
    shapes = job_shapes(z)
    legs = m - 1 + 2
    sems = m - 1 + 2 * (z.replicas - 1)
    scratch = dict(
        w_v=pltpu.VMEM((d // z.fc, m, z.rows, z.fc), bf16), wk_v=pltpu.VMEM((m, z.rows, w), bf16),
        t1=pltpu.VMEM((n, d), bf16), t2=pltpu.VMEM((n, d), bf16), q_v=pltpu.VMEM((n, d), bf16), do_v=pltpu.VMEM((n, d), bf16),
        dq=pltpu.VMEM((n, d), f32), kd_st=pltpu.VMEM((2, n, w), bf16), ds_st=pltpu.VMEM((2, m, z.cap, w), bf16),
        dk_r=pltpu.VMEM((m, m, z.cap, w), bf16),
        w_sem=dma((2, d // z.fc)), t_sem=dma((4,)), g_sem=dma((2,)), kd_sem=dma((2,)), dk_send=dma((2, m)),
        dk_recv=dma((m,)), out_sem=dma(()))
    scratch = [scratch[k] for k in BwdScratch._fields[: len(scratch)]]
    job_outs = [s((rk, blocks * lanes), f32) for blocks, lanes in shapes]
    job_scratch = [x for blocks, lanes in shapes for x in (
        pltpu.VMEM((m, blocks, rk, lanes), bf16), pltpu.VMEM((legs, blocks, rk, lanes), bf16), dma((sems,)), dma((sems,)))]
    first_hbm = 17
    got = pl.pallas_call(
        lambda *refs: bwd_kernel(z, *refs),
        in_specs=[vm] * first_hbm + [hbm] * (len(BwdIn._fields) - first_hbm),
        out_specs=[hbm] + [vm] * len(shapes),
        out_shape=[s((n, d), bf16)] + job_outs,
        scratch_shapes=scratch + job_scratch,
        compiler_params=pltpu.CompilerParams(
            vmem_limit_bytes=FWD_VMEM, collective_id=2, has_side_effects=True),
    )(*BwdIn(**args))
    return BwdOut(*got)


def final(sums, z, experts, rank):
    c, n = z.rows, z.w // z.members
    ff = z.ff // z.members
    cuts = ((4, 0, c), (5, 0, c), (6, 0, c), (6, c, n), (2, c, c), (3, c, c), (2, 0, c), (0, 0, ff), (1, 0, ff), (3, 0, c))

    def kernel(*refs):
        for (job, at, width), out in zip(cuts, refs[len(sums):]):
            out[...] = refs[job][:, at : at + width].reshape(experts, rank, width)

    vm = pl.BlockSpec(memory_space=pltpu.VMEM)
    return pl.pallas_call(
        kernel, in_specs=[vm] * len(sums), out_specs=[vm] * len(cuts),
        out_shape=[jax.ShapeDtypeStruct((experts, rank, w), f32) for _, _, w in cuts])(*sums)


def local(tokens, out_grad, token_perm, seq_lens, adapter_ids,
          attn_g, attn_b, wq, bq, wkv, bv, wmix, bmix, mlp_g, mlp_b, wexp, bexp, wred, bred,
          q_dn, q_up, kv_dn, kv_up, mix_dn, mix_up, exp_dn, exp_up, red_dn, red_up):
    members = lax.axis_size("shard")
    replicas = lax.axis_size("rep")
    rep = lax.axis_index("rep")
    length, d = tokens.shape
    experts, rank = q_dn.shape[:2]
    rk = experts * rank
    z = Sizes(members, replicas, length, d, wexp.shape[1], bv.shape[0] * members, rk, rank,
              seq_lens.shape[1], adapter_ids.shape[2])
    flat = lambda s: s.reshape(rk, s.shape[2])
    q_dn, q_up, kv_dn, kv_up, mix_dn, mix_up, exp_dn, exp_up, red_dn, red_up = map(
        flat, (q_dn, q_up, kv_dn, kv_up, mix_dn, mix_up, exp_dn, exp_up, red_dn, red_up))
    group = lax.dynamic_index_in_dim(
        token_perm.reshape(members, replicas, length), rep, 1, keepdims=False)

    by_chunk = lambda s: s.reshape(s.shape[0], members, SLOTS, z.sub).transpose(2, 0, 1, 3).reshape(
        SLOTS, s.shape[0], z.fc)
    chunked = (lambda s: s) if z.aligned else by_chunk
    got = forward(z, FwdIn(
        x=tokens, dy=out_grad, attn_g=attn_g, attn_b=attn_b, bq=bq, bmix=bmix, mlp_g=mlp_g, mlp_b=mlp_b, bred=bred, bexp=bexp, bv=bv,
        lens=seq_lens, ids=adapter_ids, group=group,
        q_dn=q_dn, q_up=q_up, kv_dn=kv_dn, kv_up=kv_up, mix_dn=mix_dn, mix_up=mix_up, exp_dn=exp_dn,
        exp_up=chunked(exp_up), red_dn=chunked(red_dn), red_up=red_up,
        wq=wq, wkv=wkv, wmix=wmix, wexp=chunked(wexp), wred=wred.reshape(SLOTS, z.sub, d)))
    gup, gdn = got.gup, got.gdn
    if not z.aligned:
        pack = 128 // z.sub
        gup, gdn = (g.reshape(members, SLOTS // pack, pack, rk, z.sub).transpose(0, 1, 3, 2, 4).reshape(
            members, SLOTS // pack, rk, 128) for g in (gup, gdn))
    back = backward(z, dict(
        dres=got.dres, put=got.put, slot=got.slot, info=got.info, chosen=got.chosen, low0=got.low0, low1=got.low1,
        low2=got.low2, low4=got.low4, e3=got.e3, gain=got.gain, ga=got.ga, gb=got.gb, gk=got.gk, q=got.q, a=got.a,
        o=got.o, m=got.m, kd=got.kd, gup=gup, gdn=gdn,
        mix_dn=mix_dn, mix_up=mix_up, q_dn=q_dn, q_up=q_up, kv_dn=kv_dn, kv_up=kv_up, dy=out_grad, x=tokens))
    g = final(back[1:], z, experts, rank)
    return (got.layer, back.dx, *g)


def solution(mesh):
    both = ("shard", "rep")
    row, vec = P("shard", None), P("shard")
    in_specs = (
        P(both, None), P(both, None), P(), P(both, None), P(both, None, None),
        vec, vec, row, vec, row, vec, row, vec, vec, vec, row, vec, row, vec,
    ) + (P(),) * 10
    out_specs = (P(both, None), P(both, None)) + (P(None, None, "shard"),) * 10
    return jax.shard_map(local, mesh=mesh, in_specs=in_specs, out_specs=out_specs, check_vma=False)
```
